32 devices in a mesh: dp: 8 (over y, x, core), tensor: 4 (over z).
Axes of the slice: x: 2, y: 2, z: 4, core: 2. Of those that a mesh axis runs over, the one named last changes fastest.
Arguments:
- tokens: bfloat16 [23328, 1152], P('dp'), may hold values from -6 to 6
- image_flags: int32 [32], P('dp'), may hold values 0 or 1
- cotangent: bfloat16 [23328, 1152], P('dp'), may hold values from -6 to 6
- gain_one: float32 [1152], replicated, may hold values from 0.25 to 1.75
- shift_one: float32 [1152], replicated, may hold values from -2 to 2
- w_query: float32 [1152, 1152], P('dp', 'tensor'), may hold values from -0.25 to 0.25
- b_query: float32 [1152], P('tensor'), may hold values from -3 to 3
- w_key: float32 [1152, 1152], P('dp', 'tensor'), may hold values from -0.25 to 0.25
- w_value: float32 [1152, 1152], P('dp', 'tensor'), may hold values from -0.1875 to 0.1875
- b_value: float32 [1152], P('tensor'), may hold values from -3 to 3
- w_out: float32 [1152, 1152], P('tensor', 'dp'), may hold values from -0.75 to 0.75
- b_out: float32 [1152], replicated, may hold values from -3 to 3
- gain_two: float32 [1152], replicated, may hold values from 0.25 to 1.75
- shift_two: float32 [1152], replicated, may hold values from -2 to 2
- w_up: float32 [1152, 4304], P('dp', 'tensor'), may hold values from -0.1875 to 0.1875
- b_up: float32 [4304], P('tensor'), may hold values from -3 to 3
- w_down: float32 [4304, 1152], P('tensor', 'dp'), may hold values from -0.125 to 0.125
- b_down: float32 [1152], replicated, may hold values from -3 to 3
Outputs:
- mixed: bfloat16 [23328, 1152], P(('dp', 'tensor'))
- tokens_grad: bfloat16 [23328, 1152], P(('dp', 'tensor'))
- grad_gain_one: float32 [1152], replicated
- grad_shift_one: float32 [1152], replicated
- grad_w_query: float32 [1152, 1152], P('dp', 'tensor')
- grad_b_query: float32 [1152], P('tensor')
- grad_w_key: float32 [1152, 1152], P('dp', 'tensor')
- grad_w_value: float32 [1152, 1152], P('dp', 'tensor')
- grad_b_value: float32 [1152], P('tensor')
- grad_w_out: float32 [1152, 1152], P('tensor', 'dp')
- grad_b_out: float32 [1152], replicated
- grad_gain_two: float32 [1152], replicated
- grad_shift_two: float32 [1152], replicated
- grad_w_up: float32 [1152, 4304], P('dp', 'tensor')
- grad_b_up: float32 [4304], P('tensor')
- grad_w_down: float32 [4304, 1152], P('tensor', 'dp')
- grad_b_down: float32 [1152], replicated
The draws below stay inside these ranges and needn't reach their ends.
Inputs may be any that keep to these rules, and one draw needn't show every extreme that they name: `image_flags`: 1 marks a real image, 0 a padded empty one.
All inputs are finite; a program needn't handle non-finite values. No bound on the sum of `image_flags` on one device may be relied on, other than what follows from the above.
Results may differ from the reference program's by a relative error of at most 0.014.
The reference program's roundings to bfloat16 on the way count: a program that leaves them out, or rounds other values in their place, can miss the bound.
Values may be sent and summed in bfloat16 or wider, within the bound.
No kernel may reach another device: no remote copies, remote signals or barrier semaphores. Data moves between devices by JAX's collectives and lax.ppermute only.
A program may use at most 192 MiB of HBM per device.

```python
import jax
import jax.numpy as jnp
from jax import lax

D = 1152
H = 16
HD = 72
FF = 4304
SEQ = 729
IMAGES = 32
TOKENS = 23328


def set_ends(values, key, least, largest):
    longest = values.shape.index(max(values.shape))
    spots = []
    for shift in (0, 1):
        where = [jax.random.randint(jax.random.fold_in(key, axis), (), 0, length) for axis, length in enumerate(values.shape)]
        where[longest] = (where[longest] + shift) % values.shape[longest]
        spots.append(tuple(where))
    return values.at[spots[0]].set(least).at[spots[1]].set(largest)


def block_levels(own_key, dims, cuts, low, largest):
    level, own = 1.0, jax.random.fold_in(own_key, 6)
    for dim, parts in cuts:
        draws = jnp.exp(jax.random.uniform(jax.random.fold_in(own, dim), (parts,), jnp.float32, low / len(cuts), largest / len(cuts)))
        level = level * jnp.repeat(draws, dims[dim] // parts).reshape([-1 if axis == dim else 1 for axis in range(len(dims))])
    return level


def noise(own_key, extent, spread, limit, pieces=(), dtype=jnp.bfloat16):
    array = spread * jax.random.normal(own_key, extent, jnp.float32)
    if pieces:
        array = array * block_levels(own_key, extent, pieces, -0.22, 0.18)
    return jnp.clip(array, -limit, limit).astype(dtype)


def setup_inputs(seed: int = 0) -> dict:
    streams_of = jax.random.split(jax.random.key(seed), 19)
    tokens = noise(streams_of[0], (TOKENS, D), 1.0, 6.0, ((0, 8),))
    image_flags = set_ends((jax.random.randint(streams_of[1], (IMAGES,), 0, 4) < 3).astype(jnp.int32), jax.random.fold_in(streams_of[1], 1), 0, 1)
    cotangent = noise(streams_of[2], (TOKENS, D), 1.0, 6.0, ((0, 8),))
    gain_one = jnp.clip(1.0 + 0.15 * jax.random.normal(streams_of[3], (D,), jnp.float32), 0.25, 1.75)
    shift_one = noise(streams_of[4], (D,), 0.3, 2.0, (), jnp.float32)
    w_query = noise(streams_of[5], (D, D), (D // 2) ** -0.5, 0.25, ((0, 8), (1, 4)), jnp.float32)
    b_query = noise(streams_of[6], (D,), 0.5, 3.0, ((0, 4),), jnp.float32)
    w_key = noise(streams_of[7], (D, D), (D // 2) ** -0.5, 0.25, ((0, 8), (1, 4)), jnp.float32)
    w_value = noise(streams_of[8], (D, D), D ** -0.5, 0.1875, ((0, 8), (1, 4)), jnp.float32)
    b_value = noise(streams_of[9], (D,), 0.5, 3.0, ((0, 4),), jnp.float32)
    w_out = noise(streams_of[10], (D, D), (D // 16) ** -0.5, 0.75, ((0, 4), (1, 8)), jnp.float32)
    b_out = noise(streams_of[11], (D,), 0.5, 3.0, (), jnp.float32)
    gain_two = jnp.clip(1.0 + 0.15 * jax.random.normal(streams_of[12], (D,), jnp.float32), 0.25, 1.75)
    shift_two = noise(streams_of[13], (D,), 0.3, 2.0, (), jnp.float32)
    w_up = noise(streams_of[14], (D, FF), D ** -0.5, 0.1875, ((0, 8), (1, 4)), jnp.float32)
    b_up = noise(streams_of[15], (FF,), 0.5, 3.0, ((0, 4),), jnp.float32)
    w_down = noise(streams_of[16], (FF, D), (FF // 2) ** -0.5, 0.125, ((0, 4), (1, 8)), jnp.float32)
    b_down = noise(streams_of[17], (D,), 0.5, 3.0, (), jnp.float32)
    return dict(tokens=tokens, image_flags=image_flags, cotangent=cotangent, gain_one=gain_one, shift_one=shift_one, w_query=w_query, b_query=b_query, w_key=w_key, w_value=w_value, b_value=b_value, w_out=w_out, b_out=b_out, gain_two=gain_two, shift_two=shift_two, w_up=w_up, b_up=b_up, w_down=w_down, b_down=b_down)


EPSILON = 1e-06
HIGHEST = lax.Precision.HIGHEST

@jax.custom_vjp
def low(v):
    return lax.optimization_barrier(v.astype(jnp.bfloat16)).astype(jnp.float32)

@jax.custom_vjp
def low_back(v):
    return v

def low_keep(v):
    return (low(v), None)

def low_pass(kept, grad):
    return (grad,)

def back_keep(v):
    return (v, None)

def back_low(kept, grad):
    return (low(grad),)
low.defvjp(low_keep, low_pass)
low_back.defvjp(back_keep, back_low)

def layer_norm(inputs, gain_vec, shift_vec):
    average = lax.optimization_barrier(jnp.mean(inputs, axis=-1, keepdims=True))
    centred = inputs - average
    variance = lax.optimization_barrier(jnp.mean(centred * centred, axis=-1, keepdims=True))
    return centred * lax.rsqrt(variance + EPSILON) * gain_vec + shift_vec

def matmul(left, right):
    return jnp.dot(left, right, precision=HIGHEST)

def image_block(inputs, flag_value, weights):
    gain_one, shift_one, w_query, b_query, w_key, w_value, b_value, w_out, b_out, gain_two, shift_two, w_up, b_up, w_down, b_down = weights
    normed = low(layer_norm(inputs, gain_one, shift_one))
    queries = low(low_back(matmul(normed, w_query) + b_query))
    key_rows = low(low_back(matmul(normed, w_key)))
    value_rows = low(low_back(matmul(normed, w_value) + b_value))
    head_queries = queries.reshape(SEQ, H, HD)
    head_keys = key_rows.reshape(SEQ, H, HD)
    head_values = value_rows.reshape(SEQ, H, HD)
    scores = low_back(jnp.einsum('qhd,khd->hqk', head_queries, head_keys, precision=HIGHEST) * HD ** (-0.5))
    softmax_rows = low(jax.nn.softmax(scores, axis=-1))
    mixed_heads = low(low_back(jnp.einsum('hqk,khd->qhd', softmax_rows, head_values, precision=HIGHEST)))
    mixed_heads = mixed_heads.reshape(SEQ, D)
    residual = inputs + low_back(matmul(mixed_heads, w_out)) + b_out
    normed_two = low(layer_norm(residual, gain_two, shift_two))
    pre_act = low_back(matmul(normed_two, w_up) + b_up)
    hidden = low(jax.nn.gelu(pre_act, approximate=True))
    result = residual + low_back(matmul(hidden, w_down)) + b_down
    return result * flag_value

def reference(tokens, image_flags, cotangent, gain_one, shift_one, w_query, b_query, w_key, w_value, b_value, w_out, b_out, gain_two, shift_two, w_up, b_up, w_down, b_down):
    inputs = tokens.astype(jnp.float32).reshape(IMAGES, SEQ, D)
    flag_values = image_flags.astype(jnp.float32)
    image_step = jax.checkpoint(image_block)

    def forward(image_inputs, *weights):
        rounded = list(weights)
        for position in (2, 4, 5, 7, 11, 13):
            rounded[position] = low(rounded[position])
        rounded = tuple(rounded)

        def scan_body(state_carry, element):
            return (state_carry, image_step(element[0], element[1], rounded))
        _, results = lax.scan(scan_body, jnp.zeros((), jnp.float32), (image_inputs, flag_values))
        return results
    result, pullback = jax.vjp(forward, inputs, gain_one, shift_one, w_query, b_query, w_key, w_value, b_value, w_out, b_out, gain_two, shift_two, w_up, b_up, w_down, b_down)
    gradients = pullback(cotangent.astype(jnp.float32).reshape(IMAGES, SEQ, D))
    mixed = result.reshape(TOKENS, D).astype(jnp.bfloat16)
    tokens_grad = gradients[0].reshape(TOKENS, D).astype(jnp.bfloat16)
    return (mixed, tokens_grad, gradients[1], gradients[2], gradients[3], gradients[4], gradients[5], gradients[6], gradients[7], gradients[8], gradients[9], gradients[10], gradients[11], gradients[12], gradients[13], gradients[14], gradients[15])
```

```python
from functools import partial

import jax
import jax.numpy as jnp
from jax import lax
from jax.experimental import pallas as pl
from jax.experimental.pallas import tpu as pltpu
from jax.sharding import PartitionSpec as P

HD = 72
LANES = 128
EPSILON = 1e-06
SCALE = HD**-0.5
SHARP = SCALE * 1.4426950408889634
GELU_A = 0.7978845608028654
GELU_B = 0.044715
BF = jnp.bfloat16
F32 = jnp.float32
VMEM_BYTES = 40 * 2**20
ANY = pl.BlockSpec(memory_space=pl.ANY)
SMEM = pl.BlockSpec(memory_space=pltpu.SMEM)
VMEM = pl.BlockSpec(memory_space=pltpu.VMEM)


def up(value, step):
    return -(-value // step) * step


def nn(left, right):
    return lax.dot_general(left, right, (((1,), (0,)), ((), ())), preferred_element_type=F32)


def nt(left, right):
    return lax.dot_general(left, right, (((1,), (1,)), ((), ())), preferred_element_type=F32)


def call(kernel, name, us, place, weights, after, ins, outs, scratch, aliases=()):
    weights, after = list(weights), list(after)
    lead = 1 + len(weights) + len(after)

    def body(*refs):
        kernel(refs[0], refs[1 : 1 + len(weights)], *refs[lead:])

    return pl.pallas_call(
        body,
        in_specs=[SMEM] + [ANY] * (lead - 1) + [VMEM] * len(ins),
        out_specs=[VMEM] * len(outs),
        out_shape=[jax.ShapeDtypeStruct(*out) for out in outs],
        scratch_shapes=scratch,
        input_output_aliases={lead + i: o for i, o in aliases},
        compiler_params=pltpu.CompilerParams(vmem_limit_bytes=VMEM_BYTES),
        cost_estimate=pl.CostEstimate(
            flops=int(us * 1.15e9), bytes_accessed=int(us * 1e5), transcendentals=0
        ),
        name=name,
    )(place, *weights, *after, *ins)


class Piece:
    def __init__(self, arrays, blocks):
        self.arrays, self.blocks = arrays, blocks

    def fetch(self, refs, place_ref, buffer, sem):
        for array, lead, first, rows in self.blocks(place_ref[0], place_ref[1]):
            pltpu.make_async_copy(
                refs[array].at[lead], buffer.at[pl.ds(first, rows), :], sem
            ).start()


def landed(buffer, sem):
    pltpu.make_async_copy(buffer, buffer, sem).wait()


def turn(cfg, d, value, out_ref, scratch):
    rows, order = cfg["rows"], cfg["order"]
    if order is None:
        out_ref[...] = value.T
        return
    scratch[...] = value.T
    for place, offset in enumerate(order):
        first = pl.multiple_of(jnp.bitwise_xor(d, offset) * rows, 16)
        out_ref[place * rows : (place + 1) * rows, :] = scratch[pl.ds(first, rows), :]


STEP = 32


def over_rows(total, body, carry):
    def step(t, carry):
        return body(pl.ds(pl.multiple_of(t * STEP, STEP), STEP), carry)

    return lax.fori_loop(0, total // STEP, step, carry)


def norm_stats(rows):
    average = jnp.mean(rows, axis=-1, keepdims=True)
    centred = rows - average
    inverse = lax.rsqrt(jnp.mean(centred * centred, axis=-1, keepdims=True) + EPSILON)
    return centred * inverse, inverse


def fold(value):
    return jnp.sum(value.reshape(STEP // 8, 8, value.shape[1]), axis=0)


def total_of(partial_sums):
    return jnp.sum(partial_sums, axis=0, keepdims=True)


def norm_one_kernel(
    cfg, place_ref, _, x_ref, eb_ref, gain_ref, shift_ref, a_ref, at_ref, et_ref, sum_ref, scratch
):
    def rows_of(rows, carry):
        unit, _ = norm_stats(x_ref[rows, :].astype(F32))
        a_ref[rows, :] = (unit * gain_ref[...] + shift_ref[...]).astype(BF)
        return carry + fold(eb_ref[rows, :].astype(F32))

    m, dim = x_ref.shape
    sum_ref[...] = total_of(over_rows(m, rows_of, jnp.zeros((8, dim), F32)))
    turn(cfg, place_ref[0], a_ref[...], at_ref, scratch)
    turn(cfg, place_ref[0], eb_ref[...], et_ref, scratch)


def norm_one(cfg, place, x, eb, gain, shift):
    m, d = x.shape
    outs = [((m, d), BF), ((d, m), BF), ((d, m), BF), ((1, d), F32)]
    return call(
        partial(norm_one_kernel, cfg), "norm_one", 6, place, [], [], [x, eb, gain, shift], outs,
        [pltpu.VMEM((d, m), BF)],
    )


def norm_two_kernel(
    cfg, place_ref, _, x_ref, att_ref, b_out, gain, shift, h_ref, a_ref, at_ref, scratch
):
    def rows_of(rows, carry):
        h = x_ref[rows, :].astype(F32) + att_ref[rows, :] + b_out[...]
        h_ref[rows, :] = h
        unit, _ = norm_stats(h)
        a_ref[rows, :] = (unit * gain[...] + shift[...]).astype(BF)
        return carry

    over_rows(x_ref.shape[0], rows_of, 0)
    turn(cfg, place_ref[0], a_ref[...], at_ref, scratch)


def norm_two(cfg, place, after, x, att, b_out, gain, shift):
    m, d = x.shape
    outs = [((m, d), F32), ((m, d), BF), ((d, m), BF)]
    return call(
        partial(norm_two_kernel, cfg), "norm_two", 6, place, [], after,
        [x, att, b_out, gain, shift], outs, [pltpu.VMEM((d, m), BF)],
    )


def norm_two_back_kernel(
    cfg, place_ref, _, h_ref, feed_ref, dn_ref, eb_ref, b_down, gain,
    mixed_ref, dh_ref, dhb_ref, dht_ref, vec_ref, scratch,
):
    flag = place_ref[2].astype(F32)

    def rows_of(rows, carry):
        h = h_ref[rows, :]
        mixed_ref[rows, :] = ((h + feed_ref[rows, :] + b_down[...]) * flag).astype(BF)
        unit, inverse = norm_stats(h)
        grad = dn_ref[rows, :]
        scaled = grad * gain[...]
        dh = eb_ref[rows, :].astype(F32) + inverse * (
            scaled
            - jnp.mean(scaled, axis=-1, keepdims=True)
            - unit * jnp.mean(scaled * unit, axis=-1, keepdims=True)
        )
        dh_ref[rows, :] = dh
        dhb_ref[rows, :] = dh.astype(BF)
        return carry[0] + fold(grad * unit), carry[1] + fold(grad), carry[2] + fold(dh)

    m, dim = h_ref.shape
    zero = jnp.zeros((8, dim), F32)
    sums = over_rows(m, rows_of, (zero, zero, zero))
    for i, value in enumerate(sums):
        vec_ref[i : i + 1, :] = total_of(value)
    turn(cfg, place_ref[0], dhb_ref[...], dht_ref, scratch)


def norm_two_back(cfg, place, after, h, feed, dn, eb, b_down, gain):
    m, d = h.shape
    outs = [((m, d), BF), ((m, d), F32), ((m, d), BF), ((d, m), BF), ((3, d), F32)]
    return call(
        partial(norm_two_back_kernel, cfg), "norm_two_back", 10, place, [], after,
        [h, feed, dn, eb, b_down, gain], outs, [pltpu.VMEM((d, m), BF)],
    )


def norm_back_kernel(place_ref, _, x_ref, dn_ref, dh_ref, gain, out_ref, vec_ref):
    def rows_of(rows, carry):
        unit, inverse = norm_stats(x_ref[rows, :].astype(F32))
        grad = dn_ref[rows, :]
        scaled = grad * gain[...]
        out = dh_ref[rows, :] + inverse * (
            scaled
            - jnp.mean(scaled, axis=-1, keepdims=True)
            - unit * jnp.mean(scaled * unit, axis=-1, keepdims=True)
        )
        out_ref[rows, :] = out.astype(BF)
        return carry[0] + fold(grad * unit), carry[1] + fold(grad)

    m, dim = x_ref.shape
    zero = jnp.zeros((8, dim), F32)
    for i, value in enumerate(over_rows(m, rows_of, (zero, zero))):
        vec_ref[i : i + 1, :] = total_of(value)


def norm_back(place, after, x, dn, dh, gain):
    m, d = x.shape
    outs = [((m, d), BF), ((2, d), F32)]
    return call(
        norm_back_kernel, "norm_back", 8, place, [], after, [x, dn, dh, gain], outs, []
    )


def pad_heads(cfg, refs):
    m, seq = cfg["m"], cfg["seq"]
    lane = lax.broadcasted_iota(jnp.int32, (m, LANES - HD), 1)
    row = lax.broadcasted_iota(jnp.int32, (m, LANES - HD), 0)
    one = jnp.where(lane == 0, 1.0, 0.0).astype(BF)
    past = jnp.where((lane == 0) & (row >= seq), -1e30, 0.0).astype(BF)
    for h in range(cfg["heads"]):
        for ref, fill in zip(refs, (one, past, one)):
            ref[h, :, HD:] = fill


def attn_fwd_kernel(cfg, piece, begin, place_ref, w_refs, a_ref, bias_ref, *refs):
    if not begin:
        acc_in, *refs = refs
    qkv_ref, o_ref, lse_ref, acc_ref, w, q_s, k_s, v_s, vt, ot, sem = refs
    m, heads, base, wide = cfg["m"], cfg["heads"], cfg["base"], cfg["wide"]
    piece.fetch(w_refs, place_ref, w, sem)
    pad_heads(cfg, (q_s, k_s, v_s))
    ot[...] = jnp.zeros_like(ot)
    lse_ref[...] = jnp.zeros_like(lse_ref)
    landed(w, sem)
    qkv_ref[...] = (nn(a_ref[...], w[:, base:]) + bias_ref[...]).astype(BF)
    span = heads * HD
    skip = span - base
    for h in range(heads):
        for n, s in enumerate((q_s, k_s, v_s)):
            at = skip + n * span + h * HD
            s[h, :, :HD] = qkv_ref[:, at : at + HD]
        vt[h] = v_s[h].T
        s = nt(k_s[h], q_s[h])
        highest = jnp.max(s, axis=0, keepdims=True) * SHARP
        p = jnp.exp2(s * SHARP - highest).astype(BF)
        mixed = nn(vt[h], p)
        total = mixed[HD : HD + 1, :]
        ot[h * HD : (h + 1) * HD, :] = mixed[:HD, :] * (1.0 / total)
        lse_ref[h : h + 1, :] = highest + jnp.log2(total)
    o_ref[...] = ot[...].T.astype(BF)
    part = nt(o_ref[...], w[:, :wide])
    acc_ref[...] = part if begin else acc_in[...] + part


def attn_fwd(cfg, place, after, piece, a, bias, acc):
    m, dim = a.shape
    qw, wide, heads, width = cfg["qw"], cfg["wide"], cfg["heads"], cfg["width"]
    begin = acc is None
    outs = [((m, qw), BF), ((m, wide), BF), ((8, m), F32), ((m, dim), F32)]
    scratch = (
        [pltpu.VMEM((dim, width), BF)]
        + [pltpu.VMEM((heads, m, LANES), BF)] * 3
        + [
            pltpu.VMEM((heads, LANES, m), BF),
            pltpu.VMEM((wide, m), F32),
            pltpu.SemaphoreType.DMA,
        ]
    )
    return call(
        partial(attn_fwd_kernel, cfg, piece, begin), "attn_fwd", 10, place, piece.arrays, after,
        [a, bias] + ([] if begin else [acc]), outs, scratch, () if begin else ((2, 3),),
    )


def attn_bwd_kernel(cfg, piece, begin, place_ref, w_refs, *refs):
    at_ref, dh_ref, dht_ref, qkv_ref, o_ref, lse_ref, *refs = refs
    if not begin:
        acc_in, *refs = refs
    ga_ref, gb_ref, sum_ref, acc_ref, *refs = refs
    w, q_s, k_s, v_s, do_s, kt, do_all, dqkv, dqt, p_s, ds_s, sem = refs
    m, heads, base, wide = cfg["m"], cfg["heads"], cfg["base"], cfg["wide"]
    tile = m // 2
    piece.fetch(w_refs, place_ref, w, sem)
    span = heads * HD
    skip = span - base
    pad_heads(cfg, (q_s, k_s))
    dqt[...] = jnp.zeros_like(dqt)
    dqkv[:, :LANES] = jnp.zeros((m, LANES), BF)
    for h in range(heads):
        v_s[h, :, HD:] = jnp.zeros((m, LANES - HD), BF)
        do_s[h, :, HD:] = jnp.zeros((m, LANES - HD), BF)
        for n, s in enumerate((q_s, k_s, v_s)):
            at = skip + n * span + h * HD
            s[h, :, :HD] = qkv_ref[:, at : at + HD]
        kt[h] = k_s[h].T
    landed(w, sem)
    do_all[...] = nn(dh_ref[...], w[:, :wide]).astype(BF)
    for h in range(heads):
        do_s[h, :, :HD] = do_all[:, h * HD : (h + 1) * HD]
        for t in range(m // tile):
            cols = slice(t * tile, (t + 1) * tile)
            p = jnp.exp2(nt(k_s[h], q_s[h, cols, :]) * SHARP - lse_ref[h : h + 1, cols])
            dp = nt(v_s[h], do_s[h, cols, :])
            ds = (p * (dp - jnp.sum(dp * p, axis=0, keepdims=True))).astype(BF)
            p_s[h % 2, :, cols] = p.astype(BF)
            ds_s[h % 2, :, cols] = ds
            dqt[h * HD : (h + 1) * HD, cols] = nn(kt[h], ds)[:HD] * SCALE
        dk = (nn(ds_s[h % 2], q_s[h]) * SCALE).astype(BF)
        dv = nn(p_s[h % 2], do_s[h]).astype(BF)
        at = skip + span + h * HD
        dqkv[:, at : at + HD] = dk[:, :HD]
        at = skip + 2 * span + h * HD
        dqkv[:, at : at + HD] = dv[:, :HD]
    dqkv[:, skip : skip + span] = dqt[...].T.astype(BF)[:, :span]
    grads = dqkv[...]
    sum_ref[...] = jnp.sum(grads.astype(F32), axis=0, keepdims=True)
    half = at_ref.shape[0] // 2
    for n, g_ref in ((1, gb_ref), (0, ga_ref)):
        rows = slice(n * half, (n + 1) * half)
        left = nn(dht_ref[rows, :], o_ref[...])
        right = nn(at_ref[rows, :], grads)
        g_ref[:, :base] = left[:, :base].astype(BF)
        g_ref[:, base:wide] = (left[:, base:] + right[:, : wide - base]).astype(BF)
        g_ref[:, wide:] = right[:, wide - base :].astype(BF)
    part = nt(grads, w[:, base:])
    acc_ref[...] = part if begin else acc_in[...] + part


def attn_bwd(cfg, place, after, piece, at, dh, dht, qkv, o, lse, acc):
    dim, m = at.shape
    qw, wide, heads, width = cfg["qw"], cfg["wide"], cfg["heads"], cfg["width"]
    begin = acc is None
    outs = [((dim // 2, width), BF), ((dim // 2, width), BF), ((1, qw), F32), ((m, dim), F32)]
    scratch = (
        [pltpu.VMEM((dim, width), BF)]
        + [pltpu.VMEM((heads, m, LANES), BF)] * 4
        + [
            pltpu.VMEM((heads, LANES, m), BF),
            pltpu.VMEM((m, wide), BF),
            pltpu.VMEM((m, qw), BF),
            pltpu.VMEM((wide, m), F32),
            pltpu.VMEM((2, m, m), BF),
            pltpu.VMEM((2, m, m), BF),
            pltpu.SemaphoreType.DMA,
        ]
    )
    return call(
        partial(attn_bwd_kernel, cfg, piece, begin), "attn_bwd", 20, place, piece.arrays, after,
        [at, dh, dht, qkv, o, lse] + ([] if begin else [acc]), outs, scratch,
        () if begin else ((6, 3),),
    )


def ffn_one_kernel(cfg, piece, place_ref, w_refs, a_ref, bias_ref, et_ref, *refs):
    g_ref, gp_ref, ga_ref, gb_ref, w, sem = refs
    piece.fetch(w_refs, place_ref, w, sem)
    landed(w, sem)
    width = g_ref.shape[1]
    for n in range(0, width, 256):
        cols = slice(n, min(n + 256, width))
        pre = nn(a_ref[...], w[:, cols]) + bias_ref[:, cols]
        square = pre * pre
        bent = jnp.tanh(pre * (GELU_A + GELU_A * GELU_B * square))
        half = 0.5 + 0.5 * bent
        g_ref[:, cols] = (pre * half).astype(BF)
        slope = half + 0.5 * pre * (1.0 - bent * bent) * (GELU_A + 3 * GELU_A * GELU_B * square)
        gp_ref[:, cols] = slope.astype(BF)
    middle = et_ref.shape[0] // 2
    gb_ref[...] = nn(et_ref[middle:, :], g_ref[...]).astype(BF)
    ga_ref[...] = nn(et_ref[:middle, :], g_ref[...]).astype(BF)


def ffn_one(cfg, place, after, piece, a, bias, et):
    dim, m = et.shape
    width = bias.shape[1]
    outs = [((m, width), BF), ((m, width), BF), ((dim // 2, width), BF), ((dim // 2, width), BF)]
    return call(
        partial(ffn_one_kernel, cfg, piece), "ffn_one", 9, place, piece.arrays, after,
        [a, bias, et], outs, [pltpu.VMEM((dim, width), BF), pltpu.SemaphoreType.DMA],
    )


def ffn_two_kernel(cfg, ups, downs, begin, place_ref, w_refs, eb_ref, at_ref, g_ref, gp_ref, *refs):
    if not begin:
        feed_in, dn_in, *refs = refs
    ga_ref, gb_ref, sum_ref, feed_ref, dn_ref, wu, wd, dz, sems = refs
    count = len(ups.arrays)
    downs.fetch(w_refs[count:], place_ref, wd, sems.at[1])
    ups.fetch(w_refs[:count], place_ref, wu, sems.at[0])
    landed(wd, sems.at[1])
    width = g_ref.shape[1]
    for n in range(0, width, 256):
        cols = slice(n, min(n + 256, width))
        grad = (nn(eb_ref[...], wd[:, cols]) * gp_ref[:, cols].astype(F32)).astype(BF)
        dz[:, cols] = grad
        sum_ref[:, cols] = jnp.sum(grad.astype(F32), axis=0, keepdims=True)
    middle = at_ref.shape[0] // 2
    gb_ref[...] = nn(at_ref[middle:, :], dz[...]).astype(BF)
    ga_ref[...] = nn(at_ref[:middle, :], dz[...]).astype(BF)
    landed(wu, sems.at[0])
    part = nt(g_ref[...], wd[...])
    feed_ref[...] = part if begin else feed_in[...] + part
    part = nt(dz[...], wu[...])
    dn_ref[...] = part if begin else dn_in[...] + part


def ffn_two(cfg, place, after, ups, downs, eb, at, g, gp, feed, dn):
    dim, m = at.shape
    width = g.shape[1]
    begin = feed is None
    outs = [
        ((dim // 2, width), BF), ((dim // 2, width), BF), ((1, width), F32), ((m, dim), F32),
        ((m, dim), F32),
    ]
    return call(
        partial(ffn_two_kernel, cfg, ups, downs, begin), "ffn_two", 14, place,
        ups.arrays + downs.arrays, after,
        [eb, at, g, gp] + ([] if begin else [feed, dn]), outs,
        [
            pltpu.VMEM((dim, width), BF),
            pltpu.VMEM((dim, width), BF),
            pltpu.VMEM((m, width), BF),
            pltpu.SemaphoreType.DMA((2,)),
        ],
        () if begin else ((4, 3), (5, 4)),
    )


CORE, ACROSS, ALONG = 1, 2, 4
CUBE = 8
ORDER = (0, ACROSS, ALONG, ACROSS + ALONG, CORE, CORE + ACROSS, CORE + ALONG, CORE + ACROSS + ALONG)


def ring(value, by, size):
    return lax.ppermute(value, "tensor", [(i, (i + by) % size) for i in range(size)])


def swap(value, offset):
    return lax.ppermute(value, "dp", [(i, i ^ offset) for i in range(lax.axis_size("dp"))])


def tie(value, *others):
    return lax.optimization_barrier((value, *others))[0]


def gather_all(own, split):
    dp, size = lax.axis_size("dp"), lax.axis_size("tensor")
    rows = own.shape[0]
    full = lax.all_gather(own, ("dp", "tensor"), axis=0, tiled=False)
    if split:

        def blocks(k, d, z):
            t = lax.rem(z - k + size, size)
            return [(0, i * size + t, i * rows, rows) for i in range(dp)]
    else:
        full = full.reshape(dp, size, rows, -1).transpose(1, 0, 2, 3)
        full = full.reshape(size, dp * rows, -1)

        def blocks(k, d, z):
            return [(0, lax.rem(z - k + size, size), 0, dp * rows)]

    return [Piece([full], partial(blocks, k)) for k in range(size)]


def gather_ring(own):
    size = lax.axis_size("tensor")
    held = [own]
    for _ in range(size - 1):
        held.append(ring(held[-1], 1, size))
    return held


def gather_near(held, group):
    mine = jnp.stack(held[2 * group : 2 * group + 2])
    return jnp.stack([mine, swap(mine, (ACROSS, ALONG)[group])])


def gather_far(both, group):
    return swap(both, (ALONG, ACROSS)[group])


def gather_core(both, far, group, rows):
    first, second = ((ACROSS, ALONG), (ALONG, ACROSS))[group]
    arrays = [both, far, swap(both, CORE), swap(far, CORE)]

    def blocks(n, d, z):
        return [
            (
                index,
                (other, n),
                pl.multiple_of(jnp.bitwise_xor(d, offset + other * first) * rows, 16),
                rows,
            )
            for index, offset in enumerate((0, second, CORE, CORE + second))
            for other in range(2)
        ]

    return [Piece(arrays, partial(blocks, n)) for n in range(2)]


def scatter_all(near, far, cube):
    size, dp = lax.axis_size("tensor"), lax.axis_size("dp")
    d, z = lax.axis_index("dp"), lax.axis_index("tensor")
    pieces = jnp.stack([jnp.concatenate(halves) for halves in zip(near, far)])
    dim, width = pieces.shape[1:]
    rows = dim // dp
    pieces = pieces.reshape(size, dp, rows, width).transpose(1, 0, 2, 3)
    order = jnp.stack([lax.rem(z - t + size, size) for t in range(size)])
    index = (jnp.arange(dp)[:, None] * size + order[None]).reshape(-1)
    absolute = jnp.take(pieces.reshape(dp * size, rows, width), index, axis=0)
    return lax.psum_scatter(absolute, ("dp", "tensor"), scatter_dimension=0, tiled=True)[0].astype(F32)


def add(*terms):
    total = terms[0].astype(F32)
    for term in terms[1:]:
        total = total + term.astype(F32)
    return total


class Scatter:
    def __init__(self, near, far, first, second):
        half, self.width = near[0].shape
        self.quarter = half // 4
        self.near = [self.shaped(v) for v in near]
        self.far = far
        self.first, self.second = first, second

    def shaped(self, value):
        return value.reshape(2, 2, self.quarter, self.width)

    def pick(self, value, i, j):
        return value[j, i] if self.first == ACROSS else value[i, j]

    def step_core(self):
        self.core = [self.shaped(swap(v, CORE)) for v in self.far]
        return self.core

    def step_first(self):
        out = [
            add(self.pick(a, 1, j), self.pick(b, 1, j)).astype(BF)
            for j in range(2)
            for a, b in zip(self.near, self.core)
        ]
        self.one = swap(jnp.stack(out), self.first)
        return [self.one]

    def step_second(self):
        count = len(self.near)
        out = [
            add(self.pick(a, 0, 1), self.pick(b, 0, 1), self.one[count + i]).astype(BF)
            for i, (a, b) in enumerate(zip(self.near, self.core))
        ]
        self.two = swap(jnp.stack(out), self.second)
        return [self.two]

    def terms(self, i):
        return [
            self.pick(self.near[i], 0, 0), self.pick(self.core[i], 0, 0), self.one[i], self.two[i]
        ]


def sum_all(vector, cube):
    if not cube:
        return lax.psum(vector, ("dp", "tensor"))
    size = lax.axis_size("tensor")
    for offset in (CORE, ACROSS, ALONG):
        vector = vector + swap(vector, offset)
    offset = 1
    while offset < size:
        vector = vector + lax.ppermute(vector, "tensor", [(i, i ^ offset) for i in range(size)])
        offset *= 2
    return vector


def on_device(
    tokens, image_flags, cotangent, gain_one, shift_one, w_query, b_query, w_key, w_value, b_value,
    w_out, b_out, gain_two, shift_two, w_up, b_up, w_down, b_down,
):
    dp, size = lax.axis_size("dp"), lax.axis_size("tensor")
    d, z = lax.axis_index("dp"), lax.axis_index("tensor")
    images = image_flags.shape[0]
    all_rows, dim = tokens.shape
    seq = all_rows // images
    assert images == size
    m = up(seq, 256)
    rows = dim // dp
    split = rows % 16 == 0
    span = w_query.shape[1]
    units = w_up.shape[1]
    hidden = up(units, LANES)
    width = 4 * span
    base, wide = span // LANES * LANES, up(span, LANES)
    qw = width - base
    cube = dp == CUBE and split and size == 4
    cfg = dict(m=m, seq=seq, heads=span // HD, base=base, wide=wide, width=width, qw=qw)
    cfg.update(rows=rows, order=ORDER if cube else None)

    own_attn = jnp.concatenate([w_out.T, w_query, w_key, w_value], axis=1).astype(BF)
    own_up = jnp.pad(w_up.astype(BF), ((0, 0), (0, hidden - units)))
    own_down = jnp.pad(w_down.T.astype(BF), ((0, 0), (0, hidden - units)))
    skip = jnp.zeros((span - base,), F32)
    own_bias = jnp.concatenate(
        [skip, b_query, jnp.zeros((span,), F32), b_value, b_up, jnp.zeros((hidden - units,), F32)]
    )[None]
    bias = [own_bias] + [ring(own_bias, k, size) for k in range(1, size)]
    flag = lax.dynamic_index_in_dim(image_flags, z, 0, keepdims=False)
    place = jnp.stack([d, z, flag]).astype(jnp.int32)

    pad_rows = ((0, m - seq), (0, 0))
    x = jnp.pad(lax.dynamic_slice_in_dim(tokens, z * seq, seq, 0), pad_rows)
    eb = jnp.pad(lax.dynamic_slice_in_dim(cotangent, z * seq, seq, 0) * flag.astype(BF), pad_rows)
    a1, a1t, et, sum_e = norm_one(cfg, place, x, eb, gain_one[None], shift_one[None])

    pins = [[] for _ in range(2 * size)]
    if cube:
        held = gather_ring(own_attn)
        both = [gather_near(held, 0), gather_near(held, 1)]
        far = [gather_far(both[0], 0), gather_far(both[1], 1)]
        attn_w = gather_core(both[0], far[0], 0, rows) + gather_core(both[1], far[1], 1, rows)
        up_held = gather_ring(tie(own_up, held[-1]))
        down_held = gather_ring(tie(own_down, up_held[-1]))
        up_held = [tie(v, far[0]) for v in up_held]
        both_up = [gather_near(up_held, 0), gather_near(up_held, 1)]
        far_up = [gather_far(tie(both_up[i], far[1]), i) for i in range(2)]
        up_w = gather_core(both_up[0], far_up[0], 0, rows) + gather_core(both_up[1], far_up[1], 1, rows)
        down_held = [tie(v, far_up[0]) for v in down_held]
        both_down = [gather_near(down_held, 0), gather_near(down_held, 1)]
        far_down = [gather_far(tie(both_down[i], far_up[1]), i) for i in range(2)]
        down_w = gather_core(both_down[0], far_down[0], 0, rows) + gather_core(
            both_down[1], far_down[1], 1, rows
        )
        pins[0] = [up_held[-1]]
        pins[2] = [*both_up]
        pins[3] = []
    else:
        attn_w, up_w, down_w = (gather_all(w, split) for w in (own_attn, own_up, own_down))
    every = list(range(size))
    att, kept = None, []
    for k in every:
        *saved, att = attn_fwd(cfg, place, pins[k], attn_w[k], a1, bias[k][:, :qw], att)
        kept.append(saved)
    h, a2, a2t = norm_two(cfg, place, [], x, att, b_out[None], gain_two[None], shift_two[None])
    hidden_of, down_near, down_far = [], [], []
    for k in every:
        g, gp, near, far_half = ffn_one(cfg, place, pins[size + k], up_w[k], a2, bias[k][:, qw:], et)
        hidden_of.append((g, gp))
        down_near.append(near)
        down_far.append(far_half)

    feed = dn2 = dn1 = None
    sum_dz, up_near, up_far = [None] * size, [None] * size, [None] * size
    sum_qkv, attn_near, attn_far = [None] * size, [None] * size, [None] * size
    back = list(reversed(every))
    after = {}
    if cube:
        down_out = [
            Scatter([down_near[3], down_near[2]], [down_far[3], down_far[2]], ACROSS, ALONG),
            Scatter([down_near[1], down_near[0]], [down_far[1], down_far[0]], ALONG, ACROSS),
        ]
        after["f2"] = down_out[0].step_core() + down_out[1].step_core()
        after["f0"] = down_out[0].step_first() + down_out[1].step_first()
        after["a3"] = down_out[0].step_second() + down_out[1].step_second()
    for k in back:
        up_near[k], up_far[k], sum_dz[k], feed, dn2 = ffn_two(
            cfg, place, after.get(f"f{k}", []), up_w[k], down_w[k], eb, a2t, *hidden_of[k], feed, dn2
        )
    if cube:
        up_out = [
            Scatter([up_near[3], up_near[2]], [up_far[3], up_far[2]], ACROSS, ALONG),
            Scatter([up_near[1], up_near[0]], [up_far[1], up_far[0]], ALONG, ACROSS),
        ]
        after["b"] = up_out[0].step_core()
        after["a3"] += up_out[1].step_core()
        after["a1"] = up_out[0].step_first() + up_out[1].step_first()
        after["a0"] = up_out[0].step_second() + up_out[1].step_second()
    mixed, dh, dhb, dht, vec_two = norm_two_back(
        cfg, place, after.get("b", []), h, feed, dn2, eb, b_down[None], gain_two[None]
    )
    attn_out = {}
    for k in back:
        attn_near[k], attn_far[k], sum_qkv[k], dn1 = attn_bwd(
            cfg, place, after.get(f"a{k}", []), attn_w[k], a1t, dhb, dht, *kept[k], dn1
        )
        if cube:
            links = (ACROSS, ALONG) if k % 2 else (ALONG, ACROSS)
            attn_out[k] = Scatter([attn_near[k]], [attn_far[k]], *links)
            if k > 1:
                after[f"a{k - 2}"] = after.get(f"a{k - 2}", []) + attn_out[k].step_core()
            if k == 3:
                after["a0"] += attn_out[k].step_first()
            if k == 1:
                after["n"] = attn_out[3].step_second() + attn_out[2].step_first()
                after["n"] += attn_out[1].step_core()
    tokens_grad, vec_one = norm_back(place, after.get("n", []), x, dn1, dh, gain_one[None])

    if cube:
        attn_out[0].step_core()
        attn_out[1].step_first()
        attn_out[2].step_second()
        attn_out[0].step_first()
        attn_out[1].step_second()
        attn_out[0].step_second()

        def along_z(terms):
            total = add(*terms(size - 1))
            for k in range(size - 2, -1, -1):
                total = add(*terms(k), ring(total.astype(BF), -1, size))
            return total

        grad_down = along_z(lambda k: down_out[k < 2].terms((3 - k) % 2))
        grad_up = along_z(lambda k: up_out[k < 2].terms((3 - k) % 2))
        grad_attn = along_z(lambda k: attn_out[k].terms(0))
    else:
        grad_down = scatter_all(down_near, down_far, cube)
        grad_up = scatter_all(up_near, up_far, cube)
        grad_attn = scatter_all(attn_near, attn_far, cube)
    grad_down = grad_down[:, :units].T
    grad_up = grad_up[:, :units]
    pieces = jnp.concatenate([jnp.concatenate(sum_qkv), jnp.concatenate(sum_dz)], axis=1)
    order = jnp.stack([lax.rem(z - t + size, size) for t in range(size)])
    pieces = jnp.take(pieces, order, axis=0)
    sums = sum_all(
        jnp.concatenate([pieces.reshape(-1), vec_one.reshape(-1), vec_two.reshape(-1), sum_e[0]]),
        cube,
    )
    per = qw + hidden
    mine = lax.dynamic_index_in_dim(sums[: size * per].reshape(size, per), z, 0, keepdims=False)
    rest = sums[size * per :].reshape(6, dim)
    at = span - base
    return (
        mixed[:seq],
        tokens_grad[:seq],
        rest[0],
        rest[1],
        grad_attn[:, span : 2 * span],
        mine[at : at + span],
        grad_attn[:, 2 * span : 3 * span],
        grad_attn[:, 3 * span :],
        mine[at + 2 * span : at + 3 * span],
        grad_attn[:, :span].T,
        rest[4],
        rest[2],
        rest[3],
        grad_up,
        mine[qw : qw + units],
        grad_down,
        rest[5],
    )


SPECS_IN = (
    P("dp", None), P("dp"), P("dp", None), P(), P(), P("dp", "tensor"), P("tensor"),
    P("dp", "tensor"), P("dp", "tensor"), P("tensor"), P("tensor", "dp"), P(), P(), P(),
    P("dp", "tensor"), P("tensor"), P("tensor", "dp"), P(),
)
SPECS_OUT = (
    P(("dp", "tensor"), None), P(("dp", "tensor"), None), P(), P(), P("dp", "tensor"), P("tensor"),
    P("dp", "tensor"), P("dp", "tensor"), P("tensor"), P("tensor", "dp"), P(), P(), P(),
    P("dp", "tensor"), P("tensor"), P("tensor", "dp"), P(),
)


def solution(mesh):
    return jax.shard_map(
        on_device, mesh=mesh, in_specs=SPECS_IN, out_specs=SPECS_OUT, check_vma=False
    )
```

```python
from functools import partial

import jax
import jax.numpy as jnp
from jax import lax
from jax.experimental import pallas as pl
from jax.experimental.pallas import tpu as pltpu
from jax.sharding import PartitionSpec as P

HD = 72
LANES = 128
EPSILON = 1e-06
SCALE = HD**-0.5
SHARP = SCALE * 1.4426950408889634
GELU_A = 0.7978845608028654
GELU_B = 0.044715
BF = jnp.bfloat16
F32 = jnp.float32
ANY = pl.BlockSpec(memory_space=pl.ANY)
SMEM = pl.BlockSpec(memory_space=pltpu.SMEM)
VMEM = pl.BlockSpec(memory_space=pltpu.VMEM)


def up(value, step):
    return -(-value // step) * step


def nn(left, right):
    return lax.dot_general(left, right, (((1,), (0,)), ((), ())), preferred_element_type=F32)


def nt(left, right):
    return lax.dot_general(left, right, (((1,), (1,)), ((), ())), preferred_element_type=F32)


def whole(shape):
    return pl.BlockSpec(shape, lambda *_: (0,) * len(shape), pipeline_mode=pl.Buffered(1))


def stepped(shape, index=lambda i: i):
    return pl.BlockSpec((1,) + shape, lambda i, *_: (index(i),) + (0,) * len(shape))


def call(
    kernel, name, us, place, weights, after, ins, outs, scratch, late=(), grid=None, specs=None, mib=40,
    prefetch=False,
):
    weights, after, late = list(weights), list(after), list(late)
    lead = 1 + len(weights) + len(after) + len(late)
    scratch = list(scratch)
    if late:
        scratch += [pltpu.VMEM(v.shape, v.dtype) for v in late] + [pltpu.SemaphoreType.DMA((len(late),))]

    def body(*refs):
        if not late:
            return kernel(refs[0], refs[1 : 1 + len(weights)], *refs[lead:])
        n = len(late)
        *rest, sems = refs[lead:]
        inputs = Late(refs[lead - n : lead], rest[-n:], sems)
        return kernel(refs[0], refs[1 : 1 + len(weights)], *rest[:-n], inputs)

    in_specs, out_specs = specs or ([VMEM] * len(ins), [VMEM] * len(outs))
    return pl.pallas_call(
        body,
        grid_spec=pltpu.PrefetchScalarGridSpec(
            num_scalar_prefetch=1 if prefetch else 0,
            grid=grid or (),
            in_specs=([] if prefetch else [SMEM]) + [ANY] * (lead - 1) + list(in_specs),
            out_specs=list(out_specs),
            scratch_shapes=scratch,
        ),
        out_shape=[jax.ShapeDtypeStruct(*out) for out in outs],
        compiler_params=pltpu.CompilerParams(vmem_limit_bytes=mib * 2**20),
        cost_estimate=pl.CostEstimate(
            flops=int(us * 1.15e9), bytes_accessed=int(us * 1e5), transcendentals=0
        ),
        name=name,
    )(place, *weights, *after, *late, *ins)


class Late:
    def __init__(self, sources, buffers, sems):
        self.buffers = buffers
        self.copies = [
            pltpu.make_async_copy(source, buffer, sems.at[i])
            for i, (source, buffer) in enumerate(zip(sources, buffers))
        ]

    def start(self):
        for copy in self.copies:
            copy.start()

    def take(self, i):
        self.copies[i].wait()
        return self.buffers[i]


class Piece:
    def __init__(self, arrays, blocks):
        self.arrays, self.blocks = arrays, blocks

    def fetch(self, refs, place_ref, buffer, sem, columns=None):
        for array, lead, first, rows in self.blocks(place_ref[0], place_ref[1]):
            source = refs[array].at[lead]
            if columns is not None:
                source = source.at[:, :columns]
            pltpu.make_async_copy(source, buffer.at[pl.ds(first, rows), :], sem).start()


def fetch_step(pieces, which, refs, place_ref, buffer, sem):
    begin = 0
    for index, piece in enumerate(pieces):
        mine = refs[begin : begin + len(piece.arrays)]
        begin += len(piece.arrays)

        @pl.when(which == index)
        def _():
            piece.fetch(mine, place_ref, buffer, sem)


def arrays_of(pieces):
    return [array for piece in pieces for array in piece.arrays]


def landed(buffer, sem):
    pltpu.make_async_copy(buffer, buffer, sem).wait()


def turn(cfg, d, value, out_ref, scratch):
    rows, order = cfg["rows"], cfg["order"]
    if order is None:
        out_ref[...] = value.T
        return
    scratch[...] = value.T
    for place, offset in enumerate(order):
        first = pl.multiple_of(jnp.bitwise_xor(d, offset) * rows, 16)
        out_ref[place * rows : (place + 1) * rows, :] = scratch[pl.ds(first, rows), :]


STEP = 32


def over_rows(total, body, carry):
    def step(t, carry):
        return body(pl.ds(pl.multiple_of(t * STEP, STEP), STEP), carry)

    return lax.fori_loop(0, total // STEP, step, carry)


def norm_stats(rows):
    average = jnp.mean(rows, axis=-1, keepdims=True)
    centred = rows - average
    inverse = lax.rsqrt(jnp.mean(centred * centred, axis=-1, keepdims=True) + EPSILON)
    return centred * inverse, inverse


def fold(value):
    return jnp.sum(value.reshape(STEP // 8, 8, value.shape[1]), axis=0)


def total_of(partial_sums):
    return jnp.sum(partial_sums, axis=0, keepdims=True)


def norm_one_kernel(
    cfg, place_ref, _, x_ref, eb_ref, gain_ref, shift_ref, a_ref, at_ref, et_ref, sum_ref, scratch
):
    def rows_of(rows, carry):
        unit, _ = norm_stats(x_ref[rows, :].astype(F32))
        a_ref[rows, :] = (unit * gain_ref[...] + shift_ref[...]).astype(BF)
        return carry + fold(eb_ref[rows, :].astype(F32))

    m, dim = x_ref.shape
    sum_ref[...] = total_of(over_rows(m, rows_of, jnp.zeros((8, dim), F32)))
    turn(cfg, place_ref[0], a_ref[...], at_ref, scratch)
    et_ref[...] = eb_ref[...].T


def norm_one(cfg, place, x, eb, gain, shift):
    m, d = x.shape
    outs = [((m, d), BF), ((d, m), BF), ((d, m), BF), ((1, d), F32)]
    return call(
        partial(norm_one_kernel, cfg), "norm_one", 6, place, [], [], [x, eb, gain, shift], outs,
        [pltpu.VMEM((d, m), BF)],
    )


def norm_two_kernel(cfg, pieces, place_ref, w_refs, b_out, gain, shift, *refs):
    n = len(pieces)
    h_ref, a_ref, at_ref, w, scratch, sems, late = refs
    late.start()
    begin = 0
    for i, piece in enumerate(pieces):
        mine = w_refs[begin : begin + len(piece.arrays)]
        begin += len(piece.arrays)
        piece.fetch(mine, place_ref, w.at[i], sems.at[i], cfg["wide"])
    for i in range(n):
        landed(w.at[i], sems.at[i])
        part = nt(late.take(i)[...], w[i])
        h_ref[...] = part if i == 0 else h_ref[...] + part
    x_ref = late.take(n)

    def rows_of(rows, carry):
        h = x_ref[rows, :].astype(F32) + h_ref[rows, :] + b_out[...]
        h_ref[rows, :] = h
        unit, _ = norm_stats(h)
        a_ref[rows, :] = (unit * gain[...] + shift[...]).astype(BF)
        return carry

    over_rows(x_ref.shape[0], rows_of, 0)
    turn(cfg, place_ref[0], a_ref[...], at_ref, scratch)


def norm_two(cfg, place, after, pieces, x, b_out, gain, shift, o):
    m, d = x.shape
    n = len(pieces)
    outs = [((m, d), F32), ((m, d), BF), ((d, m), BF)]
    return call(
        partial(norm_two_kernel, cfg, pieces), "norm_two", 12, place, arrays_of(pieces), after,
        [b_out, gain, shift], outs,
        [
            pltpu.VMEM((n, d, cfg["wide"]), BF),
            pltpu.VMEM((d, m), BF),
            pltpu.SemaphoreType.DMA((n,)),
        ],
        late=[*o, x],
    )


def mixed_kernel(pieces, place_ref, w_refs, h_ref, g_ref, b_down, out_ref, acc, w, sems):
    step = pl.program_id(0)
    flag = place_ref[2].astype(F32)

    @pl.when(step == 0)
    def _():
        fetch_step(pieces, 0, w_refs, place_ref, w.at[0], sems.at[0])
        acc[...] = h_ref[...] + b_down[...]

    slot = lax.rem(step, 2)
    fetch_step(pieces, step + 1, w_refs, place_ref, w.at[1 - slot], sems.at[1 - slot])
    landed(w.at[slot], sems.at[slot])
    acc[...] += nt(g_ref[0], w[slot])

    @pl.when(step == len(pieces) - 1)
    def _():
        out_ref[...] = (acc[...] * flag).astype(BF)


def mix(place, after, pieces, h, g, b_down):
    m, d = h.shape
    width = g.shape[2]
    return call(
        partial(mixed_kernel, pieces), "mixed", 14, place, arrays_of(pieces), after, [h, g, b_down],
        [((m, d), BF)],
        [pltpu.VMEM((m, d), F32), pltpu.VMEM((2, d, width), BF), pltpu.SemaphoreType.DMA((2,))],
        grid=(len(pieces),),
        specs=([whole((m, d)), stepped((m, width)), whole((1, d))], [whole((m, d))]),
    )[0]


def norm_back_kernel(cfg, pieces, place_ref, w_refs, gain, *refs):
    n = len(pieces)
    out_ref, vec_ref, dn, w, sems, late = refs
    late.start()
    parts, begin = [], 0
    for piece in pieces:
        parts.append(w_refs[begin : begin + len(piece.arrays)])
        begin += len(piece.arrays)
    pieces[0].fetch(parts[0], place_ref, w.at[0], sems.at[0])
    for i in range(n):
        if i + 1 < n:
            pieces[i + 1].fetch(parts[i + 1], place_ref, w.at[(i + 1) % 2], sems.at[(i + 1) % 2])
        landed(w.at[i % 2], sems.at[i % 2])
        part = nt(late.take(i)[...], w[i % 2, :, cfg["base"] :])
        dn[...] = part if i == 0 else dn[...] + part
    x_ref, dh_ref = late.take(n), late.take(n + 1)

    def rows_of(rows, carry):
        unit, inverse = norm_stats(x_ref[rows, :].astype(F32))
        grad = dn[rows, :]
        scaled = grad * gain[...]
        out = dh_ref[rows, :] + inverse * (
            scaled
            - jnp.mean(scaled, axis=-1, keepdims=True)
            - unit * jnp.mean(scaled * unit, axis=-1, keepdims=True)
        )
        out_ref[rows, :] = out.astype(BF)
        return carry[0] + fold(grad * unit), carry[1] + fold(grad)

    m, dim = x_ref.shape
    zero = jnp.zeros((8, dim), F32)
    for i, value in enumerate(over_rows(m, rows_of, (zero, zero))):
        vec_ref[i : i + 1, :] = total_of(value)


def norm_back(cfg, place, after, pieces, x, dh, gain, grads):
    m, d = x.shape
    outs = [((m, d), BF), ((2, d), F32)]
    return call(
        partial(norm_back_kernel, cfg, pieces), "norm_back", 18, place, arrays_of(pieces), after,
        [gain], outs,
        [
            pltpu.VMEM((m, d), F32),
            pltpu.VMEM((2, d, cfg["width"]), BF),
            pltpu.SemaphoreType.DMA((2,)),
        ],
        late=[*grads, x, dh],
    )


def pad_heads(cfg, refs):
    m, seq = cfg["m"], cfg["seq"]
    lane = lax.broadcasted_iota(jnp.int32, (m, LANES - HD), 1)
    row = lax.broadcasted_iota(jnp.int32, (m, LANES - HD), 0)
    one = jnp.where(lane == 0, 1.0, 0.0).astype(BF)
    past = jnp.where((lane == 0) & (row >= seq), -1e30, 0.0).astype(BF)
    for h in range(cfg["heads"]):
        for ref, fill in zip(refs, (one, past, one)):
            ref[h, :, HD:] = fill


def attn_fwd_kernel(cfg, piece, place_ref, w_refs, a_ref, bias_ref, *refs):
    qkv_ref, o_ref, lse_ref, w, q_s, k_s, v_s, vt, ot, sem = refs
    m, heads, base, wide = cfg["m"], cfg["heads"], cfg["base"], cfg["wide"]
    piece.fetch(w_refs, place_ref, w, sem)
    pad_heads(cfg, (q_s, k_s, v_s))
    ot[...] = jnp.zeros_like(ot)
    lse_ref[...] = jnp.zeros_like(lse_ref)
    landed(w, sem)
    qkv_ref[...] = (nn(a_ref[...], w[:, base:]) + bias_ref[...]).astype(BF)
    span = heads * HD
    skip = span - base
    for h in range(heads):
        for n, s in enumerate((q_s, k_s, v_s)):
            at = skip + n * span + h * HD
            s[h, :, :HD] = qkv_ref[:, at : at + HD]
        vt[h] = v_s[h].T
        s = nt(k_s[h], q_s[h])
        highest = jnp.max(s, axis=0, keepdims=True) * SHARP
        p = jnp.exp2(s * SHARP - highest).astype(BF)
        mixed = nn(vt[h], p)
        total = mixed[HD : HD + 1, :]
        ot[h * HD : (h + 1) * HD, :] = mixed[:HD, :] * (1.0 / total)
        lse_ref[h : h + 1, :] = highest + jnp.log2(total)
    o_ref[...] = ot[...].T.astype(BF)


def attn_fwd(cfg, place, after, piece, a, bias):
    m, dim = a.shape
    qw, wide, heads, width = cfg["qw"], cfg["wide"], cfg["heads"], cfg["width"]
    outs = [((m, qw), BF), ((m, wide), BF), ((8, m), F32)]
    scratch = (
        [pltpu.VMEM((dim, width), BF)]
        + [pltpu.VMEM((heads, m, LANES), BF)] * 3
        + [
            pltpu.VMEM((heads, LANES, m), BF),
            pltpu.VMEM((wide, m), F32),
            pltpu.SemaphoreType.DMA,
        ]
    )
    return call(
        partial(attn_fwd_kernel, cfg, piece), "attn_fwd", 8, place, piece.arrays, after, [a, bias],
        outs, scratch, mib=28,
    )


def attn_bwd_kernel(cfg, piece, place_ref, w_refs, *refs):
    dh_ref, qkv_ref, lse_ref, ga_ref, gb_ref, sum_ref, dqkv, *refs = refs
    w, q_s, k_s, v_s, do_s, kt, do_all, dqt, p_s, ds_s, sem, late = refs
    m, heads, base, wide = cfg["m"], cfg["heads"], cfg["base"], cfg["wide"]
    tile = m // 2
    piece.fetch(w_refs, place_ref, w, sem, wide)
    late.start()
    span = heads * HD
    skip = span - base
    pad_heads(cfg, (q_s, k_s))
    dqt[...] = jnp.zeros_like(dqt)
    dqkv[:, :LANES] = jnp.zeros((m, LANES), BF)
    for h in range(heads):
        v_s[h, :, HD:] = jnp.zeros((m, LANES - HD), BF)
        do_s[h, :, HD:] = jnp.zeros((m, LANES - HD), BF)
        for n, s in enumerate((q_s, k_s, v_s)):
            at = skip + n * span + h * HD
            s[h, :, :HD] = qkv_ref[:, at : at + HD]
        kt[h] = k_s[h].T
    landed(w, sem)
    do_all[...] = nn(dh_ref[...], w[...]).astype(BF)
    for h in range(heads):
        do_s[h, :, :HD] = do_all[:, h * HD : (h + 1) * HD]
        for t in range(m // tile):
            cols = slice(t * tile, (t + 1) * tile)
            p = jnp.exp2(nt(k_s[h], q_s[h, cols, :]) * SHARP - lse_ref[h : h + 1, cols])
            dp = nt(v_s[h], do_s[h, cols, :])
            ds = (p * (dp - jnp.sum(dp * p, axis=0, keepdims=True))).astype(BF)
            p_s[h % 2, :, cols] = p.astype(BF)
            ds_s[h % 2, :, cols] = ds
            dqt[h * HD : (h + 1) * HD, cols] = nn(kt[h], ds)[:HD] * SCALE
        dk = (nn(ds_s[h % 2], q_s[h]) * SCALE).astype(BF)
        dv = nn(p_s[h % 2], do_s[h]).astype(BF)
        at = skip + span + h * HD
        dqkv[:, at : at + HD] = dk[:, :HD]
        at = skip + 2 * span + h * HD
        dqkv[:, at : at + HD] = dv[:, :HD]
    dqkv[:, skip : skip + span] = dqt[...].T.astype(BF)[:, :span]
    grads = dqkv[...]
    sum_ref[...] = jnp.sum(grads.astype(F32), axis=0, keepdims=True)
    at_ref, dht_ref, o_ref = (late.take(i) for i in range(3))
    half = at_ref.shape[0] // 2
    for n, g_ref in ((1, gb_ref), (0, ga_ref)):
        rows = slice(n * half, (n + 1) * half)
        left = nn(dht_ref[rows, :], o_ref[...])
        right = nn(at_ref[rows, :], grads)
        g_ref[0, :, :base] = left[:, :base].astype(BF)
        g_ref[0, :, base:wide] = (left[:, base:] + right[:, : wide - base]).astype(BF)
        g_ref[0, :, wide:] = right[:, wide - base :].astype(BF)


def attn_bwd(cfg, place, after, piece, at, dh, dht, qkv, o, lse):
    dim, m = at.shape
    qw, wide, heads, width = cfg["qw"], cfg["wide"], cfg["heads"], cfg["width"]
    outs = [((1, dim // 2, width), BF)] * 2 + [((1, qw), F32), ((m, qw), BF)]
    scratch = (
        [pltpu.VMEM((dim, wide), BF)]
        + [pltpu.VMEM((heads, m, LANES), BF)] * 4
        + [
            pltpu.VMEM((heads, LANES, m), BF),
            pltpu.VMEM((m, wide), BF),
            pltpu.VMEM((wide, m), F32),
            pltpu.VMEM((2, m, m), BF),
            pltpu.VMEM((2, m, m), BF),
            pltpu.SemaphoreType.DMA,
        ]
    )
    return call(
        partial(attn_bwd_kernel, cfg, piece), "attn_bwd", 17, place, piece.arrays, after,
        [dh, qkv, lse], outs, scratch, late=[at, dht, o], mib=36,
    )


def ffn_one_kernel(cfg, pieces, place_ref, w_refs, a_ref, bias_ref, *refs):
    g_ref, gp_ref, grad_ref, w, sems, late = refs
    step = pl.program_id(0)

    @pl.when(step == 0)
    def _():
        late.start()
        fetch_step(pieces, 0, w_refs, place_ref, w.at[0], sems.at[0])

    slot = lax.rem(step, 2)
    fetch_step(pieces, step + 1, w_refs, place_ref, w.at[1 - slot], sems.at[1 - slot])
    landed(w.at[slot], sems.at[slot])
    width = g_ref.shape[2]
    for n in range(0, width, 256):
        cols = slice(n, min(n + 256, width))
        pre = nn(a_ref[...], w[slot, :, cols]) + bias_ref[0, :, cols]
        square = pre * pre
        bent = jnp.tanh(pre * (GELU_A + GELU_A * GELU_B * square))
        half = 0.5 + 0.5 * bent
        g_ref[0, :, cols] = (pre * half).astype(BF)
        slope = half + 0.5 * pre * (1.0 - bent * bent) * (GELU_A + 3 * GELU_A * GELU_B * square)
        gp_ref[0, :, cols] = slope.astype(BF)

    @pl.when(step == 0)
    def _():
        late.take(0)

    et_ref = late.buffers[0]
    count, _, rows, _ = grad_ref.shape
    for part in range(2):
        half = et_ref.shape[0] // 2
        value = nn(et_ref[part * half : (part + 1) * half, :], g_ref[0]).astype(BF)
        for i in range(count // 2):
            grad_ref[part * count // 2 + i, 0] = value[i * rows : (i + 1) * rows]


def ffn_one(cfg, place, after, pieces, a, bias, et):
    dim, m = et.shape
    n, width = len(pieces), bias.shape[2]
    rows = cfg["rows"] if cfg["rows"] % 16 == 0 else dim // 2
    outs = [((n, m, width), BF)] * 2 + [((dim // rows, n, rows, width), BF)]
    return call(
        partial(ffn_one_kernel, cfg, pieces), "ffn_one", 30, place, arrays_of(pieces), after,
        [a, bias], outs,
        [pltpu.VMEM((2, dim, width), BF), pltpu.SemaphoreType.DMA((2,))],
        late=[et], grid=(n,),
        specs=(
            [whole((m, dim)), stepped((1, width))],
            [stepped((m, width))] * 2
            + [
                pl.BlockSpec(
                    (dim // rows, 1, rows, width),
                    lambda i, place_ref: (0, lax.rem(place_ref[1] - i + n, n), 0, 0),
                )
            ],
        ),
        mib=56, prefetch=True,
    )


def ffn_two_kernel(cfg, ups, downs, first, last, place_ref, w_refs, eb_ref, gp_ref, *refs):
    *refs, late = refs
    if last:
        gain, *refs = refs
    near_ref, far_ref, sum_ref, *refs = refs
    if last:
        dh_ref, dhb_ref, dht_ref, vec_ref, *refs = refs
        wu, wd, dz, dn_ref, scratch, sems = refs
    else:
        dn_ref, wu, wd, dz, sems = refs
    step = pl.program_id(0)
    count = len(arrays_of(ups))
    n = len(ups)

    at_ref = late.buffers[0]

    def get(which, slot):
        fetch_step(downs, which, w_refs[count:], place_ref, wd.at[slot], sems.at[1, slot])
        fetch_step(ups, which, w_refs[:count], place_ref, wu.at[slot], sems.at[0, slot])

    @pl.when(step == 0)
    def _():
        get(0, 0)
        late.start()
        if first:
            dn_ref[...] = jnp.zeros_like(dn_ref)

    slot = lax.rem(step, 2)
    get(step + 1, 1 - slot)
    landed(wd.at[slot], sems.at[1, slot])
    width = dz.shape[1]
    for c in range(0, width, 256):
        cols = slice(c, min(c + 256, width))
        grad = (nn(eb_ref[...], wd[slot, :, cols]) * gp_ref[0, :, cols].astype(F32)).astype(BF)
        dz[:, cols] = grad
        sum_ref[0, :, cols] = jnp.sum(grad.astype(F32), axis=0, keepdims=True)
    landed(wu.at[slot], sems.at[0, slot])
    part = nt(dz[...], wu[slot])

    @pl.when(step == 0)
    def _():
        late.take(0)
        if not first:
            dn_ref[...] = late.take(1)[...]

    dn_ref[...] += part
    middle = at_ref.shape[0] // 2
    far_ref[0] = nn(at_ref[middle:, :], dz[...]).astype(BF)
    near_ref[0] = nn(at_ref[:middle, :], dz[...]).astype(BF)
    if not last:
        return

    @pl.when(step == n - 1)
    def _():
        h_ref = late.take(2)

        def rows_of(rows, carry):
            unit, inverse = norm_stats(h_ref[rows, :])
            grad = dn_ref[rows, :]
            scaled = grad * gain[...]
            dh = eb_ref[rows, :].astype(F32) + inverse * (
                scaled
                - jnp.mean(scaled, axis=-1, keepdims=True)
                - unit * jnp.mean(scaled * unit, axis=-1, keepdims=True)
            )
            dh_ref[rows, :] = dh
            dhb_ref[rows, :] = dh.astype(BF)
            return carry[0] + fold(grad * unit), carry[1] + fold(grad), carry[2] + fold(dh)

        m, dim = h_ref.shape
        zero = jnp.zeros((8, dim), F32)
        sums = over_rows(m, rows_of, (zero, zero, zero))
        for i, value in enumerate(sums):
            vec_ref[i : i + 1, :] = total_of(value)
        turn(cfg, place_ref[0], dhb_ref[...], dht_ref, scratch)


def ffn_two(cfg, place, after, ups, downs, ks, eb, at, gp, dn, closing=None):
    dim, m = at.shape
    n, width = len(ups), gp.shape[2]
    block = (dim // 2, width)
    at_k = lambda i: ks[0] + i if ks[0] < ks[-1] else ks[0] - i
    ins, in_specs, late = [eb, gp], [whole((m, dim)), stepped((m, width), at_k)], [at]
    if closing:
        ins.append(closing[1])
        in_specs.append(whole((1, dim)))
        late += [dn, closing[0]]
    outs = [((n,) + block, BF)] * 2 + [((n, 1, width), F32)]
    out_specs = [stepped(block)] * 2 + [stepped((1, width))]
    scratch = [
        pltpu.VMEM((2, dim, width), BF), pltpu.VMEM((2, dim, width), BF), pltpu.VMEM((m, width), BF)
    ]
    if closing:
        shapes = [((m, dim), F32), ((m, dim), BF), ((dim, m), BF), ((3, dim), F32)]
        scratch += [pltpu.VMEM((m, dim), F32), pltpu.VMEM((dim, m), BF)]
    else:
        shapes = [((m, dim), F32)]
    outs += shapes
    out_specs += [whole(shape) for shape, _ in shapes]
    return call(
        partial(ffn_two_kernel, cfg, ups, downs, dn is None, bool(closing)), "ffn_two",
        30 if closing else 24, place, arrays_of(ups) + arrays_of(downs), after, ins, outs,
        scratch + [pltpu.SemaphoreType.DMA((2, 2))], late=late, grid=(n,),
        specs=(in_specs, out_specs), mib=58,
    )


CORE, ACROSS, ALONG = 1, 2, 4
CUBE = 8
ORDER = (0, ACROSS, ALONG, ACROSS + ALONG, CORE, CORE + ACROSS, CORE + ALONG, CORE + ACROSS + ALONG)


def ring(value, by, size):
    return lax.ppermute(value, "tensor", [(i, (i + by) % size) for i in range(size)])


def swap(value, offset):
    return lax.ppermute(value, "dp", [(i, i ^ offset) for i in range(lax.axis_size("dp"))])


def tie(value, *others):
    return lax.optimization_barrier((value, *others))[0]


def ties(values, mark):
    return list(lax.optimization_barrier((*values, mark))[:-1])


def gather_all(own, split):
    dp, size = lax.axis_size("dp"), lax.axis_size("tensor")
    rows = own.shape[0]
    full = lax.all_gather(own, ("dp", "tensor"), axis=0, tiled=False)
    if split:

        def blocks(k, d, z):
            t = lax.rem(z - k + size, size)
            return [(0, i * size + t, i * rows, rows) for i in range(dp)]
    else:
        full = full.reshape(dp, size, rows, -1).transpose(1, 0, 2, 3)
        full = full.reshape(size, dp * rows, -1)

        def blocks(k, d, z):
            return [(0, lax.rem(z - k + size, size), 0, dp * rows)]

    return [Piece([full], partial(blocks, k)) for k in range(size)]


def gather_ring(own):
    size = lax.axis_size("tensor")
    held = [own]
    for _ in range(size - 1):
        held.append(ring(held[-1], 1, size))
    return held


def gather_near(held, group):
    mine = jnp.stack(held[2 * group : 2 * group + 2])
    return jnp.stack([mine, swap(mine, (ACROSS, ALONG)[group])])


def gather_far(both, group):
    return swap(both, (ALONG, ACROSS)[group])


def gather_pieces(nears, fars, firsts, rows):
    own = jnp.stack([jnp.stack(pair) for pair in zip(nears, fars)])
    arrays = [own, swap(own, CORE)]

    def blocks(n, d, z):
        first = firsts[n]
        second = ACROSS + ALONG - first
        return [
            (
                core,
                (n, i, j),
                pl.multiple_of(jnp.bitwise_xor(d, core * CORE + i * second + j * first) * rows, 16),
                rows,
            )
            for core in range(2)
            for i in range(2)
            for j in range(2)
        ]

    return [Piece(arrays, partial(blocks, n)) for n in range(len(nears))]


def gather_groups(both, both_core, far, far_core, rows):
    firsts = (ACROSS, ACROSS, ALONG, ALONG)

    def blocks(k, d, z):
        group, n = k // 2, k % 2
        first = firsts[k]
        second = ACROSS + ALONG - first
        out = []
        for other in range(2):
            for index, lead, offset in (
                (group, (other, n), 0),
                (2, (group, other, n), CORE),
                (3 + group, (other, n), second),
                (5, (group, other, n), CORE + second),
            ):
                at = pl.multiple_of(jnp.bitwise_xor(d, offset + other * first) * rows, 16)
                out.append((index, lead, at, rows))
        return out

    return [Piece([*both, both_core, *far, far_core], partial(blocks, k)) for k in range(4)]


def scatter_all(near, far):
    size, dp = lax.axis_size("tensor"), lax.axis_size("dp")
    z = lax.axis_index("tensor")
    pieces = jnp.stack([jnp.concatenate(halves) for halves in zip(near, far)])
    dim, width = pieces.shape[1:]
    order = jnp.stack([lax.rem(z - t + size, size) for t in range(size)])
    return scatter_placed(jnp.take(pieces, order, axis=0)[None])


def scatter_placed(value):
    size, dp = lax.axis_size("tensor"), lax.axis_size("dp")
    blocks, _, rows, width = value.shape
    if blocks != dp:
        value = value.transpose(1, 0, 2, 3).reshape(size, dp, -1, width).transpose(1, 0, 2, 3)
    value = value.reshape(dp * size, -1, width)
    return lax.psum_scatter(value, ("dp", "tensor"), scatter_dimension=0, tiled=True)[0]


def add(*terms):
    total = terms[0].astype(F32)
    for term in terms[1:]:
        total = total + term.astype(F32)
    return total


class Scatter:
    def __init__(self, halves, links):
        self.links = links
        self.near = [piece for near, _ in halves for piece in self.split(near)]
        self.far = [far for _, far in halves]

    def split(self, value):
        count, half, width = value.shape
        value = value.reshape(count, 2, 2, half // 4, width)
        return [value[i] for i in range(count)]

    def pick(self, value, link, i, j):
        return value[j, i] if link == ACROSS else value[i, j]

    def send(self, step, outs):
        got, sent = [None] * len(outs), []
        for link in (ACROSS, ALONG):
            mine = [i for i, first in enumerate(self.links) if (first == link) == (step == 1)]
            if not mine:
                continue
            value = swap(jnp.stack([v for i in mine for v in outs[i]]), link)
            sent.append(value)
            for n, i in enumerate(mine):
                count = len(outs[i])
                got[i] = [value[n * count + c] for c in range(count)]
        return got, sent

    def step_core(self):
        sent = [swap(far, CORE) for far in self.far]
        self.core = [piece for value in sent for piece in self.split(value)]
        return sent

    def step_first(self, mark=None):
        if mark is not None:
            self.core = ties(self.core, mark)
        outs = [
            [add(self.pick(a, link, 1, j), self.pick(b, link, 1, j)).astype(BF) for j in range(2)]
            for a, b, link in zip(self.near, self.core, self.links)
        ]
        self.one, sent = self.send(1, outs)
        return sent

    def step_second(self, mark=None):
        if mark is not None:
            flat = ties([v for one in self.one for v in one], mark)
            self.one = [flat[2 * i : 2 * i + 2] for i in range(len(self.one))]
        outs = [
            [add(self.pick(a, link, 0, 1), self.pick(b, link, 0, 1), one[1]).astype(BF)]
            for a, b, one, link in zip(self.near, self.core, self.one, self.links)
        ]
        self.two, sent = self.send(2, outs)
        return sent

    def terms(self, i):
        link = self.links[i]
        return [
            self.pick(self.near[i], link, 0, 0),
            self.pick(self.core[i], link, 0, 0),
            self.one[i][0],
            self.two[i][0],
        ]


class Around:
    def __init__(self, terms, size):
        self.terms, self.size, self.k, self.total = terms, size, size - 1, None

    def step(self, mark=None):
        terms = self.terms(self.k) + ([] if self.total is None else [self.total])
        if mark is not None:
            terms = terms[:-1] + [tie(terms[-1], mark)]
        total = add(*terms)
        self.k -= 1
        if self.k < 0:
            return total
        self.total = ring(total.astype(BF), -1, self.size)
        return [self.total]


def sum_all(vector, cube):
    if not cube:
        return lax.psum(vector, ("dp", "tensor"))
    size = lax.axis_size("tensor")
    for offset in (CORE, ACROSS, ALONG):
        vector = vector + swap(vector, offset)
    offset = 1
    while offset < size:
        vector = vector + lax.ppermute(vector, "tensor", [(i, i ^ offset) for i in range(size)])
        offset *= 2
    return vector


def on_device(
    tokens, image_flags, cotangent, gain_one, shift_one, w_query, b_query, w_key, w_value, b_value,
    w_out, b_out, gain_two, shift_two, w_up, b_up, w_down, b_down,
):
    dp, size = lax.axis_size("dp"), lax.axis_size("tensor")
    d, z = lax.axis_index("dp"), lax.axis_index("tensor")
    images = image_flags.shape[0]
    all_rows, dim = tokens.shape
    seq = all_rows // images
    assert images == size
    m = up(seq, 256)
    rows = dim // dp
    split = rows % 16 == 0
    span = w_query.shape[1]
    units = w_up.shape[1]
    hidden = up(units, LANES)
    width = 4 * span
    base, wide = span // LANES * LANES, up(span, LANES)
    qw = width - base
    cube = dp == CUBE and split and size == 4
    cfg = dict(m=m, seq=seq, heads=span // HD, base=base, wide=wide, width=width, qw=qw)
    cfg.update(rows=rows, order=ORDER if cube else None)

    own_attn = jnp.concatenate([w_out.T, w_query, w_key, w_value], axis=1).astype(BF)
    own_up = jnp.pad(w_up.astype(BF), ((0, 0), (0, hidden - units)))
    own_down = jnp.pad(w_down.T.astype(BF), ((0, 0), (0, hidden - units)))
    skip = jnp.zeros((span - base,), F32)
    own_bias = jnp.concatenate(
        [skip, b_query, jnp.zeros((span,), F32), b_value, b_up, jnp.zeros((hidden - units,), F32)]
    )[None]
    flag = lax.dynamic_index_in_dim(image_flags, z, 0, keepdims=False)
    place = jnp.stack([d, z, flag]).astype(jnp.int32)

    pad_rows = ((0, m - seq), (0, 0))
    x = jnp.pad(lax.dynamic_slice_in_dim(tokens, z * seq, seq, 0), pad_rows)
    eb = jnp.pad(lax.dynamic_slice_in_dim(cotangent, z * seq, seq, 0) * flag.astype(BF), pad_rows)
    a1, a1t, et, sum_e = norm_one(cfg, place, x, eb, gain_one[None], shift_one[None])

    every = list(range(size))
    pin = {}
    if cube:
        held = gather_ring(own_attn)
        firsts = [ACROSS if k % 2 == 0 else ALONG for k in every]
        nears, fars = [], []
        for k in every:
            nears.append(jnp.stack([held[k], swap(held[k], firsts[k])]))
            fars.append(swap(nears[k], ACROSS + ALONG - firsts[k]))
        attn_w = gather_pieces(nears[:2], fars[:2], firsts[:2], rows)
        attn_w += gather_pieces(nears[2:], fars[2:], firsts[2:], rows)
        bits = []
        for _ in range(3):
            top = lax.reduce_precision(own_bias[0], 8, 7)
            bits.append(top.astype(BF))
            own_bias = own_bias - top[None]
        bits = jnp.concatenate(bits)
        count = bits.shape[0]
        extra = up(-(-count // hidden), 16)
        bits = jnp.pad(bits, (0, extra * hidden - count)).reshape(extra, hidden)
        ffn_held = gather_ring(tie(jnp.concatenate([own_up, bits]), held[-1]))
        bias = []
        for v in ffn_held:
            v = v[rows:].reshape(-1)[:count].reshape(3, -1).astype(F32)
            bias.append((v[0] + v[1] + v[2])[None])
        ffn_held = ties(ffn_held, fars[3])
        up_held = [v[:rows] for v in ffn_held]
        both_up = [gather_near(up_held, i) for i in range(2)]
    else:
        bias = gather_ring(own_bias)
        attn_w, up_w = (gather_all(w, split) for w in (own_attn, own_up))
    kept = [
        attn_fwd(cfg, place, pin.get(f"attn{k}", []), attn_w[k], a1, bias[k][:, :qw]) for k in every
    ]
    if cube:
        far_up = [gather_far(both_up[i], i) for i in range(2)]
        core_up = swap(jnp.stack(both_up), CORE)
    h, a2, a2t = norm_two(
        cfg, place, pin.get("norm_two", []), attn_w, x, b_out[None], gain_two[None], shift_two[None],
        [o for _, o, _ in kept],
    )
    down_w = gather_all(own_down, split)
    if cube:
        far_up = ties(far_up, kept[3][2])
        up_w = gather_groups(both_up, core_up, far_up, swap(jnp.stack(far_up), CORE), rows)
    g, gp, g_down = ffn_one(
        cfg, place, pin.get("ffn_one", []), up_w, a2, jnp.stack(bias)[:, :, qw:], et
    )

    sum_down = scatter_placed(g_down)

    low, high = [1, 0], [3, 2]
    near3, far3, sum_high, dn2 = ffn_two(
        cfg, place, pin.get("two0", []), [up_w[k] for k in high], [down_w[k] for k in high], high, eb,
        a2t, gp, None,
    )
    mixed_links = [ACROSS, ALONG]
    if cube:
        up_high = Scatter([(near3, far3)], mixed_links)
        up_high_core = up_high.step_core()
    near1, far1, sum_low, dh, dhb, dht, vec_two = ffn_two(
        cfg, place, pin.get("two1", []), [up_w[k] for k in low], [down_w[k] for k in low], low, eb,
        a2t, gp, dn2, [h, gain_two[None]],
    )
    sum_dz = [sum_low[1], sum_low[0], sum_high[1], sum_high[0]]
    grads = [None] * size

    def backward(k, after):
        near, far, sums, dqkv = attn_bwd(cfg, place, after, attn_w[k], a1t, dhb, dht, *kept[k])
        grads[k] = (near, far, sums, dqkv)
        return Scatter([(near, far)], [ACROSS if k % 2 else ALONG])

    def finish(after):
        return mix(place, after, down_w, h, g, b_down[None])

    def finish_norm(after):
        return norm_back(
            cfg, place, after, attn_w, x, dh, gain_one[None], [grads[k][3] for k in every]
        )

    if cube:
        up_low = Scatter([(near1, far1)], mixed_links)
        up_z = Around(lambda k: (up_high if k > 1 else up_low).terms(1 - k % 2), size)
        attn_z = Around(lambda k: out[k].terms(0), size)
        out = {}
        pins = {k: [] for k in ("a3", "a2", "a1", "a0", "nb", "mix")}
        pins["a3"] += up_high_core
        pins["a2"] += up_low.step_core() + up_high.step_first(vec_two)
        out[3] = backward(3, pins["a3"])
        mark = grads[3][2]
        pins["a1"] += up_high.step_second(mark) + up_low.step_first(mark) + out[3].step_core()
        out[2] = backward(2, pins["a2"])
        mark = grads[2][2]
        pins["a0"] += up_low.step_second(mark) + out[3].step_first(mark) + out[2].step_core()
        out[1] = backward(1, pins["a1"])
        mark = grads[1][2]
        pins["nb"] += out[3].step_second(mark) + out[2].step_first(mark) + out[1].step_core()
        pins["nb"] += up_z.step(mark)
        out[0] = backward(0, pins["a0"])
        mark = grads[0][2]
        pins["nb"] += out[0].step_core()
        pins["mix"] += out[1].step_first(mark) + out[2].step_second(mark) + attn_z.step(mark)
        pins["mix"] += out[0].step_first() + up_z.step(mark)
        tokens_grad, vec_one = finish_norm(pins["nb"])
        out[1].step_second(vec_one)
        out[0].step_second(vec_one)
        attn_z.step(vec_one)
        up_z.step(vec_one)
        mixed = finish(pins["mix"])
        attn_z.step(mixed)
        grad_up, grad_attn = up_z.step(), attn_z.step()
    else:
        for k in high + low:
            backward(k, [])
        mixed = finish([])
        tokens_grad, vec_one = finish_norm([])
        rejoin = lambda a, b: [a[1], a[0], b[1], b[0]]
        grad_up = scatter_all(rejoin(near1, near3), rejoin(far1, far3))
        grad_attn = scatter_all([g[0][0] for g in grads], [g[1][0] for g in grads])
    sum_qkv = [g[2] for g in grads]
    grad_down = tie(sum_down, vec_one).astype(F32)[:, :units].T
    grad_up, grad_attn = grad_up.astype(F32), grad_attn.astype(F32)
    grad_up = grad_up[:, :units]
    pieces = jnp.concatenate([jnp.concatenate(sum_qkv), jnp.concatenate(sum_dz)], axis=1)
    order = jnp.stack([lax.rem(z - t + size, size) for t in range(size)])
    pieces = jnp.take(pieces, order, axis=0)
    sums = sum_all(
        jnp.concatenate([pieces.reshape(-1), vec_one.reshape(-1), vec_two.reshape(-1), sum_e[0]]),
        cube,
    )
    per = qw + hidden
    mine = lax.dynamic_index_in_dim(sums[: size * per].reshape(size, per), z, 0, keepdims=False)
    rest = sums[size * per :].reshape(6, dim)
    at = span - base
    return (
        mixed[:seq],
        tokens_grad[:seq],
        rest[0],
        rest[1],
        grad_attn[:, span : 2 * span],
        mine[at : at + span],
        grad_attn[:, 2 * span : 3 * span],
        grad_attn[:, 3 * span :],
        mine[at + 2 * span : at + 3 * span],
        grad_attn[:, :span].T,
        rest[4],
        rest[2],
        rest[3],
        grad_up,
        mine[qw : qw + units],
        grad_down,
        rest[5],
    )


SPECS_IN = (
    P("dp", None), P("dp"), P("dp", None), P(), P(), P("dp", "tensor"), P("tensor"),
    P("dp", "tensor"), P("dp", "tensor"), P("tensor"), P("tensor", "dp"), P(), P(), P(),
    P("dp", "tensor"), P("tensor"), P("tensor", "dp"), P(),
)
SPECS_OUT = (
    P(("dp", "tensor"), None), P(("dp", "tensor"), None), P(), P(), P("dp", "tensor"), P("tensor"),
    P("dp", "tensor"), P("dp", "tensor"), P("tensor"), P("tensor", "dp"), P(), P(), P(),
    P("dp", "tensor"), P("tensor"), P("tensor", "dp"), P(),
)


def solution(mesh):
    return jax.shard_map(
        on_device, mesh=mesh, in_specs=SPECS_IN, out_specs=SPECS_OUT, check_vma=False
    )
```

```python
from functools import partial

import jax
import jax.numpy as jnp
from jax import lax
from jax.experimental import pallas as pl
from jax.experimental.pallas import tpu as pltpu
from jax.sharding import PartitionSpec as P

HD = 72
LANES = 128
EPSILON = 1e-06
SCALE = HD**-0.5
SHARP = SCALE * 1.4426950408889634
GELU_A = 0.7978845608028654
GELU_B = 0.044715
BF = jnp.bfloat16
F32 = jnp.float32
ANY = pl.BlockSpec(memory_space=pl.ANY)
SMEM = pl.BlockSpec(memory_space=pltpu.SMEM)
VMEM = pl.BlockSpec(memory_space=pltpu.VMEM)


def up(value, step):
    return -(-value // step) * step


def nn(left, right):
    return lax.dot_general(left, right, (((1,), (0,)), ((), ())), preferred_element_type=F32)


def nt(left, right):
    return lax.dot_general(left, right, (((1,), (1,)), ((), ())), preferred_element_type=F32)


def whole(shape):
    return pl.BlockSpec(shape, lambda *_: (0,) * len(shape), pipeline_mode=pl.Buffered(1))


def stepped(shape, index=lambda i: i):
    return pl.BlockSpec((1,) + shape, lambda i, *_: (index(i),) + (0,) * len(shape))


def call(
    kernel, name, us, place, weights, after, ins, outs, scratch, late=(), grid=None, specs=None, mib=40,
    prefetch=False,
):
    weights, after, late = list(weights), list(after), list(late)
    lead = 1 + len(weights) + len(after) + len(late)
    scratch = list(scratch)
    if late:
        scratch += [pltpu.VMEM(v.shape, v.dtype) for v in late] + [pltpu.SemaphoreType.DMA((len(late),))]

    def body(*refs):
        if not late:
            return kernel(refs[0], refs[1 : 1 + len(weights)], *refs[lead:])
        n = len(late)
        *rest, sems = refs[lead:]
        inputs = Late(refs[lead - n : lead], rest[-n:], sems)
        return kernel(refs[0], refs[1 : 1 + len(weights)], *rest[:-n], inputs)

    in_specs, out_specs = specs or ([VMEM] * len(ins), [VMEM] * len(outs))
    return pl.pallas_call(
        body,
        grid_spec=pltpu.PrefetchScalarGridSpec(
            num_scalar_prefetch=1 if prefetch else 0,
            grid=grid or (),
            in_specs=([] if prefetch else [SMEM]) + [ANY] * (lead - 1) + list(in_specs),
            out_specs=list(out_specs),
            scratch_shapes=scratch,
        ),
        out_shape=[jax.ShapeDtypeStruct(*out) for out in outs],
        compiler_params=pltpu.CompilerParams(vmem_limit_bytes=mib * 2**20),
        cost_estimate=pl.CostEstimate(
            flops=int(us * 1.15e9), bytes_accessed=int(us * 1e5), transcendentals=0
        ),
        name=name,
    )(place, *weights, *after, *late, *ins)


class Late:
    def __init__(self, sources, buffers, sems):
        self.buffers = buffers
        self.copies = [
            pltpu.make_async_copy(source, buffer, sems.at[i])
            for i, (source, buffer) in enumerate(zip(sources, buffers))
        ]

    def start(self):
        for copy in self.copies:
            copy.start()

    def take(self, i):
        self.copies[i].wait()
        return self.buffers[i]


class Piece:
    def __init__(self, arrays, blocks):
        self.arrays, self.blocks = arrays, blocks

    def fetch(self, refs, place_ref, buffer, sem, columns=None):
        for array, lead, first, rows in self.blocks(place_ref[0], place_ref[1]):
            source = refs[array].at[lead]
            if columns is not None:
                source = source.at[:, :columns]
            pltpu.make_async_copy(source, buffer.at[pl.ds(first, rows), :], sem).start()


def fetch_step(pieces, which, refs, place_ref, buffer, sem):
    begin = 0
    for index, piece in enumerate(pieces):
        mine = refs[begin : begin + len(piece.arrays)]
        begin += len(piece.arrays)

        @pl.when(which == index)
        def _():
            piece.fetch(mine, place_ref, buffer, sem)


def arrays_of(pieces):
    return [array for piece in pieces for array in piece.arrays]


def landed(buffer, sem):
    pltpu.make_async_copy(buffer, buffer, sem).wait()


def turn(cfg, d, value, out_ref, scratch):
    rows, order = cfg["rows"], cfg["order"]
    if order is None:
        out_ref[...] = value.T
        return
    scratch[...] = value.T
    for place, offset in enumerate(order):
        first = pl.multiple_of(jnp.bitwise_xor(d, offset) * rows, 16)
        out_ref[place * rows : (place + 1) * rows, :] = scratch[pl.ds(first, rows), :]


STEP = 32


def over_rows(total, body, carry):
    def step(t, carry):
        return body(pl.ds(pl.multiple_of(t * STEP, STEP), STEP), carry)

    return lax.fori_loop(0, total // STEP, step, carry, unroll=4)


def norm_stats(rows):
    average = jnp.mean(rows, axis=-1, keepdims=True)
    centred = rows - average
    inverse = lax.rsqrt(jnp.mean(centred * centred, axis=-1, keepdims=True) + EPSILON)
    return centred * inverse, inverse


def fold(value):
    return jnp.sum(value.reshape(STEP // 8, 8, value.shape[1]), axis=0)


def total_of(partial_sums):
    return jnp.sum(partial_sums, axis=0, keepdims=True)


def norm_one_kernel(
    cfg, place_ref, _, x_ref, eb_ref, gain_ref, shift_ref, a_ref, at_ref, et_ref, sum_ref, scratch
):
    def rows_of(rows, carry):
        unit, _ = norm_stats(x_ref[rows, :].astype(F32))
        a_ref[rows, :] = (unit * gain_ref[...] + shift_ref[...]).astype(BF)
        return carry + fold(eb_ref[rows, :].astype(F32))

    m, dim = x_ref.shape
    sum_ref[...] = total_of(over_rows(m, rows_of, jnp.zeros((8, dim), F32)))
    turn(cfg, place_ref[0], a_ref[...], at_ref, scratch)
    et_ref[...] = eb_ref[...].T


def norm_one(cfg, place, x, eb, gain, shift):
    m, d = x.shape
    outs = [((m, d), BF), ((d, m), BF), ((d, m), BF), ((1, d), F32)]
    return call(
        partial(norm_one_kernel, cfg), "norm_one", 6, place, [], [], [x, eb, gain, shift], outs,
        [pltpu.VMEM((d, m), BF)],
    )


def norm_two_kernel(cfg, pieces, place_ref, w_refs, b_out, gain, shift, *refs):
    n = len(pieces)
    h_ref, a_ref, at_ref, w, scratch, sems, late = refs
    late.start()
    begin = 0
    for i, piece in enumerate(pieces):
        mine = w_refs[begin : begin + len(piece.arrays)]
        begin += len(piece.arrays)
        piece.fetch(mine, place_ref, w.at[i], sems.at[i], cfg["wide"])
    for i in range(n):
        landed(w.at[i], sems.at[i])
        part = nt(late.take(i)[...], w[i])
        h_ref[...] = part if i == 0 else h_ref[...] + part
    x_ref = late.take(n)

    def rows_of(rows, carry):
        h = x_ref[rows, :].astype(F32) + h_ref[rows, :] + b_out[...]
        h_ref[rows, :] = h
        unit, _ = norm_stats(h)
        a_ref[rows, :] = (unit * gain[...] + shift[...]).astype(BF)
        return carry

    over_rows(x_ref.shape[0], rows_of, 0)
    turn(cfg, place_ref[0], a_ref[...], at_ref, scratch)


def norm_two(cfg, place, after, pieces, x, b_out, gain, shift, o):
    m, d = x.shape
    n = len(pieces)
    outs = [((m, d), F32), ((m, d), BF), ((d, m), BF)]
    return call(
        partial(norm_two_kernel, cfg, pieces), "norm_two", 12, place, arrays_of(pieces), after,
        [b_out, gain, shift], outs,
        [
            pltpu.VMEM((n, d, cfg["wide"]), BF),
            pltpu.VMEM((d, m), BF),
            pltpu.SemaphoreType.DMA((n,)),
        ],
        late=[*o, x],
    )


def mixed_kernel(pieces, place_ref, w_refs, h_ref, g_ref, b_down, out_ref, acc, w, sems):
    step = pl.program_id(0)
    flag = place_ref[2].astype(F32)

    @pl.when(step == 0)
    def _():
        fetch_step(pieces, 0, w_refs, place_ref, w.at[0], sems.at[0])
        acc[...] = h_ref[...] + b_down[...]

    slot = lax.rem(step, 2)
    fetch_step(pieces, step + 1, w_refs, place_ref, w.at[1 - slot], sems.at[1 - slot])
    landed(w.at[slot], sems.at[slot])
    acc[...] += nt(g_ref[0], w[slot])

    @pl.when(step == len(pieces) - 1)
    def _():
        out_ref[...] = (acc[...] * flag).astype(BF)


def mix(place, after, pieces, h, g, b_down):
    m, d = h.shape
    width = g.shape[2]
    return call(
        partial(mixed_kernel, pieces), "mixed", 14, place, arrays_of(pieces), after, [h, g, b_down],
        [((m, d), BF)],
        [pltpu.VMEM((m, d), F32), pltpu.VMEM((2, d, width), BF), pltpu.SemaphoreType.DMA((2,))],
        grid=(len(pieces),),
        specs=([whole((m, d)), stepped((m, width)), whole((1, d))], [whole((m, d))]),
    )[0]


def norm_back_kernel(cfg, pieces, place_ref, w_refs, gain, *refs):
    n = len(pieces)
    out_ref, vec_ref, dn, w, sems, late = refs
    late.start()
    parts, begin = [], 0
    for piece in pieces:
        parts.append(w_refs[begin : begin + len(piece.arrays)])
        begin += len(piece.arrays)
    pieces[0].fetch(parts[0], place_ref, w.at[0], sems.at[0])
    for i in range(n):
        if i + 1 < n:
            pieces[i + 1].fetch(parts[i + 1], place_ref, w.at[(i + 1) % 2], sems.at[(i + 1) % 2])
        landed(w.at[i % 2], sems.at[i % 2])
        part = nt(late.take(i)[...], w[i % 2, :, cfg["base"] :])
        dn[...] = part if i == 0 else dn[...] + part
    x_ref, dh_ref = late.take(n), late.take(n + 1)

    def rows_of(rows, carry):
        unit, inverse = norm_stats(x_ref[rows, :].astype(F32))
        grad = dn[rows, :]
        scaled = grad * gain[...]
        out = dh_ref[rows, :] + inverse * (
            scaled
            - jnp.mean(scaled, axis=-1, keepdims=True)
            - unit * jnp.mean(scaled * unit, axis=-1, keepdims=True)
        )
        out_ref[rows, :] = out.astype(BF)
        return carry[0] + fold(grad * unit), carry[1] + fold(grad)

    m, dim = x_ref.shape
    zero = jnp.zeros((8, dim), F32)
    for i, value in enumerate(over_rows(m, rows_of, (zero, zero))):
        vec_ref[i : i + 1, :] = total_of(value)


def norm_back(cfg, place, after, pieces, x, dh, gain, grads):
    m, d = x.shape
    outs = [((m, d), BF), ((2, d), F32)]
    return call(
        partial(norm_back_kernel, cfg, pieces), "norm_back", 18, place, arrays_of(pieces), after,
        [gain], outs,
        [
            pltpu.VMEM((m, d), F32),
            pltpu.VMEM((2, d, cfg["width"]), BF),
            pltpu.SemaphoreType.DMA((2,)),
        ],
        late=[*grads, x, dh],
    )


def pad_heads(cfg, refs):
    m, seq = cfg["m"], cfg["seq"]
    lane = lax.broadcasted_iota(jnp.int32, (m, LANES - HD), 1)
    row = lax.broadcasted_iota(jnp.int32, (m, LANES - HD), 0)
    one = jnp.where(lane == 0, 1.0, 0.0).astype(BF)
    past = jnp.where((lane == 0) & (row >= seq), -1e30, 0.0).astype(BF)
    for h in range(cfg["heads"]):
        for ref, fill in zip(refs, (one, past, one)):
            ref[h, :, HD:] = fill


def attn_fwd_kernel(cfg, piece, place_ref, w_refs, a_ref, bias_ref, *refs):
    qkv_ref, o_ref, lse_ref, w, q_s, k_s, v_s, vt, ot, sem = refs
    m, heads, base, wide = cfg["m"], cfg["heads"], cfg["base"], cfg["wide"]
    piece.fetch(w_refs, place_ref, w, sem)
    pad_heads(cfg, (q_s, k_s, v_s))
    ot[...] = jnp.zeros_like(ot)
    lse_ref[...] = jnp.zeros_like(lse_ref)
    landed(w, sem)
    qkv_ref[...] = (nn(a_ref[...], w[:, base:]) + bias_ref[...]).astype(BF)
    span = heads * HD
    skip = span - base
    for h in range(heads):
        for n, s in enumerate((q_s, k_s, v_s)):
            at = skip + n * span + h * HD
            s[h, :, :HD] = qkv_ref[:, at : at + HD]
        vt[h] = v_s[h].T
        s = nt(k_s[h], q_s[h])
        highest = jnp.max(s, axis=0, keepdims=True) * SHARP
        p = jnp.exp2(s * SHARP - highest).astype(BF)
        mixed = nn(vt[h], p)
        total = mixed[HD : HD + 1, :]
        ot[h * HD : (h + 1) * HD, :] = mixed[:HD, :] * (1.0 / total)
        lse_ref[h : h + 1, :] = highest + jnp.log2(total)
    o_ref[...] = ot[...].T.astype(BF)


def attn_fwd(cfg, place, after, piece, a, bias):
    m, dim = a.shape
    qw, wide, heads, width = cfg["qw"], cfg["wide"], cfg["heads"], cfg["width"]
    outs = [((m, qw), BF), ((m, wide), BF), ((8, m), F32)]
    scratch = (
        [pltpu.VMEM((dim, width), BF)]
        + [pltpu.VMEM((heads, m, LANES), BF)] * 3
        + [
            pltpu.VMEM((heads, LANES, m), BF),
            pltpu.VMEM((wide, m), F32),
            pltpu.SemaphoreType.DMA,
        ]
    )
    return call(
        partial(attn_fwd_kernel, cfg, piece), "attn_fwd", 8, place, piece.arrays, after, [a, bias],
        outs, scratch, mib=28,
    )


def attn_bwd_kernel(cfg, piece, place_ref, w_refs, *refs):
    dh_ref, qkv_ref, lse_ref, ga_ref, gb_ref, sum_ref, dqkv, *refs = refs
    w, q_s, k_s, v_s, do_s, kt, do_all, dqt, p_s, ds_s, sem, late = refs
    m, heads, base, wide = cfg["m"], cfg["heads"], cfg["base"], cfg["wide"]
    tile = m // 2
    piece.fetch(w_refs, place_ref, w, sem, wide)
    late.start()
    span = heads * HD
    skip = span - base
    pad_heads(cfg, (q_s, k_s))
    dqt[...] = jnp.zeros_like(dqt)
    dqkv[:, :LANES] = jnp.zeros((m, LANES), BF)
    for h in range(heads):
        v_s[h, :, HD:] = jnp.zeros((m, LANES - HD), BF)
        do_s[h, :, HD:] = jnp.zeros((m, LANES - HD), BF)
        for n, s in enumerate((q_s, k_s, v_s)):
            at = skip + n * span + h * HD
            s[h, :, :HD] = qkv_ref[:, at : at + HD]
        kt[h] = k_s[h].T
    landed(w, sem)
    do_all[...] = nn(dh_ref[...], w[...]).astype(BF)
    for h in range(heads):
        do_s[h, :, :HD] = do_all[:, h * HD : (h + 1) * HD]
        for t in range(m // tile):
            cols = slice(t * tile, (t + 1) * tile)
            p = jnp.exp2(nt(k_s[h], q_s[h, cols, :]) * SHARP - lse_ref[h : h + 1, cols])
            dp = nt(v_s[h], do_s[h, cols, :])
            ds = (p * (dp - jnp.sum(dp * p, axis=0, keepdims=True))).astype(BF)
            p_s[h % 2, :, cols] = p.astype(BF)
            ds_s[h % 2, :, cols] = ds
            dqt[h * HD : (h + 1) * HD, cols] = nn(kt[h], ds)[:HD] * SCALE
        dk = (nn(ds_s[h % 2], q_s[h]) * SCALE).astype(BF)
        dv = nn(p_s[h % 2], do_s[h]).astype(BF)
        at = skip + span + h * HD
        dqkv[:, at : at + HD] = dk[:, :HD]
        at = skip + 2 * span + h * HD
        dqkv[:, at : at + HD] = dv[:, :HD]
    dqkv[:, skip : skip + span] = dqt[...].T.astype(BF)[:, :span]
    grads = dqkv[...]
    sum_ref[...] = jnp.sum(grads.astype(F32), axis=0, keepdims=True)
    at_ref, dht_ref, o_ref = (late.take(i) for i in range(3))
    half = at_ref.shape[0] // 2
    for n, g_ref in ((1, gb_ref), (0, ga_ref)):
        rows = slice(n * half, (n + 1) * half)
        left = nn(dht_ref[rows, :], o_ref[...])
        right = nn(at_ref[rows, :], grads)
        g_ref[0, :, :base] = left[:, :base].astype(BF)
        g_ref[0, :, base:wide] = (left[:, base:] + right[:, : wide - base]).astype(BF)
        g_ref[0, :, wide:] = right[:, wide - base :].astype(BF)


def attn_bwd(cfg, place, after, piece, at, dh, dht, qkv, o, lse):
    dim, m = at.shape
    qw, wide, heads, width = cfg["qw"], cfg["wide"], cfg["heads"], cfg["width"]
    outs = [((1, dim // 2, width), BF)] * 2 + [((1, qw), F32), ((m, qw), BF)]
    scratch = (
        [pltpu.VMEM((dim, wide), BF)]
        + [pltpu.VMEM((heads, m, LANES), BF)] * 4
        + [
            pltpu.VMEM((heads, LANES, m), BF),
            pltpu.VMEM((m, wide), BF),
            pltpu.VMEM((wide, m), F32),
            pltpu.VMEM((2, m, m), BF),
            pltpu.VMEM((2, m, m), BF),
            pltpu.SemaphoreType.DMA,
        ]
    )
    return call(
        partial(attn_bwd_kernel, cfg, piece), "attn_bwd", 17, place, piece.arrays, after,
        [dh, qkv, lse], outs, scratch, late=[at, dht, o], mib=36,
    )


def ffn_one_kernel(cfg, pieces, place_ref, w_refs, a_ref, bias_ref, *refs):
    g_ref, gp_ref, grad_ref, w, sems, late = refs
    step = pl.program_id(0)

    @pl.when(step == 0)
    def _():
        late.start()
        fetch_step(pieces, 0, w_refs, place_ref, w.at[0], sems.at[0])

    slot = lax.rem(step, 2)
    fetch_step(pieces, step + 1, w_refs, place_ref, w.at[1 - slot], sems.at[1 - slot])
    landed(w.at[slot], sems.at[slot])
    width = g_ref.shape[2]
    for n in range(0, width, 256):
        cols = slice(n, min(n + 256, width))
        pre = nn(a_ref[...], w[slot, :, cols]) + bias_ref[0, :, cols]
        square = pre * pre
        half = 0.5 + 0.5 * jnp.tanh(pre * (GELU_A + GELU_A * GELU_B * square))
        g_ref[0, :, cols] = (pre * half).astype(BF)
        slope = half + (half - half * half) * (pre * (2 * GELU_A + 6 * GELU_A * GELU_B * square))
        gp_ref[0, :, cols] = slope.astype(BF)

    @pl.when(step == 0)
    def _():
        late.take(0)

    et_ref = late.buffers[0]
    count, _, rows, _ = grad_ref.shape
    for part in range(2):
        half = et_ref.shape[0] // 2
        value = nn(et_ref[part * half : (part + 1) * half, :], g_ref[0]).astype(BF)
        for i in range(count // 2):
            grad_ref[part * count // 2 + i, 0] = value[i * rows : (i + 1) * rows]


def ffn_one(cfg, place, after, pieces, a, bias, et):
    dim, m = et.shape
    n, width = len(pieces), bias.shape[2]
    rows = cfg["rows"] if cfg["rows"] % 16 == 0 else dim // 2
    outs = [((n, m, width), BF)] * 2 + [((dim // rows, n, rows, width), BF)]
    return call(
        partial(ffn_one_kernel, cfg, pieces), "ffn_one", 30, place, arrays_of(pieces), after,
        [a, bias], outs,
        [pltpu.VMEM((2, dim, width), BF), pltpu.SemaphoreType.DMA((2,))],
        late=[et], grid=(n,),
        specs=(
            [whole((m, dim)), stepped((1, width))],
            [stepped((m, width))] * 2
            + [
                pl.BlockSpec(
                    (dim // rows, 1, rows, width),
                    lambda i, place_ref: (0, lax.rem(place_ref[1] - i + n, n), 0, 0),
                )
            ],
        ),
        mib=56, prefetch=True,
    )


def ffn_two_kernel(cfg, ups, downs, first, last, place_ref, w_refs, eb_ref, gp_ref, *refs):
    *refs, late = refs
    if last:
        gain, *refs = refs
    near_ref, far_ref, sum_ref, *refs = refs
    if last:
        dh_ref, dhb_ref, dht_ref, vec_ref, *refs = refs
        wu, wd, dz, dn_ref, scratch, sems = refs
    else:
        dn_ref, wu, wd, dz, sems = refs
    step = pl.program_id(0)
    count = len(arrays_of(ups))
    n = len(ups)

    at_ref = late.buffers[0]

    def get(which, slot):
        fetch_step(downs, which, w_refs[count:], place_ref, wd.at[slot], sems.at[1, slot])
        fetch_step(ups, which, w_refs[:count], place_ref, wu.at[slot], sems.at[0, slot])

    @pl.when(step == 0)
    def _():
        get(0, 0)
        late.start()
        if first:
            dn_ref[...] = jnp.zeros_like(dn_ref)

    slot = lax.rem(step, 2)
    get(step + 1, 1 - slot)
    landed(wd.at[slot], sems.at[1, slot])
    width = dz.shape[1]
    for c in range(0, width, 256):
        cols = slice(c, min(c + 256, width))
        grad = (nn(eb_ref[...], wd[slot, :, cols]) * gp_ref[0, :, cols].astype(F32)).astype(BF)
        dz[:, cols] = grad
        sum_ref[0, :, cols] = jnp.sum(grad.astype(F32), axis=0, keepdims=True)
    landed(wu.at[slot], sems.at[0, slot])
    part = nt(dz[...], wu[slot])

    @pl.when(step == 0)
    def _():
        late.take(0)
        if not first:
            dn_ref[...] = late.take(1)[...]

    dn_ref[...] += part
    middle = at_ref.shape[0] // 2
    far_ref[0] = nn(at_ref[middle:, :], dz[...]).astype(BF)
    near_ref[0] = nn(at_ref[:middle, :], dz[...]).astype(BF)
    if not last:
        return

    @pl.when(step == n - 1)
    def _():
        h_ref = late.take(2)

        def rows_of(rows, carry):
            unit, inverse = norm_stats(h_ref[rows, :])
            grad = dn_ref[rows, :]
            scaled = grad * gain[...]
            dh = eb_ref[rows, :].astype(F32) + inverse * (
                scaled
                - jnp.mean(scaled, axis=-1, keepdims=True)
                - unit * jnp.mean(scaled * unit, axis=-1, keepdims=True)
            )
            dh_ref[rows, :] = dh
            dhb_ref[rows, :] = dh.astype(BF)
            return carry[0] + fold(grad * unit), carry[1] + fold(grad), carry[2] + fold(dh)

        m, dim = h_ref.shape
        zero = jnp.zeros((8, dim), F32)
        sums = over_rows(m, rows_of, (zero, zero, zero))
        for i, value in enumerate(sums):
            vec_ref[i : i + 1, :] = total_of(value)
        turn(cfg, place_ref[0], dhb_ref[...], dht_ref, scratch)


def ffn_two(cfg, place, after, ups, downs, ks, eb, at, gp, dn, closing=None):
    dim, m = at.shape
    n, width = len(ups), gp.shape[2]
    block = (dim // 2, width)
    at_k = lambda i: ks[0] + i if ks[0] < ks[-1] else ks[0] - i
    ins, in_specs, late = [eb, gp], [whole((m, dim)), stepped((m, width), at_k)], [at]
    if closing:
        ins.append(closing[1])
        in_specs.append(whole((1, dim)))
        late += [dn, closing[0]]
    outs = [((n,) + block, BF)] * 2 + [((n, 1, width), F32)]
    out_specs = [stepped(block)] * 2 + [stepped((1, width))]
    scratch = [
        pltpu.VMEM((2, dim, width), BF), pltpu.VMEM((2, dim, width), BF), pltpu.VMEM((m, width), BF)
    ]
    if closing:
        shapes = [((m, dim), F32), ((m, dim), BF), ((dim, m), BF), ((3, dim), F32)]
        scratch += [pltpu.VMEM((m, dim), F32), pltpu.VMEM((dim, m), BF)]
    else:
        shapes = [((m, dim), F32)]
    outs += shapes
    out_specs += [whole(shape) for shape, _ in shapes]
    return call(
        partial(ffn_two_kernel, cfg, ups, downs, dn is None, bool(closing)), "ffn_two",
        30 if closing else 24, place, arrays_of(ups) + arrays_of(downs), after, ins, outs,
        scratch + [pltpu.SemaphoreType.DMA((2, 2))], late=late, grid=(n,),
        specs=(in_specs, out_specs), mib=58,
    )


CORE, ACROSS, ALONG = 1, 2, 4
CUBE = 8
ORDER = (0, ACROSS, ALONG, ACROSS + ALONG, CORE, CORE + ACROSS, CORE + ALONG, CORE + ACROSS + ALONG)


def ring(value, by, size):
    return lax.ppermute(value, "tensor", [(i, (i + by) % size) for i in range(size)])


def swap(value, offset):
    return lax.ppermute(value, "dp", [(i, i ^ offset) for i in range(lax.axis_size("dp"))])


def tie(value, *others):
    return lax.optimization_barrier((value, *others))[0]


def ties(values, mark):
    return list(lax.optimization_barrier((*values, mark))[:-1])


def gather_all(own, split):
    dp, size = lax.axis_size("dp"), lax.axis_size("tensor")
    rows = own.shape[0]
    full = lax.all_gather(own, ("dp", "tensor"), axis=0, tiled=False)
    if split:

        def blocks(k, d, z):
            t = lax.rem(z - k + size, size)
            return [(0, i * size + t, i * rows, rows) for i in range(dp)]
    else:
        full = full.reshape(dp, size, rows, -1).transpose(1, 0, 2, 3)
        full = full.reshape(size, dp * rows, -1)

        def blocks(k, d, z):
            return [(0, lax.rem(z - k + size, size), 0, dp * rows)]

    return [Piece([full], partial(blocks, k)) for k in range(size)]


def gather_ring(own):
    size = lax.axis_size("tensor")
    held = [own]
    for _ in range(size - 1):
        held.append(ring(held[-1], 1, size))
    return held


def gather_near(held, group):
    mine = jnp.stack(held[2 * group : 2 * group + 2])
    return jnp.stack([mine, swap(mine, (ACROSS, ALONG)[group])])


def gather_far(both, group):
    return swap(both, (ALONG, ACROSS)[group])


def gather_groups(both, both_core, far, far_core, rows):
    firsts = (ACROSS, ACROSS, ALONG, ALONG)

    def blocks(k, d, z):
        group, n = k // 2, k % 2
        first = firsts[k]
        second = ACROSS + ALONG - first
        out = []
        for other in range(2):
            for index, lead, offset in (
                (group, (other, n), 0),
                (2, (group, other, n), CORE),
                (3 + group, (other, n), second),
                (5, (group, other, n), CORE + second),
            ):
                at = pl.multiple_of(jnp.bitwise_xor(d, offset + other * first) * rows, 16)
                out.append((index, lead, at, rows))
        return out

    return [Piece([*both, both_core, *far, far_core], partial(blocks, k)) for k in range(4)]


def scatter_all(near, far):
    size, dp = lax.axis_size("tensor"), lax.axis_size("dp")
    z = lax.axis_index("tensor")
    pieces = jnp.stack([jnp.concatenate(halves) for halves in zip(near, far)])
    dim, width = pieces.shape[1:]
    order = jnp.stack([lax.rem(z - t + size, size) for t in range(size)])
    return scatter_placed(jnp.take(pieces, order, axis=0)[None])


def scatter_placed(value):
    size, dp = lax.axis_size("tensor"), lax.axis_size("dp")
    blocks, _, rows, width = value.shape
    if blocks != dp:
        value = value.transpose(1, 0, 2, 3).reshape(size, dp, -1, width).transpose(1, 0, 2, 3)
    value = value.reshape(dp * size, -1, width)
    return lax.psum_scatter(value, ("dp", "tensor"), scatter_dimension=0, tiled=True)[0]


def add(*terms):
    total = terms[0].astype(F32)
    for term in terms[1:]:
        total = total + term.astype(F32)
    return total


class Scatter:
    def __init__(self, halves, links):
        self.links = links
        self.near = [piece for near, _ in halves for piece in self.split(near)]
        self.far = [far for _, far in halves]

    def split(self, value):
        count, half, width = value.shape
        value = value.reshape(count, 2, 2, half // 4, width)
        return [value[i] for i in range(count)]

    def pick(self, value, link, i, j):
        return value[j, i] if link == ACROSS else value[i, j]

    def send(self, step, outs):
        got, sent = [None] * len(outs), []
        for link in (ACROSS, ALONG):
            mine = [i for i, first in enumerate(self.links) if (first == link) == (step == 1)]
            if not mine:
                continue
            value = swap(jnp.stack([v for i in mine for v in outs[i]]), link)
            sent.append(value)
            for n, i in enumerate(mine):
                count = len(outs[i])
                got[i] = [value[n * count + c] for c in range(count)]
        return got, sent

    def step_core(self):
        sent = [swap(far, CORE) for far in self.far]
        self.core = [piece for value in sent for piece in self.split(value)]
        return sent

    def step_first(self, mark=None):
        if mark is not None:
            self.core = ties(self.core, mark)
        outs = [
            [add(self.pick(a, link, 1, j), self.pick(b, link, 1, j)).astype(BF) for j in range(2)]
            for a, b, link in zip(self.near, self.core, self.links)
        ]
        self.one, sent = self.send(1, outs)
        return sent

    def step_second(self, mark=None):
        if mark is not None:
            flat = ties([v for one in self.one for v in one], mark)
            self.one = [flat[2 * i : 2 * i + 2] for i in range(len(self.one))]
        outs = [
            [add(self.pick(a, link, 0, 1), self.pick(b, link, 0, 1), one[1]).astype(BF)]
            for a, b, one, link in zip(self.near, self.core, self.one, self.links)
        ]
        self.two, sent = self.send(2, outs)
        return sent

    def terms(self, i):
        link = self.links[i]
        return [
            self.pick(self.near[i], link, 0, 0),
            self.pick(self.core[i], link, 0, 0),
            self.one[i][0],
            self.two[i][0],
        ]


class Around:
    def __init__(self, terms, size):
        self.terms, self.size, self.k, self.total = terms, size, size - 1, None

    def step(self, mark=None):
        terms = self.terms(self.k) + ([] if self.total is None else [self.total])
        if mark is not None:
            terms = terms[:-1] + [tie(terms[-1], mark)]
        total = add(*terms)
        self.k -= 1
        if self.k < 0:
            return total
        self.total = ring(total.astype(BF), -1, self.size)
        return [self.total]


def sum_all(vector, cube):
    if not cube:
        return lax.psum(vector, ("dp", "tensor"))
    size = lax.axis_size("tensor")
    for offset in (CORE, ACROSS, ALONG):
        vector = vector + swap(vector, offset)
    offset = 1
    while offset < size:
        vector = vector + lax.ppermute(vector, "tensor", [(i, i ^ offset) for i in range(size)])
        offset *= 2
    return vector


def on_device(
    tokens, image_flags, cotangent, gain_one, shift_one, w_query, b_query, w_key, w_value, b_value,
    w_out, b_out, gain_two, shift_two, w_up, b_up, w_down, b_down,
):
    dp, size = lax.axis_size("dp"), lax.axis_size("tensor")
    d, z = lax.axis_index("dp"), lax.axis_index("tensor")
    images = image_flags.shape[0]
    all_rows, dim = tokens.shape
    seq = all_rows // images
    assert images == size
    m = up(seq, 256)
    rows = dim // dp
    split = rows % 16 == 0
    span = w_query.shape[1]
    units = w_up.shape[1]
    hidden = up(units, LANES)
    width = 4 * span
    base, wide = span // LANES * LANES, up(span, LANES)
    qw = width - base
    cube = dp == CUBE and split and size == 4
    cfg = dict(m=m, seq=seq, heads=span // HD, base=base, wide=wide, width=width, qw=qw)
    cfg.update(rows=rows, order=ORDER if cube else None)

    own_attn = jnp.concatenate([w_out.T, w_query, w_key, w_value], axis=1).astype(BF)
    own_up = jnp.pad(w_up.astype(BF), ((0, 0), (0, hidden - units)))
    own_down = jnp.pad(w_down.T.astype(BF), ((0, 0), (0, hidden - units)))
    skip = jnp.zeros((span - base,), F32)
    own_bias = jnp.concatenate(
        [skip, b_query, jnp.zeros((span,), F32), b_value, b_up, jnp.zeros((hidden - units,), F32)]
    )[None]
    flag = lax.dynamic_index_in_dim(image_flags, z, 0, keepdims=False)
    place = jnp.stack([d, z, flag]).astype(jnp.int32)

    pad_rows = ((0, m - seq), (0, 0))
    x = jnp.pad(lax.dynamic_slice_in_dim(tokens, z * seq, seq, 0), pad_rows)
    eb = jnp.pad(lax.dynamic_slice_in_dim(cotangent, z * seq, seq, 0) * flag.astype(BF), pad_rows)
    a1, a1t, et, sum_e = norm_one(cfg, place, x, eb, gain_one[None], shift_one[None])

    every = list(range(size))
    pin = {}
    attn_w = gather_all(own_attn, split)
    if cube:
        bits = []
        for _ in range(3):
            top = lax.reduce_precision(own_bias[0], 8, 7)
            bits.append(top.astype(BF))
            own_bias = own_bias - top[None]
        bits = jnp.concatenate(bits)
        count = bits.shape[0]
        extra = up(-(-count // hidden), 16)
        bits = jnp.pad(bits, (0, extra * hidden - count)).reshape(extra, hidden)
        ffn_held = gather_ring(jnp.concatenate([own_up, bits]))
        bias = []
        for v in ffn_held:
            v = v[rows:].reshape(-1)[:count].reshape(3, -1).astype(F32)
            bias.append((v[0] + v[1] + v[2])[None])
        up_held = [v[:rows] for v in ffn_held]
        both_up = [gather_near(up_held, 0), gather_near(ties(up_held, sum_e), 1)]
        far_up = [gather_far(both_up[i], i) for i in range(2)]
        core_up = swap(jnp.stack(both_up), CORE)
        pin["attn0"] = [*far_up]
        own_down = tie(own_down, *far_up)
    else:
        bias = gather_ring(own_bias)
        up_w = gather_all(own_up, split)
    kept = [
        attn_fwd(cfg, place, pin.get(f"attn{k}", []), attn_w[k], a1, bias[k][:, :qw]) for k in every
    ]
    h, a2, a2t = norm_two(
        cfg, place, pin.get("norm_two", []), attn_w, x, b_out[None], gain_two[None], shift_two[None],
        [o for _, o, _ in kept],
    )
    down_w = gather_all(tie(own_down, attn_w[0].arrays[0]), split)
    if cube:
        up_w = gather_groups(both_up, core_up, far_up, swap(jnp.stack(far_up), CORE), rows)
    g, gp, g_down = ffn_one(
        cfg, place, pin.get("ffn_one", []), up_w, a2, jnp.stack(bias)[:, :, qw:], et
    )

    sum_down = scatter_placed(g_down)

    low, high = [1, 0], [3, 2]
    near3, far3, sum_high, dn2 = ffn_two(
        cfg, place, pin.get("two0", []), [up_w[k] for k in high], [down_w[k] for k in high], high, eb,
        a2t, gp, None,
    )
    mixed_links = [ACROSS, ALONG]
    if cube:
        up_high = Scatter([(near3, far3)], mixed_links)
        up_high_core = up_high.step_core()
    near1, far1, sum_low, dh, dhb, dht, vec_two = ffn_two(
        cfg, place, pin.get("two1", []), [up_w[k] for k in low], [down_w[k] for k in low], low, eb,
        a2t, gp, dn2, [h, gain_two[None]],
    )
    sum_dz = [sum_low[1], sum_low[0], sum_high[1], sum_high[0]]
    grads = [None] * size

    def backward(k, after):
        near, far, sums, dqkv = attn_bwd(cfg, place, after, attn_w[k], a1t, dhb, dht, *kept[k])
        grads[k] = (near, far, sums, dqkv)
        return Scatter([(near, far)], [ACROSS if k % 2 else ALONG])

    def finish(after):
        return mix(place, after, down_w, h, g, b_down[None])

    def finish_norm(after):
        return norm_back(
            cfg, place, after, attn_w, x, dh, gain_one[None], [grads[k][3] for k in every]
        )

    if cube:
        up_low = Scatter([(near1, far1)], mixed_links)
        up_z = Around(lambda k: (up_high if k > 1 else up_low).terms(1 - k % 2), size)
        attn_z = Around(lambda k: out[k].terms(0), size)
        out = {}
        pins = {k: [] for k in ("a3", "a2", "a1", "a0", "nb", "mix")}
        pins["a3"] += up_high_core
        pins["a2"] += up_low.step_core() + up_high.step_first(vec_two)
        out[3] = backward(3, pins["a3"])
        mark = grads[3][2]
        pins["a1"] += up_high.step_second(mark) + up_low.step_first(mark) + out[3].step_core()
        out[2] = backward(2, pins["a2"])
        mark = grads[2][2]
        pins["a0"] += up_low.step_second(mark) + out[3].step_first(mark) + out[2].step_core()
        out[1] = backward(1, pins["a1"])
        mark = grads[1][2]
        pins["nb"] += out[3].step_second(mark) + out[2].step_first(mark) + out[1].step_core()
        pins["nb"] += up_z.step(mark)
        out[0] = backward(0, pins["a0"])
        mark = grads[0][2]
        pins["nb"] += out[0].step_core()
        pins["mix"] += out[1].step_first(mark) + out[2].step_second(mark) + attn_z.step(mark)
        pins["mix"] += out[0].step_first() + up_z.step(mark)
        tokens_grad, vec_one = finish_norm(pins["nb"])
        out[1].step_second(vec_one)
        out[0].step_second(vec_one)
        attn_z.step(vec_one)
        up_z.step(vec_one)
        mixed = finish(pins["mix"])
        attn_z.step(mixed)
        grad_up, grad_attn = up_z.step(), attn_z.step()
    else:
        for k in high + low:
            backward(k, [])
        mixed = finish([])
        tokens_grad, vec_one = finish_norm([])
        rejoin = lambda a, b: [a[1], a[0], b[1], b[0]]
        grad_up = scatter_all(rejoin(near1, near3), rejoin(far1, far3))
        grad_attn = scatter_all([g[0][0] for g in grads], [g[1][0] for g in grads])
    sum_qkv = [g[2] for g in grads]
    grad_down = tie(sum_down, vec_one).astype(F32)[:, :units].T
    grad_up, grad_attn = grad_up.astype(F32), grad_attn.astype(F32)
    grad_up = grad_up[:, :units]
    pieces = jnp.concatenate([jnp.concatenate(sum_qkv), jnp.concatenate(sum_dz)], axis=1)
    order = jnp.stack([lax.rem(z - t + size, size) for t in range(size)])
    pieces = jnp.take(pieces, order, axis=0)
    sums = sum_all(
        jnp.concatenate([pieces.reshape(-1), vec_one.reshape(-1), vec_two.reshape(-1), sum_e[0]]),
        cube,
    )
    per = qw + hidden
    mine = lax.dynamic_index_in_dim(sums[: size * per].reshape(size, per), z, 0, keepdims=False)
    rest = sums[size * per :].reshape(6, dim)
    at = span - base
    return (
        mixed[:seq],
        tokens_grad[:seq],
        rest[0],
        rest[1],
        grad_attn[:, span : 2 * span],
        mine[at : at + span],
        grad_attn[:, 2 * span : 3 * span],
        grad_attn[:, 3 * span :],
        mine[at + 2 * span : at + 3 * span],
        grad_attn[:, :span].T,
        rest[4],
        rest[2],
        rest[3],
        grad_up,
        mine[qw : qw + units],
        grad_down,
        rest[5],
    )


SPECS_IN = (
    P("dp", None), P("dp"), P("dp", None), P(), P(), P("dp", "tensor"), P("tensor"),
    P("dp", "tensor"), P("dp", "tensor"), P("tensor"), P("tensor", "dp"), P(), P(), P(),
    P("dp", "tensor"), P("tensor"), P("tensor", "dp"), P(),
)
SPECS_OUT = (
    P(("dp", "tensor"), None), P(("dp", "tensor"), None), P(), P(), P("dp", "tensor"), P("tensor"),
    P("dp", "tensor"), P("dp", "tensor"), P("tensor"), P("tensor", "dp"), P(), P(), P(),
    P("dp", "tensor"), P("tensor"), P("tensor", "dp"), P(),
)


def solution(mesh):
    return jax.shard_map(
        on_device, mesh=mesh, in_specs=SPECS_IN, out_specs=SPECS_OUT, check_vma=False
    )
```

```python
from functools import partial

import jax
import jax.numpy as jnp
from jax import lax
from jax.experimental import pallas as pl
from jax.experimental.pallas import tpu as pltpu
from jax.sharding import PartitionSpec as P

HD = 72
LANES = 128
EPSILON = 1e-06
SCALE = HD**-0.5
SHARP = SCALE * 1.4426950408889634
GELU_A = 0.7978845608028654
GELU_B = 0.044715
BF = jnp.bfloat16
F32 = jnp.float32
ANY = pl.BlockSpec(memory_space=pl.ANY)
SMEM = pl.BlockSpec(memory_space=pltpu.SMEM)
VMEM = pl.BlockSpec(memory_space=pltpu.VMEM)


def up(value, step):
    return -(-value // step) * step


def nn(left, right):
    return lax.dot_general(left, right, (((1,), (0,)), ((), ())), preferred_element_type=F32)


def nt(left, right):
    return lax.dot_general(left, right, (((1,), (1,)), ((), ())), preferred_element_type=F32)


def whole(shape):
    return pl.BlockSpec(shape, lambda *_: (0,) * len(shape), pipeline_mode=pl.Buffered(1))


def stepped(shape, index=lambda i: i):
    return pl.BlockSpec((1,) + shape, lambda i, *_: (index(i),) + (0,) * len(shape))


def call(
    kernel, name, us, place, weights, after, ins, outs, scratch, late=(), grid=None, specs=None, mib=40,
    prefetch=False,
):
    weights, after, late = list(weights), list(after), list(late)
    lead = 1 + len(weights) + len(after) + len(late)
    scratch = list(scratch)
    if late:
        scratch += [pltpu.VMEM(v.shape, v.dtype) for v in late] + [pltpu.SemaphoreType.DMA((len(late),))]

    def body(*refs):
        if not late:
            return kernel(refs[0], refs[1 : 1 + len(weights)], *refs[lead:])
        n = len(late)
        *rest, sems = refs[lead:]
        inputs = Late(refs[lead - n : lead], rest[-n:], sems)
        return kernel(refs[0], refs[1 : 1 + len(weights)], *rest[:-n], inputs)

    in_specs, out_specs = specs or ([VMEM] * len(ins), [VMEM] * len(outs))
    return pl.pallas_call(
        body,
        grid_spec=pltpu.PrefetchScalarGridSpec(
            num_scalar_prefetch=1 if prefetch else 0,
            grid=grid or (),
            in_specs=([] if prefetch else [SMEM]) + [ANY] * (lead - 1) + list(in_specs),
            out_specs=list(out_specs),
            scratch_shapes=scratch,
        ),
        out_shape=[jax.ShapeDtypeStruct(*out) for out in outs],
        compiler_params=pltpu.CompilerParams(vmem_limit_bytes=mib * 2**20),
        cost_estimate=pl.CostEstimate(
            flops=int(us * 1.15e9), bytes_accessed=int(us * 1e5), transcendentals=0
        ),
        name=name,
    )(place, *weights, *after, *late, *ins)


class Late:
    def __init__(self, sources, buffers, sems):
        self.buffers = buffers
        self.copies = [
            pltpu.make_async_copy(source, buffer, sems.at[i])
            for i, (source, buffer) in enumerate(zip(sources, buffers))
        ]

    def start(self):
        for copy in self.copies:
            copy.start()

    def take(self, i):
        self.copies[i].wait()
        return self.buffers[i]


class Piece:
    def __init__(self, arrays, blocks):
        self.arrays, self.blocks = arrays, blocks

    def fetch(self, refs, place_ref, buffer, sem, columns=None):
        for array, lead, first, rows in self.blocks(place_ref[0], place_ref[1]):
            source = refs[array].at[lead]
            if columns is not None:
                source = source.at[:, :columns]
            pltpu.make_async_copy(source, buffer.at[pl.ds(first, rows), :], sem).start()


def fetch_step(pieces, which, refs, place_ref, buffer, sem):
    begin = 0
    for index, piece in enumerate(pieces):
        mine = refs[begin : begin + len(piece.arrays)]
        begin += len(piece.arrays)

        @pl.when(which == index)
        def _():
            piece.fetch(mine, place_ref, buffer, sem)


def arrays_of(pieces):
    return [array for piece in pieces for array in piece.arrays]


def landed(buffer, sem):
    pltpu.make_async_copy(buffer, buffer, sem).wait()


def turn(cfg, d, value, out_ref, scratch):
    rows, order = cfg["rows"], cfg["order"]
    if order is None:
        out_ref[...] = value.T
        return
    scratch[...] = value.T
    for place, offset in enumerate(order):
        first = pl.multiple_of(jnp.bitwise_xor(d, offset) * rows, 16)
        out_ref[place * rows : (place + 1) * rows, :] = scratch[pl.ds(first, rows), :]


STEP = 32


def over_rows(total, body, carry):
    def step(t, carry):
        return body(pl.ds(pl.multiple_of(t * STEP, STEP), STEP), carry)

    return lax.fori_loop(0, total // STEP, step, carry, unroll=4)


def norm_stats(rows):
    average = jnp.mean(rows, axis=-1, keepdims=True)
    centred = rows - average
    inverse = lax.rsqrt(jnp.mean(centred * centred, axis=-1, keepdims=True) + EPSILON)
    return centred * inverse, inverse


def fold(value):
    return jnp.sum(value.reshape(STEP // 8, 8, value.shape[1]), axis=0)


def total_of(partial_sums):
    return jnp.sum(partial_sums, axis=0, keepdims=True)


def norm_one_kernel(
    cfg, place_ref, _, x_ref, eb_ref, gain_ref, shift_ref, a_ref, at_ref, et_ref, sum_ref, scratch
):
    def rows_of(rows, carry):
        unit, _ = norm_stats(x_ref[rows, :].astype(F32))
        a_ref[rows, :] = (unit * gain_ref[...] + shift_ref[...]).astype(BF)
        return carry + fold(eb_ref[rows, :].astype(F32))

    m, dim = x_ref.shape
    sum_ref[...] = total_of(over_rows(m, rows_of, jnp.zeros((8, dim), F32)))
    turn(cfg, place_ref[0], a_ref[...], at_ref, scratch)
    et_ref[...] = eb_ref[...].T


def norm_one(cfg, place, x, eb, gain, shift):
    m, d = x.shape
    outs = [((m, d), BF), ((d, m), BF), ((d, m), BF), ((1, d), F32)]
    return call(
        partial(norm_one_kernel, cfg), "norm_one", 6, place, [], [], [x, eb, gain, shift], outs,
        [pltpu.VMEM((d, m), BF)],
    )


def norm_two_kernel(cfg, pieces, place_ref, w_refs, b_out, gain, shift, *refs):
    n = len(pieces)
    h_ref, a_ref, at_ref, w, scratch, sems, late = refs
    late.start()
    begin = 0
    for i, piece in enumerate(pieces):
        mine = w_refs[begin : begin + len(piece.arrays)]
        begin += len(piece.arrays)
        piece.fetch(mine, place_ref, w.at[i], sems.at[i], cfg["wide"])
    for i in range(n):
        landed(w.at[i], sems.at[i])
        part = nt(late.take(i)[...], w[i])
        h_ref[...] = part if i == 0 else h_ref[...] + part
    x_ref = late.take(n)

    def rows_of(rows, carry):
        h = x_ref[rows, :].astype(F32) + h_ref[rows, :] + b_out[...]
        h_ref[rows, :] = h
        unit, _ = norm_stats(h)
        a_ref[rows, :] = (unit * gain[...] + shift[...]).astype(BF)
        return carry

    over_rows(x_ref.shape[0], rows_of, 0)
    turn(cfg, place_ref[0], a_ref[...], at_ref, scratch)


def norm_two(cfg, place, after, pieces, x, b_out, gain, shift, o):
    m, d = x.shape
    n = len(pieces)
    outs = [((m, d), F32), ((m, d), BF), ((d, m), BF)]
    return call(
        partial(norm_two_kernel, cfg, pieces), "norm_two", 12, place, arrays_of(pieces), after,
        [b_out, gain, shift], outs,
        [
            pltpu.VMEM((n, d, cfg["wide"]), BF),
            pltpu.VMEM((d, m), BF),
            pltpu.SemaphoreType.DMA((n,)),
        ],
        late=[*o, x],
    )


def mixed_kernel(pieces, place_ref, w_refs, h_ref, g_ref, b_down, out_ref, acc, w, sems):
    step = pl.program_id(0)
    flag = place_ref[2].astype(F32)

    @pl.when(step == 0)
    def _():
        fetch_step(pieces, 0, w_refs, place_ref, w.at[0], sems.at[0])
        acc[...] = h_ref[...] + b_down[...]

    slot = lax.rem(step, 2)
    fetch_step(pieces, step + 1, w_refs, place_ref, w.at[1 - slot], sems.at[1 - slot])
    landed(w.at[slot], sems.at[slot])
    acc[...] += nt(g_ref[0], w[slot])

    @pl.when(step == len(pieces) - 1)
    def _():
        out_ref[...] = (acc[...] * flag).astype(BF)


def mix(place, after, pieces, h, g, b_down):
    m, d = h.shape
    width = g.shape[2]
    return call(
        partial(mixed_kernel, pieces), "mixed", 14, place, arrays_of(pieces), after, [h, g, b_down],
        [((m, d), BF)],
        [pltpu.VMEM((m, d), F32), pltpu.VMEM((2, d, width), BF), pltpu.SemaphoreType.DMA((2,))],
        grid=(len(pieces),),
        specs=([whole((m, d)), stepped((m, width)), whole((1, d))], [whole((m, d))]),
    )[0]


def norm_back_kernel(cfg, pieces, place_ref, w_refs, gain, *refs):
    n = len(pieces)
    out_ref, vec_ref, dn, w, sems, late = refs
    late.start()
    parts, begin = [], 0
    for piece in pieces:
        parts.append(w_refs[begin : begin + len(piece.arrays)])
        begin += len(piece.arrays)
    pieces[0].fetch(parts[0], place_ref, w.at[0], sems.at[0])
    for i in range(n):
        if i + 1 < n:
            pieces[i + 1].fetch(parts[i + 1], place_ref, w.at[(i + 1) % 2], sems.at[(i + 1) % 2])
        landed(w.at[i % 2], sems.at[i % 2])
        part = nt(late.take(i)[...], w[i % 2, :, cfg["base"] :])
        dn[...] = part if i == 0 else dn[...] + part
    x_ref, dh_ref = late.take(n), late.take(n + 1)

    def rows_of(rows, carry):
        unit, inverse = norm_stats(x_ref[rows, :].astype(F32))
        grad = dn[rows, :]
        scaled = grad * gain[...]
        out = dh_ref[rows, :] + inverse * (
            scaled
            - jnp.mean(scaled, axis=-1, keepdims=True)
            - unit * jnp.mean(scaled * unit, axis=-1, keepdims=True)
        )
        out_ref[rows, :] = out.astype(BF)
        return carry[0] + fold(grad * unit), carry[1] + fold(grad)

    m, dim = x_ref.shape
    zero = jnp.zeros((8, dim), F32)
    for i, value in enumerate(over_rows(m, rows_of, (zero, zero))):
        vec_ref[i : i + 1, :] = total_of(value)


def norm_back(cfg, place, after, pieces, x, dh, gain, grads):
    m, d = x.shape
    outs = [((m, d), BF), ((2, d), F32)]
    return call(
        partial(norm_back_kernel, cfg, pieces), "norm_back", 18, place, arrays_of(pieces), after,
        [gain], outs,
        [
            pltpu.VMEM((m, d), F32),
            pltpu.VMEM((2, d, cfg["width"]), BF),
            pltpu.SemaphoreType.DMA((2,)),
        ],
        late=[*grads, x, dh],
    )


def pad_heads(cfg, refs):
    m, seq = cfg["m"], cfg["seq"]
    lane = lax.broadcasted_iota(jnp.int32, (m, LANES - HD), 1)
    row = lax.broadcasted_iota(jnp.int32, (m, LANES - HD), 0)
    one = jnp.where(lane == 0, 1.0, 0.0).astype(BF)
    past = jnp.where((lane == 0) & (row >= seq), -1e30, 0.0).astype(BF)
    for h in range(cfg["heads"]):
        for ref, fill in zip(refs, (one, past, one)):
            ref[h, :, HD:] = fill


def attn_fwd_kernel(cfg, piece, place_ref, w_refs, a_ref, bias_ref, *refs):
    qkv_ref, o_ref, lse_ref, w, q_s, k_s, v_s, vt, ot, sem = refs
    m, heads, base, wide = cfg["m"], cfg["heads"], cfg["base"], cfg["wide"]
    piece.fetch(w_refs, place_ref, w, sem)
    pad_heads(cfg, (q_s, k_s, v_s))
    ot[...] = jnp.zeros_like(ot)
    lse_ref[...] = jnp.zeros_like(lse_ref)
    landed(w, sem)
    qkv_ref[...] = (nn(a_ref[...], w[:, base:]) + bias_ref[...]).astype(BF)
    span = heads * HD
    skip = span - base
    for h in range(heads):
        for n, s in enumerate((q_s, k_s, v_s)):
            at = skip + n * span + h * HD
            s[h, :, :HD] = qkv_ref[:, at : at + HD]
        vt[h] = v_s[h].T
        s = nt(k_s[h], q_s[h])
        highest = jnp.max(s, axis=0, keepdims=True) * SHARP
        p = jnp.exp2(s * SHARP - highest).astype(BF)
        mixed = nn(vt[h], p)
        total = mixed[HD : HD + 1, :]
        ot[h * HD : (h + 1) * HD, :] = mixed[:HD, :] * (1.0 / total)
        lse_ref[h : h + 1, :] = highest + jnp.log2(total)
    o_ref[...] = ot[...].T.astype(BF)


def attn_fwd(cfg, place, after, piece, a, bias):
    m, dim = a.shape
    qw, wide, heads, width = cfg["qw"], cfg["wide"], cfg["heads"], cfg["width"]
    outs = [((m, qw), BF), ((m, wide), BF), ((8, m), F32)]
    scratch = (
        [pltpu.VMEM((dim, width), BF)]
        + [pltpu.VMEM((heads, m, LANES), BF)] * 3
        + [
            pltpu.VMEM((heads, LANES, m), BF),
            pltpu.VMEM((wide, m), F32),
            pltpu.SemaphoreType.DMA,
        ]
    )
    return call(
        partial(attn_fwd_kernel, cfg, piece), "attn_fwd", 8, place, piece.arrays, after, [a, bias],
        outs, scratch, mib=28,
    )


def attn_bwd_kernel(cfg, piece, place_ref, w_refs, *refs):
    dh_ref, qkv_ref, lse_ref, ga_ref, gb_ref, sum_ref, dqkv, *refs = refs
    w, q_s, k_s, v_s, do_s, kt, do_all, dqt, p_s, ds_s, sem, late = refs
    m, heads, base, wide = cfg["m"], cfg["heads"], cfg["base"], cfg["wide"]
    tile = m // 2
    piece.fetch(w_refs, place_ref, w, sem, wide)
    late.start()
    span = heads * HD
    skip = span - base
    pad_heads(cfg, (q_s, k_s))
    dqt[...] = jnp.zeros_like(dqt)
    dqkv[:, :LANES] = jnp.zeros((m, LANES), BF)
    for h in range(heads):
        v_s[h, :, HD:] = jnp.zeros((m, LANES - HD), BF)
        do_s[h, :, HD:] = jnp.zeros((m, LANES - HD), BF)
        for n, s in enumerate((q_s, k_s, v_s)):
            at = skip + n * span + h * HD
            s[h, :, :HD] = qkv_ref[:, at : at + HD]
        kt[h] = k_s[h].T
    landed(w, sem)
    do_all[...] = nn(dh_ref[...], w[...]).astype(BF)
    for h in range(heads):
        do_s[h, :, :HD] = do_all[:, h * HD : (h + 1) * HD]
        for t in range(m // tile):
            cols = slice(t * tile, (t + 1) * tile)
            p = jnp.exp2(nt(k_s[h], q_s[h, cols, :]) * SHARP - lse_ref[h : h + 1, cols])
            dp = nt(v_s[h], do_s[h, cols, :])
            ds = (p * (dp - jnp.sum(dp * p, axis=0, keepdims=True))).astype(BF)
            p_s[h % 2, :, cols] = p.astype(BF)
            ds_s[h % 2, :, cols] = ds
            dqt[h * HD : (h + 1) * HD, cols] = nn(kt[h], ds)[:HD] * SCALE
        dk = (nn(ds_s[h % 2], q_s[h]) * SCALE).astype(BF)
        dv = nn(p_s[h % 2], do_s[h]).astype(BF)
        at = skip + span + h * HD
        dqkv[:, at : at + HD] = dk[:, :HD]
        at = skip + 2 * span + h * HD
        dqkv[:, at : at + HD] = dv[:, :HD]
    dqkv[:, skip : skip + span] = dqt[...].T.astype(BF)[:, :span]
    grads = dqkv[...]
    sum_ref[...] = jnp.sum(grads.astype(F32), axis=0, keepdims=True)
    at_ref, dht_ref, o_ref = (late.take(i) for i in range(3))
    half = at_ref.shape[0] // 2
    for n, g_ref in ((1, gb_ref), (0, ga_ref)):
        rows = slice(n * half, (n + 1) * half)
        left = nn(dht_ref[rows, :], o_ref[...])
        right = nn(at_ref[rows, :], grads)
        g_ref[0, :, :base] = left[:, :base].astype(BF)
        g_ref[0, :, base:wide] = (left[:, base:] + right[:, : wide - base]).astype(BF)
        g_ref[0, :, wide:] = right[:, wide - base :].astype(BF)


def attn_bwd(cfg, place, after, piece, at, dh, dht, qkv, o, lse):
    dim, m = at.shape
    qw, wide, heads, width = cfg["qw"], cfg["wide"], cfg["heads"], cfg["width"]
    outs = [((1, dim // 2, width), BF)] * 2 + [((1, qw), F32), ((m, qw), BF)]
    scratch = (
        [pltpu.VMEM((dim, wide), BF)]
        + [pltpu.VMEM((heads, m, LANES), BF)] * 4
        + [
            pltpu.VMEM((heads, LANES, m), BF),
            pltpu.VMEM((m, wide), BF),
            pltpu.VMEM((wide, m), F32),
            pltpu.VMEM((2, m, m), BF),
            pltpu.VMEM((2, m, m), BF),
            pltpu.SemaphoreType.DMA,
        ]
    )
    return call(
        partial(attn_bwd_kernel, cfg, piece), "attn_bwd", 17, place, piece.arrays, after,
        [dh, qkv, lse], outs, scratch, late=[at, dht, o], mib=36,
    )


def ffn_one_kernel(cfg, pieces, place_ref, w_refs, a_ref, bias_ref, *refs):
    g_ref, gp_ref, grad_ref, w, sems, late = refs
    step = pl.program_id(0)

    @pl.when(step == 0)
    def _():
        late.start()
        fetch_step(pieces, 0, w_refs, place_ref, w.at[0], sems.at[0])

    slot = lax.rem(step, 2)
    fetch_step(pieces, step + 1, w_refs, place_ref, w.at[1 - slot], sems.at[1 - slot])
    landed(w.at[slot], sems.at[slot])
    width = g_ref.shape[2]

    @pl.when(step == 0)
    def _():
        late.take(0)

    et_ref = late.buffers[0]
    count, _, rows, _ = grad_ref.shape
    half_rows = et_ref.shape[0] // 2
    blocks = [slice(n, min(n + 256, width)) for n in range(0, width, 256)]

    def before(cols):
        return nn(a_ref[...], w[slot, :, cols]) + bias_ref[0, :, cols]

    pre = before(blocks[0])
    for n, cols in enumerate(blocks):
        following = before(blocks[n + 1]) if n + 1 < len(blocks) else None
        square = pre * pre
        half = 0.5 + 0.5 * jnp.tanh(pre * (GELU_A + GELU_A * GELU_B * square))
        g_ref[0, :, cols] = (pre * half).astype(BF)
        slope = half + (half - half * half) * (pre * (2 * GELU_A + 6 * GELU_A * GELU_B * square))
        gp_ref[0, :, cols] = slope.astype(BF)
        for part in range(2):
            left = et_ref[part * half_rows : (part + 1) * half_rows, :]
            value = nn(left, g_ref[0, :, cols]).astype(BF)
            for i in range(count // 2):
                grad_ref[part * count // 2 + i, 0, :, cols] = value[i * rows : (i + 1) * rows]
        pre = following


def ffn_one(cfg, place, after, pieces, a, bias, et):
    dim, m = et.shape
    n, width = len(pieces), bias.shape[2]
    rows = cfg["rows"] if cfg["rows"] % 16 == 0 else dim // 2
    outs = [((n, m, width), BF)] * 2 + [((dim // rows, n, rows, width), BF)]
    return call(
        partial(ffn_one_kernel, cfg, pieces), "ffn_one", 30, place, arrays_of(pieces), after,
        [a, bias], outs,
        [pltpu.VMEM((2, dim, width), BF), pltpu.SemaphoreType.DMA((2,))],
        late=[et], grid=(n,),
        specs=(
            [whole((m, dim)), stepped((1, width))],
            [stepped((m, width))] * 2
            + [
                pl.BlockSpec(
                    (dim // rows, 1, rows, width),
                    lambda i, place_ref: (0, lax.rem(place_ref[1] - i + n, n), 0, 0),
                )
            ],
        ),
        mib=56, prefetch=True,
    )


def ffn_two_kernel(cfg, ups, downs, first, last, place_ref, w_refs, eb_ref, gp_ref, *refs):
    *refs, late = refs
    if last:
        gain, *refs = refs
    near_ref, far_ref, sum_ref, *refs = refs
    if last:
        dh_ref, dhb_ref, dht_ref, vec_ref, *refs = refs
        wu, wd, dz, dn_ref, scratch, sems = refs
    else:
        dn_ref, wu, wd, dz, sems = refs
    step = pl.program_id(0)
    count = len(arrays_of(ups))
    n = len(ups)

    at_ref = late.buffers[0]

    def get(which, slot):
        fetch_step(downs, which, w_refs[count:], place_ref, wd.at[slot], sems.at[1, slot])
        fetch_step(ups, which, w_refs[:count], place_ref, wu.at[slot], sems.at[0, slot])

    @pl.when(step == 0)
    def _():
        get(0, 0)
        late.start()
        if first:
            dn_ref[...] = jnp.zeros_like(dn_ref)

    slot = lax.rem(step, 2)
    get(step + 1, 1 - slot)
    landed(wd.at[slot], sems.at[1, slot])
    width = dz.shape[1]
    for c in range(0, width, 256):
        cols = slice(c, min(c + 256, width))
        grad = (nn(eb_ref[...], wd[slot, :, cols]) * gp_ref[0, :, cols].astype(F32)).astype(BF)
        dz[:, cols] = grad
        sum_ref[0, :, cols] = jnp.sum(grad.astype(F32), axis=0, keepdims=True)
    landed(wu.at[slot], sems.at[0, slot])
    part = nt(dz[...], wu[slot])

    @pl.when(step == 0)
    def _():
        late.take(0)
        if not first:
            dn_ref[...] = late.take(1)[...]

    dn_ref[...] += part
    middle = at_ref.shape[0] // 2
    far_ref[0] = nn(at_ref[middle:, :], dz[...]).astype(BF)
    near_ref[0] = nn(at_ref[:middle, :], dz[...]).astype(BF)
    if not last:
        return

    @pl.when(step == n - 1)
    def _():
        h_ref = late.take(2)

        def rows_of(rows, carry):
            unit, inverse = norm_stats(h_ref[rows, :])
            grad = dn_ref[rows, :]
            scaled = grad * gain[...]
            dh = eb_ref[rows, :].astype(F32) + inverse * (
                scaled
                - jnp.mean(scaled, axis=-1, keepdims=True)
                - unit * jnp.mean(scaled * unit, axis=-1, keepdims=True)
            )
            dh_ref[rows, :] = dh
            dhb_ref[rows, :] = dh.astype(BF)
            return carry[0] + fold(grad * unit), carry[1] + fold(grad), carry[2] + fold(dh)

        m, dim = h_ref.shape
        zero = jnp.zeros((8, dim), F32)
        sums = over_rows(m, rows_of, (zero, zero, zero))
        for i, value in enumerate(sums):
            vec_ref[i : i + 1, :] = total_of(value)
        turn(cfg, place_ref[0], dhb_ref[...], dht_ref, scratch)


def ffn_two(cfg, place, after, ups, downs, ks, eb, at, gp, dn, closing=None):
    dim, m = at.shape
    n, width = len(ups), gp.shape[2]
    block = (dim // 2, width)
    at_k = lambda i: ks[0] + i if ks[0] < ks[-1] else ks[0] - i
    ins, in_specs, late = [eb, gp], [whole((m, dim)), stepped((m, width), at_k)], [at]
    if closing:
        ins.append(closing[1])
        in_specs.append(whole((1, dim)))
        late += [dn, closing[0]]
    outs = [((n,) + block, BF)] * 2 + [((n, 1, width), F32)]
    out_specs = [stepped(block)] * 2 + [stepped((1, width))]
    scratch = [
        pltpu.VMEM((2, dim, width), BF), pltpu.VMEM((2, dim, width), BF), pltpu.VMEM((m, width), BF)
    ]
    if closing:
        shapes = [((m, dim), F32), ((m, dim), BF), ((dim, m), BF), ((3, dim), F32)]
        scratch += [pltpu.VMEM((m, dim), F32), pltpu.VMEM((dim, m), BF)]
    else:
        shapes = [((m, dim), F32)]
    outs += shapes
    out_specs += [whole(shape) for shape, _ in shapes]
    return call(
        partial(ffn_two_kernel, cfg, ups, downs, dn is None, bool(closing)), "ffn_two",
        30 if closing else 24, place, arrays_of(ups) + arrays_of(downs), after, ins, outs,
        scratch + [pltpu.SemaphoreType.DMA((2, 2))], late=late, grid=(n,),
        specs=(in_specs, out_specs), mib=58,
    )


CORE, ACROSS, ALONG = 1, 2, 4
CUBE = 8
ORDER = (0, ACROSS, ALONG, ACROSS + ALONG, CORE, CORE + ACROSS, CORE + ALONG, CORE + ACROSS + ALONG)


def ring(value, by, size):
    return lax.ppermute(value, "tensor", [(i, (i + by) % size) for i in range(size)])


def swap(value, offset):
    return lax.ppermute(value, "dp", [(i, i ^ offset) for i in range(lax.axis_size("dp"))])


def tie(value, *others):
    return lax.optimization_barrier((value, *others))[0]


def ties(values, mark):
    return list(lax.optimization_barrier((*values, mark))[:-1])


def gather_all(own, split):
    dp, size = lax.axis_size("dp"), lax.axis_size("tensor")
    rows = own.shape[0]
    full = lax.all_gather(own, ("dp", "tensor"), axis=0, tiled=False)
    if split:

        def blocks(k, d, z):
            t = lax.rem(z - k + size, size)
            return [(0, i * size + t, i * rows, rows) for i in range(dp)]
    else:
        full = full.reshape(dp, size, rows, -1).transpose(1, 0, 2, 3)
        full = full.reshape(size, dp * rows, -1)

        def blocks(k, d, z):
            return [(0, lax.rem(z - k + size, size), 0, dp * rows)]

    return [Piece([full], partial(blocks, k)) for k in range(size)]


def gather_ring(own):
    size = lax.axis_size("tensor")
    held = [own]
    for _ in range(size - 1):
        held.append(ring(held[-1], 1, size))
    return held


def gather_near(held, group):
    mine = jnp.stack(held[2 * group : 2 * group + 2])
    return jnp.stack([mine, swap(mine, (ACROSS, ALONG)[group])])


def gather_far(both, group):
    return swap(both, (ALONG, ACROSS)[group])


def gather_groups(both, both_core, far, far_core, rows):
    firsts = (ACROSS, ACROSS, ALONG, ALONG)

    def blocks(k, d, z):
        group, n = k // 2, k % 2
        first = firsts[k]
        second = ACROSS + ALONG - first
        out = []
        for other in range(2):
            for index, lead, offset in (
                (group, (other, n), 0),
                (2, (group, other, n), CORE),
                (3 + group, (other, n), second),
                (5, (group, other, n), CORE + second),
            ):
                at = pl.multiple_of(jnp.bitwise_xor(d, offset + other * first) * rows, 16)
                out.append((index, lead, at, rows))
        return out

    return [Piece([*both, both_core, *far, far_core], partial(blocks, k)) for k in range(4)]


def scatter_all(near, far):
    size, dp = lax.axis_size("tensor"), lax.axis_size("dp")
    z = lax.axis_index("tensor")
    pieces = jnp.stack([jnp.concatenate(halves) for halves in zip(near, far)])
    dim, width = pieces.shape[1:]
    order = jnp.stack([lax.rem(z - t + size, size) for t in range(size)])
    return scatter_placed(jnp.take(pieces, order, axis=0)[None])


def scatter_placed(value):
    size, dp = lax.axis_size("tensor"), lax.axis_size("dp")
    blocks, _, rows, width = value.shape
    if blocks != dp:
        value = value.transpose(1, 0, 2, 3).reshape(size, dp, -1, width).transpose(1, 0, 2, 3)
    value = value.reshape(dp * size, -1, width)
    return lax.psum_scatter(value, ("dp", "tensor"), scatter_dimension=0, tiled=True)[0]


def add(*terms):
    total = terms[0].astype(F32)
    for term in terms[1:]:
        total = total + term.astype(F32)
    return total


class Scatter:
    def __init__(self, halves, links):
        self.links = links
        self.near = [piece for near, _ in halves for piece in self.split(near)]
        self.far = [far for _, far in halves]

    def split(self, value):
        count, half, width = value.shape
        value = value.reshape(count, 2, 2, half // 4, width)
        return [value[i] for i in range(count)]

    def pick(self, value, link, i, j):
        return value[j, i] if link == ACROSS else value[i, j]

    def send(self, step, outs):
        got, sent = [None] * len(outs), []
        for link in (ACROSS, ALONG):
            mine = [i for i, first in enumerate(self.links) if (first == link) == (step == 1)]
            if not mine:
                continue
            value = swap(jnp.stack([v for i in mine for v in outs[i]]), link)
            sent.append(value)
            for n, i in enumerate(mine):
                count = len(outs[i])
                got[i] = [value[n * count + c] for c in range(count)]
        return got, sent

    def step_core(self):
        sent = [swap(far, CORE) for far in self.far]
        self.core = [piece for value in sent for piece in self.split(value)]
        return sent

    def step_first(self, mark=None):
        if mark is not None:
            self.core = ties(self.core, mark)
        outs = [
            [add(self.pick(a, link, 1, j), self.pick(b, link, 1, j)).astype(BF) for j in range(2)]
            for a, b, link in zip(self.near, self.core, self.links)
        ]
        self.one, sent = self.send(1, outs)
        return sent

    def step_second(self, mark=None):
        if mark is not None:
            flat = ties([v for one in self.one for v in one], mark)
            self.one = [flat[2 * i : 2 * i + 2] for i in range(len(self.one))]
        outs = [
            [add(self.pick(a, link, 0, 1), self.pick(b, link, 0, 1), one[1]).astype(BF)]
            for a, b, one, link in zip(self.near, self.core, self.one, self.links)
        ]
        self.two, sent = self.send(2, outs)
        return sent

    def terms(self, i):
        link = self.links[i]
        return [
            self.pick(self.near[i], link, 0, 0),
            self.pick(self.core[i], link, 0, 0),
            self.one[i][0],
            self.two[i][0],
        ]


class Around:
    def __init__(self, terms, size):
        self.terms, self.size, self.k, self.total = terms, size, size - 1, None

    def step(self, mark=None):
        terms = self.terms(self.k) + ([] if self.total is None else [self.total])
        if mark is not None:
            terms = terms[:-1] + [tie(terms[-1], mark)]
        total = add(*terms)
        self.k -= 1
        if self.k < 0:
            return total
        self.total = ring(total.astype(BF), -1, self.size)
        return [self.total]


def sum_all(vector, marks):
    if marks is None:
        return lax.psum(vector, ("dp", "tensor"))
    size = lax.axis_size("tensor")
    for offset in (CORE, ACROSS, ALONG):
        if offset == ALONG:
            vector = tie(vector, *marks[0])
        vector = vector + swap(vector, offset)
    offset = 1
    while offset < size:
        if 2 * offset == size:
            vector = tie(vector, *marks[1])
        vector = vector + lax.ppermute(vector, "tensor", [(i, i ^ offset) for i in range(size)])
        offset *= 2
    return vector


def on_device(
    tokens, image_flags, cotangent, gain_one, shift_one, w_query, b_query, w_key, w_value, b_value,
    w_out, b_out, gain_two, shift_two, w_up, b_up, w_down, b_down,
):
    dp, size = lax.axis_size("dp"), lax.axis_size("tensor")
    d, z = lax.axis_index("dp"), lax.axis_index("tensor")
    images = image_flags.shape[0]
    all_rows, dim = tokens.shape
    seq = all_rows // images
    assert images == size
    m = up(seq, 256)
    rows = dim // dp
    split = rows % 16 == 0
    span = w_query.shape[1]
    units = w_up.shape[1]
    hidden = up(units, LANES)
    width = 4 * span
    base, wide = span // LANES * LANES, up(span, LANES)
    qw = width - base
    cube = dp == CUBE and split and size == 4
    cfg = dict(m=m, seq=seq, heads=span // HD, base=base, wide=wide, width=width, qw=qw)
    cfg.update(rows=rows, order=ORDER if cube else None)

    own_attn = jnp.concatenate([w_out.T, w_query, w_key, w_value], axis=1).astype(BF)
    own_up = jnp.pad(w_up.astype(BF), ((0, 0), (0, hidden - units)))
    own_down = jnp.pad(w_down.T.astype(BF), ((0, 0), (0, hidden - units)))
    skip = jnp.zeros((span - base,), F32)
    own_bias = jnp.concatenate(
        [skip, b_query, jnp.zeros((span,), F32), b_value, b_up, jnp.zeros((hidden - units,), F32)]
    )[None]
    flag = lax.dynamic_index_in_dim(image_flags, z, 0, keepdims=False)
    place = jnp.stack([d, z, flag]).astype(jnp.int32)

    pad_rows = ((0, m - seq), (0, 0))
    x = jnp.pad(lax.dynamic_slice_in_dim(tokens, z * seq, seq, 0), pad_rows)
    eb = jnp.pad(lax.dynamic_slice_in_dim(cotangent, z * seq, seq, 0) * flag.astype(BF), pad_rows)
    a1, a1t, et, sum_e = norm_one(cfg, place, x, eb, gain_one[None], shift_one[None])

    every = list(range(size))
    pin = {}
    attn_w = gather_all(own_attn, split)
    if cube:
        bits = []
        for _ in range(3):
            top = lax.reduce_precision(own_bias[0], 8, 7)
            bits.append(top.astype(BF))
            own_bias = own_bias - top[None]
        bits = jnp.concatenate(bits)
        count = bits.shape[0]
        extra = up(-(-count // hidden), 16)
        bits = jnp.pad(bits, (0, extra * hidden - count)).reshape(extra, hidden)
        ffn_held = gather_ring(jnp.concatenate([own_up, bits]))
        bias = []
        for v in ffn_held:
            v = v[rows:].reshape(-1)[:count].reshape(3, -1).astype(F32)
            bias.append((v[0] + v[1] + v[2])[None])
        up_held = [v[:rows] for v in ffn_held]
        both_up = [gather_near(up_held, 0), gather_near(ties(up_held, sum_e), 1)]
        far_up = [gather_far(both_up[i], i) for i in range(2)]
        core_up = swap(jnp.stack(both_up), CORE)
        pin["attn0"] = [*far_up]
        own_down = tie(own_down, *far_up)
    else:
        bias = gather_ring(own_bias)
        up_w = gather_all(own_up, split)
    kept = [
        attn_fwd(cfg, place, pin.get(f"attn{k}", []), attn_w[k], a1, bias[k][:, :qw]) for k in every
    ]
    h, a2, a2t = norm_two(
        cfg, place, pin.get("norm_two", []), attn_w, x, b_out[None], gain_two[None], shift_two[None],
        [o for _, o, _ in kept],
    )
    down_w = gather_all(tie(own_down, attn_w[0].arrays[0]), split)
    if cube:
        up_w = gather_groups(both_up, core_up, far_up, swap(jnp.stack(far_up), CORE), rows)
    g, gp, g_down = ffn_one(
        cfg, place, pin.get("ffn_one", []), up_w, a2, jnp.stack(bias)[:, :, qw:], et
    )

    sum_down = scatter_placed(g_down)

    low, high = [1, 0], [3, 2]
    near3, far3, sum_high, dn2 = ffn_two(
        cfg, place, pin.get("two0", []), [up_w[k] for k in high], [down_w[k] for k in high], high, eb,
        a2t, gp, None,
    )
    mixed_links = [ACROSS, ALONG]
    if cube:
        up_high = Scatter([(near3, far3)], mixed_links)
        up_high_core = up_high.step_core()
    near1, far1, sum_low, dh, dhb, dht, vec_two = ffn_two(
        cfg, place, pin.get("two1", []), [up_w[k] for k in low], [down_w[k] for k in low], low, eb,
        a2t, gp, dn2, [h, gain_two[None]],
    )
    sum_dz = [sum_low[1], sum_low[0], sum_high[1], sum_high[0]]
    grads = [None] * size

    def backward(k, after):
        near, far, sums, dqkv = attn_bwd(cfg, place, after, attn_w[k], a1t, dhb, dht, *kept[k])
        grads[k] = (near, far, sums, dqkv)
        return Scatter([(near, far)], [ACROSS if k % 2 else ALONG])

    def finish(after):
        return mix(place, after, down_w, h, g, b_down[None])

    def finish_norm(after):
        return norm_back(
            cfg, place, after, attn_w, x, dh, gain_one[None], [grads[k][3] for k in every]
        )

    if cube:
        up_low = Scatter([(near1, far1)], mixed_links)
        up_z = Around(lambda k: (up_high if k > 1 else up_low).terms(1 - k % 2), size)
        attn_z = Around(lambda k: out[k].terms(0), size)
        out = {}
        pins = {k: [] for k in ("a3", "a2", "a1", "a0", "nb", "mix")}
        pins["a3"] += up_high_core
        pins["a2"] += up_low.step_core() + up_high.step_first(vec_two)
        out[3] = backward(3, pins["a3"])
        mark = grads[3][2]
        pins["a1"] += up_high.step_second(mark) + up_low.step_first(mark) + out[3].step_core()
        out[2] = backward(2, pins["a2"])
        mark = grads[2][2]
        pins["a0"] += up_low.step_second(mark) + out[3].step_first(mark) + out[2].step_core()
        out[1] = backward(1, pins["a1"])
        mark = grads[1][2]
        pins["nb"] += out[3].step_second(mark) + out[2].step_first(mark) + out[1].step_core()
        pins["nb"] += up_z.step(mark)
        out[0] = backward(0, pins["a0"])
        mark = grads[0][2]
        pins["nb"] += out[0].step_core()
        pins["mix"] += out[1].step_first(mark) + out[2].step_second(mark) + attn_z.step(mark)
        zero_first = out[0].step_first()
        pins["mix"] += up_z.step(mark)
        tokens_grad, vec_one = finish_norm(pins["nb"])
        vec_one = tie(vec_one, *zero_first)
        seconds = out[1].step_second(vec_one) + out[0].step_second(vec_one)
        attn_z.step(vec_one)
        up_z.step(vec_one)
        mixed = finish(pins["mix"])
        marks = (seconds + [mixed], attn_z.step())
        grad_up, grad_attn = up_z.step(), attn_z.step()
    else:
        for k in high + low:
            backward(k, [])
        mixed = finish([])
        tokens_grad, vec_one = finish_norm([])
        rejoin = lambda a, b: [a[1], a[0], b[1], b[0]]
        grad_up = scatter_all(rejoin(near1, near3), rejoin(far1, far3))
        grad_attn = scatter_all([g[0][0] for g in grads], [g[1][0] for g in grads])
    sum_qkv = [g[2] for g in grads]
    grad_down = tie(sum_down, vec_one).astype(F32)[:, :units].T
    grad_up, grad_attn = grad_up.astype(F32), grad_attn.astype(F32)
    grad_up = grad_up[:, :units]
    pieces = jnp.concatenate([jnp.concatenate(sum_qkv), jnp.concatenate(sum_dz)], axis=1)
    order = jnp.stack([lax.rem(z - t + size, size) for t in range(size)])
    pieces = jnp.take(pieces, order, axis=0)
    sums = sum_all(
        jnp.concatenate([pieces.reshape(-1), vec_one.reshape(-1), vec_two.reshape(-1), sum_e[0]]),
        marks if cube else None,
    )
    per = qw + hidden
    mine = lax.dynamic_index_in_dim(sums[: size * per].reshape(size, per), z, 0, keepdims=False)
    rest = sums[size * per :].reshape(6, dim)
    at = span - base
    return (
        mixed[:seq],
        tokens_grad[:seq],
        rest[0],
        rest[1],
        grad_attn[:, span : 2 * span],
        mine[at : at + span],
        grad_attn[:, 2 * span : 3 * span],
        grad_attn[:, 3 * span :],
        mine[at + 2 * span : at + 3 * span],
        grad_attn[:, :span].T,
        rest[4],
        rest[2],
        rest[3],
        grad_up,
        mine[qw : qw + units],
        grad_down,
        rest[5],
    )


SPECS_IN = (
    P("dp", None), P("dp"), P("dp", None), P(), P(), P("dp", "tensor"), P("tensor"),
    P("dp", "tensor"), P("dp", "tensor"), P("tensor"), P("tensor", "dp"), P(), P(), P(),
    P("dp", "tensor"), P("tensor"), P("tensor", "dp"), P(),
)
SPECS_OUT = (
    P(("dp", "tensor"), None), P(("dp", "tensor"), None), P(), P(), P("dp", "tensor"), P("tensor"),
    P("dp", "tensor"), P("dp", "tensor"), P("tensor"), P("tensor", "dp"), P(), P(), P(),
    P("dp", "tensor"), P("tensor"), P("tensor", "dp"), P(),
)


def solution(mesh):
    return jax.shard_map(
        on_device, mesh=mesh, in_specs=SPECS_IN, out_specs=SPECS_OUT, check_vma=False
    )
```

```python
from functools import partial

import jax
import jax.numpy as jnp
from jax import lax
from jax.experimental import pallas as pl
from jax.experimental.pallas import tpu as pltpu
from jax.sharding import PartitionSpec as P

HD = 72
LANES = 128
EPSILON = 1e-06
SCALE = HD**-0.5
SHARP = SCALE * 1.4426950408889634
GELU_A = 0.7978845608028654
GELU_B = 0.044715
BF = jnp.bfloat16
F32 = jnp.float32
ANY = pl.BlockSpec(memory_space=pl.ANY)
SMEM = pl.BlockSpec(memory_space=pltpu.SMEM)
VMEM = pl.BlockSpec(memory_space=pltpu.VMEM)


def up(value, step):
    return -(-value // step) * step


def nn(left, right):
    return lax.dot_general(left, right, (((1,), (0,)), ((), ())), preferred_element_type=F32)


def nt(left, right):
    return lax.dot_general(left, right, (((1,), (1,)), ((), ())), preferred_element_type=F32)


def whole(shape):
    return pl.BlockSpec(shape, lambda *_: (0,) * len(shape), pipeline_mode=pl.Buffered(1))


def stepped(shape, index=lambda i: i):
    return pl.BlockSpec((1,) + shape, lambda i, *_: (index(i),) + (0,) * len(shape))


def call(
    kernel, name, us, place, weights, after, ins, outs, scratch, late=(), grid=None, specs=None, mib=40,
    prefetch=False,
):
    weights, after, late = list(weights), list(after), list(late)
    lead = 1 + len(weights) + len(after) + len(late)
    scratch = list(scratch)
    if late:
        scratch += [pltpu.VMEM(v.shape, v.dtype) for v in late] + [pltpu.SemaphoreType.DMA((len(late),))]

    def body(*refs):
        if not late:
            return kernel(refs[0], refs[1 : 1 + len(weights)], *refs[lead:])
        n = len(late)
        *rest, sems = refs[lead:]
        inputs = Late(refs[lead - n : lead], rest[-n:], sems)
        return kernel(refs[0], refs[1 : 1 + len(weights)], *rest[:-n], inputs)

    in_specs, out_specs = specs or ([VMEM] * len(ins), [VMEM] * len(outs))
    return pl.pallas_call(
        body,
        grid_spec=pltpu.PrefetchScalarGridSpec(
            num_scalar_prefetch=1 if prefetch else 0,
            grid=grid or (),
            in_specs=([] if prefetch else [SMEM]) + [ANY] * (lead - 1) + list(in_specs),
            out_specs=list(out_specs),
            scratch_shapes=scratch,
        ),
        out_shape=[jax.ShapeDtypeStruct(*out) for out in outs],
        compiler_params=pltpu.CompilerParams(vmem_limit_bytes=mib * 2**20),
        cost_estimate=pl.CostEstimate(
            flops=int(us * 1.15e9), bytes_accessed=int(us * 1e5), transcendentals=0
        ),
        name=name,
    )(place, *weights, *after, *late, *ins)


class Late:
    def __init__(self, sources, buffers, sems):
        self.buffers = buffers
        self.copies = [
            pltpu.make_async_copy(source, buffer, sems.at[i])
            for i, (source, buffer) in enumerate(zip(sources, buffers))
        ]

    def start(self):
        for copy in self.copies:
            copy.start()

    def take(self, i):
        self.copies[i].wait()
        return self.buffers[i]


class Piece:
    def __init__(self, arrays, blocks):
        self.arrays, self.blocks = arrays, blocks

    def fetch(self, refs, place_ref, buffer, sem, columns=None):
        for array, lead, first, rows in self.blocks(place_ref[0], place_ref[1]):
            source = refs[array].at[lead]
            if columns is not None:
                source = source.at[:, :columns]
            pltpu.make_async_copy(source, buffer.at[pl.ds(first, rows), :], sem).start()


def fetch_step(pieces, which, refs, place_ref, buffer, sem):
    begin = 0
    for index, piece in enumerate(pieces):
        mine = refs[begin : begin + len(piece.arrays)]
        begin += len(piece.arrays)

        @pl.when(which == index)
        def _():
            piece.fetch(mine, place_ref, buffer, sem)


def arrays_of(pieces):
    return [array for piece in pieces for array in piece.arrays]


def landed(buffer, sem):
    pltpu.make_async_copy(buffer, buffer, sem).wait()


def turn(cfg, d, value, out_ref, scratch):
    rows, order = cfg["rows"], cfg["order"]
    if order is None:
        out_ref[...] = value.T
        return
    scratch[...] = value.T
    for place, offset in enumerate(order):
        first = pl.multiple_of(jnp.bitwise_xor(d, offset) * rows, 16)
        out_ref[place * rows : (place + 1) * rows, :] = scratch[pl.ds(first, rows), :]


STEP = 32


def over_rows(total, body, carry):
    def step(t, carry):
        return body(pl.ds(pl.multiple_of(t * STEP, STEP), STEP), carry)

    return lax.fori_loop(0, total // STEP, step, carry, unroll=8)


def norm_stats(rows):
    average = jnp.mean(rows, axis=-1, keepdims=True)
    centred = rows - average
    inverse = lax.rsqrt(jnp.mean(centred * centred, axis=-1, keepdims=True) + EPSILON)
    return centred * inverse, inverse


def fold(value):
    return jnp.sum(value.reshape(STEP // 8, 8, value.shape[1]), axis=0)


def total_of(partial_sums):
    return jnp.sum(partial_sums, axis=0, keepdims=True)


def norm_one_kernel(
    cfg, place_ref, _, x_ref, eb_ref, gain_ref, shift_ref, a_ref, at_ref, et_ref, sum_ref, scratch
):
    def rows_of(rows, carry):
        unit, _ = norm_stats(x_ref[rows, :].astype(F32))
        a_ref[rows, :] = (unit * gain_ref[...] + shift_ref[...]).astype(BF)
        return carry + fold(eb_ref[rows, :].astype(F32))

    m, dim = x_ref.shape
    sum_ref[...] = total_of(over_rows(m, rows_of, jnp.zeros((8, dim), F32)))
    turn(cfg, place_ref[0], a_ref[...], at_ref, scratch)
    et_ref[...] = eb_ref[...].T


def norm_one(cfg, place, x, eb, gain, shift):
    m, d = x.shape
    outs = [((m, d), BF), ((d, m), BF), ((d, m), BF), ((1, d), F32)]
    return call(
        partial(norm_one_kernel, cfg), "norm_one", 6, place, [], [], [x, eb, gain, shift], outs,
        [pltpu.VMEM((d, m), BF)],
    )


def norm_two_kernel(cfg, pieces, place_ref, w_refs, b_out, gain, shift, *refs):
    n = len(pieces)
    h_ref, a_ref, at_ref, w, scratch, sems, late = refs
    late.start()
    begin = 0
    for i, piece in enumerate(pieces):
        mine = w_refs[begin : begin + len(piece.arrays)]
        begin += len(piece.arrays)
        piece.fetch(mine, place_ref, w.at[i], sems.at[i], cfg["wide"])
    for i in range(n):
        landed(w.at[i], sems.at[i])
        part = nt(late.take(i)[...], w[i])
        h_ref[...] = part if i == 0 else h_ref[...] + part
    x_ref = late.take(n)

    def rows_of(rows, carry):
        h = x_ref[rows, :].astype(F32) + h_ref[rows, :] + b_out[...]
        h_ref[rows, :] = h
        unit, _ = norm_stats(h)
        a_ref[rows, :] = (unit * gain[...] + shift[...]).astype(BF)
        return carry

    over_rows(x_ref.shape[0], rows_of, 0)
    turn(cfg, place_ref[0], a_ref[...], at_ref, scratch)


def norm_two(cfg, place, after, pieces, x, b_out, gain, shift, o):
    m, d = x.shape
    n = len(pieces)
    outs = [((m, d), F32), ((m, d), BF), ((d, m), BF)]
    return call(
        partial(norm_two_kernel, cfg, pieces), "norm_two", 12, place, arrays_of(pieces), after,
        [b_out, gain, shift], outs,
        [
            pltpu.VMEM((n, d, cfg["wide"]), BF),
            pltpu.VMEM((d, m), BF),
            pltpu.SemaphoreType.DMA((n,)),
        ],
        late=[*o, x],
    )


def mixed_kernel(pieces, place_ref, w_refs, h_ref, g_ref, b_down, out_ref, acc, w, sems):
    step = pl.program_id(0)
    flag = place_ref[2].astype(F32)

    @pl.when(step == 0)
    def _():
        fetch_step(pieces, 0, w_refs, place_ref, w.at[0], sems.at[0])
        acc[...] = h_ref[...] + b_down[...]

    slot = lax.rem(step, 2)
    fetch_step(pieces, step + 1, w_refs, place_ref, w.at[1 - slot], sems.at[1 - slot])
    landed(w.at[slot], sems.at[slot])
    acc[...] += nt(g_ref[0], w[slot])

    @pl.when(step == len(pieces) - 1)
    def _():
        out_ref[...] = (acc[...] * flag).astype(BF)


def mix(place, after, pieces, h, g, b_down):
    m, d = h.shape
    width = g.shape[2]
    return call(
        partial(mixed_kernel, pieces), "mixed", 14, place, arrays_of(pieces), after, [h, g, b_down],
        [((m, d), BF)],
        [pltpu.VMEM((m, d), F32), pltpu.VMEM((2, d, width), BF), pltpu.SemaphoreType.DMA((2,))],
        grid=(len(pieces),),
        specs=([whole((m, d)), stepped((m, width)), whole((1, d))], [whole((m, d))]),
    )[0]


def norm_back_kernel(cfg, pieces, place_ref, w_refs, gain, *refs):
    n = len(pieces)
    out_ref, vec_ref, dn, w, sems, late = refs
    late.start()
    parts, begin = [], 0
    for piece in pieces:
        parts.append(w_refs[begin : begin + len(piece.arrays)])
        begin += len(piece.arrays)
    pieces[0].fetch(parts[0], place_ref, w.at[0], sems.at[0])
    for i in range(n):
        if i + 1 < n:
            pieces[i + 1].fetch(parts[i + 1], place_ref, w.at[(i + 1) % 2], sems.at[(i + 1) % 2])
        landed(w.at[i % 2], sems.at[i % 2])
        part = nt(late.take(i)[...], w[i % 2, :, cfg["base"] :])
        dn[...] = part if i == 0 else dn[...] + part
    x_ref, dh_ref = late.take(n), late.take(n + 1)

    def rows_of(rows, carry):
        unit, inverse = norm_stats(x_ref[rows, :].astype(F32))
        grad = dn[rows, :]
        scaled = grad * gain[...]
        out = dh_ref[rows, :] + inverse * (
            scaled
            - jnp.mean(scaled, axis=-1, keepdims=True)
            - unit * jnp.mean(scaled * unit, axis=-1, keepdims=True)
        )
        out_ref[rows, :] = out.astype(BF)
        return carry[0] + fold(grad * unit), carry[1] + fold(grad)

    m, dim = x_ref.shape
    zero = jnp.zeros((8, dim), F32)
    for i, value in enumerate(over_rows(m, rows_of, (zero, zero))):
        vec_ref[i : i + 1, :] = total_of(value)


def norm_back(cfg, place, after, pieces, x, dh, gain, grads):
    m, d = x.shape
    outs = [((m, d), BF), ((2, d), F32)]
    return call(
        partial(norm_back_kernel, cfg, pieces), "norm_back", 18, place, arrays_of(pieces), after,
        [gain], outs,
        [
            pltpu.VMEM((m, d), F32),
            pltpu.VMEM((2, d, cfg["width"]), BF),
            pltpu.SemaphoreType.DMA((2,)),
        ],
        late=[*grads, x, dh],
    )


def pad_heads(cfg, refs):
    m, seq = cfg["m"], cfg["seq"]
    lane = lax.broadcasted_iota(jnp.int32, (m, LANES - HD), 1)
    row = lax.broadcasted_iota(jnp.int32, (m, LANES - HD), 0)
    one = jnp.where(lane == 0, 1.0, 0.0).astype(BF)
    past = jnp.where((lane == 0) & (row >= seq), -1e30, 0.0).astype(BF)
    for h in range(cfg["heads"]):
        for ref, fill in zip(refs, (one, past, one)):
            ref[h, :, HD:] = fill


def attn_fwd_kernel(cfg, piece, place_ref, w_refs, a_ref, bias_ref, *refs):
    qkv_ref, o_ref, lse_ref, w, q_s, k_s, v_s, vt, ot, sem = refs
    m, heads, base, wide = cfg["m"], cfg["heads"], cfg["base"], cfg["wide"]
    piece.fetch(w_refs, place_ref, w, sem)
    pad_heads(cfg, (q_s, k_s, v_s))
    ot[...] = jnp.zeros_like(ot)
    lse_ref[...] = jnp.zeros_like(lse_ref)
    landed(w, sem)
    qkv_ref[...] = (nn(a_ref[...], w[:, base:]) + bias_ref[...]).astype(BF)
    span = heads * HD
    skip = span - base
    for h in range(heads):
        for n, s in enumerate((q_s, k_s, v_s)):
            at = skip + n * span + h * HD
            s[h, :, :HD] = qkv_ref[:, at : at + HD]
        vt[h] = v_s[h].T
        s = nt(k_s[h], q_s[h])
        highest = jnp.max(s, axis=0, keepdims=True) * SHARP
        p = jnp.exp2(s * SHARP - highest).astype(BF)
        mixed = nn(vt[h], p)
        total = mixed[HD : HD + 1, :]
        ot[h * HD : (h + 1) * HD, :] = mixed[:HD, :] * (1.0 / total)
        lse_ref[h : h + 1, :] = highest + jnp.log2(total)
    o_ref[...] = ot[...].T.astype(BF)


def attn_fwd(cfg, place, after, piece, a, bias):
    m, dim = a.shape
    qw, wide, heads, width = cfg["qw"], cfg["wide"], cfg["heads"], cfg["width"]
    outs = [((m, qw), BF), ((m, wide), BF), ((8, m), F32)]
    scratch = (
        [pltpu.VMEM((dim, width), BF)]
        + [pltpu.VMEM((heads, m, LANES), BF)] * 3
        + [
            pltpu.VMEM((heads, LANES, m), BF),
            pltpu.VMEM((wide, m), F32),
            pltpu.SemaphoreType.DMA,
        ]
    )
    return call(
        partial(attn_fwd_kernel, cfg, piece), "attn_fwd", 8, place, piece.arrays, after, [a, bias],
        outs, scratch, mib=28,
    )


def attn_bwd_kernel(cfg, piece, place_ref, w_refs, *refs):
    dh_ref, qkv_ref, lse_ref, ga_ref, gb_ref, sum_ref, dqkv, *refs = refs
    w, q_s, k_s, v_s, do_s, kt, do_all, dqt, p_s, ds_s, sem, late = refs
    m, heads, base, wide = cfg["m"], cfg["heads"], cfg["base"], cfg["wide"]
    tile = m // 2
    piece.fetch(w_refs, place_ref, w, sem, wide)
    late.start()
    span = heads * HD
    skip = span - base
    pad_heads(cfg, (q_s, k_s))
    dqt[...] = jnp.zeros_like(dqt)
    dqkv[:, :LANES] = jnp.zeros((m, LANES), BF)
    for h in range(heads):
        v_s[h, :, HD:] = jnp.zeros((m, LANES - HD), BF)
        do_s[h, :, HD:] = jnp.zeros((m, LANES - HD), BF)
        for n, s in enumerate((q_s, k_s, v_s)):
            at = skip + n * span + h * HD
            s[h, :, :HD] = qkv_ref[:, at : at + HD]
        kt[h] = k_s[h].T
    landed(w, sem)
    do_all[...] = nn(dh_ref[...], w[...]).astype(BF)
    for h in range(heads):
        do_s[h, :, :HD] = do_all[:, h * HD : (h + 1) * HD]
        for t in range(m // tile):
            cols = slice(t * tile, (t + 1) * tile)
            p = jnp.exp2(nt(k_s[h], q_s[h, cols, :]) * SHARP - lse_ref[h : h + 1, cols])
            dp = nt(v_s[h], do_s[h, cols, :])
            ds = (p * (dp - jnp.sum(dp * p, axis=0, keepdims=True))).astype(BF)
            p_s[h % 2, :, cols] = p.astype(BF)
            ds_s[h % 2, :, cols] = ds
            dqt[h * HD : (h + 1) * HD, cols] = nn(kt[h], ds)[:HD] * SCALE
        dk = (nn(ds_s[h % 2], q_s[h]) * SCALE).astype(BF)
        dv = nn(p_s[h % 2], do_s[h]).astype(BF)
        at = skip + span + h * HD
        dqkv[:, at : at + HD] = dk[:, :HD]
        at = skip + 2 * span + h * HD
        dqkv[:, at : at + HD] = dv[:, :HD]
    dqkv[:, skip : skip + span] = dqt[...].T.astype(BF)[:, :span]
    grads = dqkv[...]
    sum_ref[...] = jnp.sum(grads.astype(F32), axis=0, keepdims=True)
    at_ref, dht_ref, o_ref = (late.take(i) for i in range(3))
    half = at_ref.shape[0] // 2
    for n, g_ref in ((1, gb_ref), (0, ga_ref)):
        rows = slice(n * half, (n + 1) * half)
        left = nn(dht_ref[rows, :], o_ref[...])
        right = nn(at_ref[rows, :], grads)
        g_ref[0, :, :base] = left[:, :base].astype(BF)
        g_ref[0, :, base:wide] = (left[:, base:] + right[:, : wide - base]).astype(BF)
        g_ref[0, :, wide:] = right[:, wide - base :].astype(BF)


def attn_bwd(cfg, place, after, piece, at, dh, dht, qkv, o, lse):
    dim, m = at.shape
    qw, wide, heads, width = cfg["qw"], cfg["wide"], cfg["heads"], cfg["width"]
    outs = [((1, dim // 2, width), BF)] * 2 + [((1, qw), F32), ((m, qw), BF)]
    scratch = (
        [pltpu.VMEM((dim, wide), BF)]
        + [pltpu.VMEM((heads, m, LANES), BF)] * 4
        + [
            pltpu.VMEM((heads, LANES, m), BF),
            pltpu.VMEM((m, wide), BF),
            pltpu.VMEM((wide, m), F32),
            pltpu.VMEM((2, m, m), BF),
            pltpu.VMEM((2, m, m), BF),
            pltpu.SemaphoreType.DMA,
        ]
    )
    return call(
        partial(attn_bwd_kernel, cfg, piece), "attn_bwd", 17, place, piece.arrays, after,
        [dh, qkv, lse], outs, scratch, late=[at, dht, o], mib=36,
    )


def ffn_one_kernel(cfg, pieces, place_ref, w_refs, a_ref, bias_ref, *refs):
    g_ref, gp_ref, grad_ref, w, sems, late = refs
    step = pl.program_id(0)

    @pl.when(step == 0)
    def _():
        late.start()
        fetch_step(pieces, 0, w_refs, place_ref, w.at[0], sems.at[0])

    slot = lax.rem(step, 2)
    fetch_step(pieces, step + 1, w_refs, place_ref, w.at[1 - slot], sems.at[1 - slot])
    landed(w.at[slot], sems.at[slot])
    width = g_ref.shape[2]

    @pl.when(step == 0)
    def _():
        late.take(0)

    et_ref = late.buffers[0]
    count, _, rows, _ = grad_ref.shape
    half_rows = et_ref.shape[0] // 2
    blocks = [slice(n, min(n + 256, width)) for n in range(0, width, 256)]

    def before(cols):
        return nn(a_ref[...], w[slot, :, cols]) + bias_ref[0, :, cols]

    pre = before(blocks[0])
    for n, cols in enumerate(blocks):
        following = before(blocks[n + 1]) if n + 1 < len(blocks) else None
        square = pre * pre
        half = 0.5 + 0.5 * jnp.tanh(pre * (GELU_A + GELU_A * GELU_B * square))
        g_ref[0, :, cols] = (pre * half).astype(BF)
        slope = half + (half - half * half) * (pre * (2 * GELU_A + 6 * GELU_A * GELU_B * square))
        gp_ref[0, :, cols] = slope.astype(BF)
        for part in range(2):
            left = et_ref[part * half_rows : (part + 1) * half_rows, :]
            value = nn(left, g_ref[0, :, cols]).astype(BF)
            for i in range(count // 2):
                grad_ref[part * count // 2 + i, 0, :, cols] = value[i * rows : (i + 1) * rows]
        pre = following


def ffn_one(cfg, place, after, pieces, a, bias, et):
    dim, m = et.shape
    n, width = len(pieces), bias.shape[2]
    rows = cfg["rows"] if cfg["rows"] % 16 == 0 else dim // 2
    outs = [((n, m, width), BF)] * 2 + [((dim // rows, n, rows, width), BF)]
    return call(
        partial(ffn_one_kernel, cfg, pieces), "ffn_one", 30, place, arrays_of(pieces), after,
        [a, bias], outs,
        [pltpu.VMEM((2, dim, width), BF), pltpu.SemaphoreType.DMA((2,))],
        late=[et], grid=(n,),
        specs=(
            [whole((m, dim)), stepped((1, width))],
            [stepped((m, width))] * 2
            + [
                pl.BlockSpec(
                    (dim // rows, 1, rows, width),
                    lambda i, place_ref: (0, lax.rem(place_ref[1] - i + n, n), 0, 0),
                )
            ],
        ),
        mib=56, prefetch=True,
    )


def ffn_two_kernel(cfg, ups, downs, first, last, place_ref, w_refs, eb_ref, gp_ref, *refs):
    *refs, late = refs
    if last:
        gain, *refs = refs
    near_ref, far_ref, sum_ref, *refs = refs
    if last:
        dh_ref, dhb_ref, dht_ref, vec_ref, *refs = refs
        wu, wd, dz, dn_ref, scratch, sems = refs
    else:
        dn_ref, wu, wd, dz, sems = refs
    step = pl.program_id(0)
    count = len(arrays_of(ups))
    n = len(ups)

    at_ref = late.buffers[0]

    def get(which, slot):
        fetch_step(downs, which, w_refs[count:], place_ref, wd.at[slot], sems.at[1, slot])
        fetch_step(ups, which, w_refs[:count], place_ref, wu.at[slot], sems.at[0, slot])

    @pl.when(step == 0)
    def _():
        get(0, 0)
        late.start()
        if first:
            dn_ref[...] = jnp.zeros_like(dn_ref)

    slot = lax.rem(step, 2)
    get(step + 1, 1 - slot)
    landed(wd.at[slot], sems.at[1, slot])
    width = dz.shape[1]
    for c in range(0, width, 256):
        cols = slice(c, min(c + 256, width))
        grad = (nn(eb_ref[...], wd[slot, :, cols]) * gp_ref[0, :, cols].astype(F32)).astype(BF)
        dz[:, cols] = grad
        sum_ref[0, :, cols] = jnp.sum(grad.astype(F32), axis=0, keepdims=True)
    landed(wu.at[slot], sems.at[0, slot])
    part = nt(dz[...], wu[slot])

    @pl.when(step == 0)
    def _():
        late.take(0)
        if not first:
            dn_ref[...] = late.take(1)[...]

    dn_ref[...] += part
    middle = at_ref.shape[0] // 2
    far_ref[0] = nn(at_ref[middle:, :], dz[...]).astype(BF)
    near_ref[0] = nn(at_ref[:middle, :], dz[...]).astype(BF)
    if not last:
        return

    @pl.when(step == n - 1)
    def _():
        h_ref = late.take(2)

        def rows_of(rows, carry):
            unit, inverse = norm_stats(h_ref[rows, :])
            grad = dn_ref[rows, :]
            scaled = grad * gain[...]
            dh = eb_ref[rows, :].astype(F32) + inverse * (
                scaled
                - jnp.mean(scaled, axis=-1, keepdims=True)
                - unit * jnp.mean(scaled * unit, axis=-1, keepdims=True)
            )
            dh_ref[rows, :] = dh
            dhb_ref[rows, :] = dh.astype(BF)
            return carry[0] + fold(grad * unit), carry[1] + fold(grad), carry[2] + fold(dh)

        m, dim = h_ref.shape
        zero = jnp.zeros((8, dim), F32)
        sums = over_rows(m, rows_of, (zero, zero, zero))
        for i, value in enumerate(sums):
            vec_ref[i : i + 1, :] = total_of(value)
        turn(cfg, place_ref[0], dhb_ref[...], dht_ref, scratch)


def ffn_two(cfg, place, after, ups, downs, ks, eb, at, gp, dn, closing=None):
    dim, m = at.shape
    n, width = len(ups), gp.shape[2]
    block = (dim // 2, width)
    at_k = lambda i: ks[0] + i if ks[0] < ks[-1] else ks[0] - i
    ins, in_specs, late = [eb, gp], [whole((m, dim)), stepped((m, width), at_k)], [at]
    if closing:
        ins.append(closing[1])
        in_specs.append(whole((1, dim)))
        late += [dn, closing[0]]
    outs = [((n,) + block, BF)] * 2 + [((n, 1, width), F32)]
    out_specs = [stepped(block)] * 2 + [stepped((1, width))]
    scratch = [
        pltpu.VMEM((2, dim, width), BF), pltpu.VMEM((2, dim, width), BF), pltpu.VMEM((m, width), BF)
    ]
    if closing:
        shapes = [((m, dim), F32), ((m, dim), BF), ((dim, m), BF), ((3, dim), F32)]
        scratch += [pltpu.VMEM((m, dim), F32), pltpu.VMEM((dim, m), BF)]
    else:
        shapes = [((m, dim), F32)]
    outs += shapes
    out_specs += [whole(shape) for shape, _ in shapes]
    return call(
        partial(ffn_two_kernel, cfg, ups, downs, dn is None, bool(closing)), "ffn_two",
        30 if closing else 24, place, arrays_of(ups) + arrays_of(downs), after, ins, outs,
        scratch + [pltpu.SemaphoreType.DMA((2, 2))], late=late, grid=(n,),
        specs=(in_specs, out_specs), mib=58,
    )


CORE, ACROSS, ALONG = 1, 2, 4
CUBE = 8
ORDER = (0, ACROSS, ALONG, ACROSS + ALONG, CORE, CORE + ACROSS, CORE + ALONG, CORE + ACROSS + ALONG)


def ring(value, by, size):
    return lax.ppermute(value, "tensor", [(i, (i + by) % size) for i in range(size)])


def swap(value, offset):
    return lax.ppermute(value, "dp", [(i, i ^ offset) for i in range(lax.axis_size("dp"))])


def tie(value, *others):
    return lax.optimization_barrier((value, *others))[0]


def ties(values, mark):
    return list(lax.optimization_barrier((*values, mark))[:-1])


def gather_all(own, split):
    dp, size = lax.axis_size("dp"), lax.axis_size("tensor")
    rows = own.shape[0]
    full = lax.all_gather(own, ("dp", "tensor"), axis=0, tiled=False)
    if split:

        def blocks(k, d, z):
            t = lax.rem(z - k + size, size)
            return [(0, i * size + t, i * rows, rows) for i in range(dp)]
    else:
        full = full.reshape(dp, size, rows, -1).transpose(1, 0, 2, 3)
        full = full.reshape(size, dp * rows, -1)

        def blocks(k, d, z):
            return [(0, lax.rem(z - k + size, size), 0, dp * rows)]

    return [Piece([full], partial(blocks, k)) for k in range(size)]


def gather_ring(own):
    size = lax.axis_size("tensor")
    held = [own]
    for _ in range(size - 1):
        held.append(ring(held[-1], 1, size))
    return held


def gather_near(held, group):
    mine = jnp.stack(held[2 * group : 2 * group + 2])
    return jnp.stack([mine, swap(mine, (ACROSS, ALONG)[group])])


def gather_far(both, group):
    return swap(both, (ALONG, ACROSS)[group])


def gather_groups(both, both_core, far, far_core, rows):
    firsts = (ACROSS, ACROSS, ALONG, ALONG)

    def blocks(k, d, z):
        group, n = k // 2, k % 2
        first = firsts[k]
        second = ACROSS + ALONG - first
        out = []
        for other in range(2):
            for index, lead, offset in (
                (group, (other, n), 0),
                (2, (group, other, n), CORE),
                (3 + group, (other, n), second),
                (5, (group, other, n), CORE + second),
            ):
                at = pl.multiple_of(jnp.bitwise_xor(d, offset + other * first) * rows, 16)
                out.append((index, lead, at, rows))
        return out

    return [Piece([*both, both_core, *far, far_core], partial(blocks, k)) for k in range(4)]


def scatter_all(near, far):
    size, dp = lax.axis_size("tensor"), lax.axis_size("dp")
    z = lax.axis_index("tensor")
    pieces = jnp.stack([jnp.concatenate(halves) for halves in zip(near, far)])
    dim, width = pieces.shape[1:]
    order = jnp.stack([lax.rem(z - t + size, size) for t in range(size)])
    return scatter_placed(jnp.take(pieces, order, axis=0)[None])


def scatter_placed(value):
    size, dp = lax.axis_size("tensor"), lax.axis_size("dp")
    blocks, _, rows, width = value.shape
    if blocks != dp:
        value = value.transpose(1, 0, 2, 3).reshape(size, dp, -1, width).transpose(1, 0, 2, 3)
    value = value.reshape(dp * size, -1, width)
    return lax.psum_scatter(value, ("dp", "tensor"), scatter_dimension=0, tiled=True)[0]


def add(*terms):
    total = terms[0].astype(F32)
    for term in terms[1:]:
        total = total + term.astype(F32)
    return total


class Scatter:
    def __init__(self, halves, links):
        self.links = links
        self.near = [piece for near, _ in halves for piece in self.split(near)]
        self.far = [far for _, far in halves]

    def split(self, value):
        count, half, width = value.shape
        value = value.reshape(count, 2, 2, half // 4, width)
        return [value[i] for i in range(count)]

    def pick(self, value, link, i, j):
        return value[j, i] if link == ACROSS else value[i, j]

    def send(self, step, outs):
        got, sent = [None] * len(outs), []
        for link in (ACROSS, ALONG):
            mine = [i for i, first in enumerate(self.links) if (first == link) == (step == 1)]
            if not mine:
                continue
            value = swap(jnp.stack([v for i in mine for v in outs[i]]), link)
            sent.append(value)
            for n, i in enumerate(mine):
                count = len(outs[i])
                got[i] = [value[n * count + c] for c in range(count)]
        return got, sent

    def step_core(self):
        sent = [swap(far, CORE) for far in self.far]
        self.core = [piece for value in sent for piece in self.split(value)]
        return sent

    def step_first(self, mark=None):
        if mark is not None:
            self.core = ties(self.core, mark)
        outs = [
            [add(self.pick(a, link, 1, j), self.pick(b, link, 1, j)).astype(BF) for j in range(2)]
            for a, b, link in zip(self.near, self.core, self.links)
        ]
        self.one, sent = self.send(1, outs)
        return sent

    def step_second(self, mark=None):
        if mark is not None:
            flat = ties([v for one in self.one for v in one], mark)
            self.one = [flat[2 * i : 2 * i + 2] for i in range(len(self.one))]
        outs = [
            [add(self.pick(a, link, 0, 1), self.pick(b, link, 0, 1), one[1]).astype(BF)]
            for a, b, one, link in zip(self.near, self.core, self.one, self.links)
        ]
        self.two, sent = self.send(2, outs)
        return sent

    def terms(self, i):
        link = self.links[i]
        return [
            self.pick(self.near[i], link, 0, 0),
            self.pick(self.core[i], link, 0, 0),
            self.one[i][0],
            self.two[i][0],
        ]


class Around:
    def __init__(self, terms, size):
        self.terms, self.size, self.k, self.total = terms, size, size - 1, None

    def step(self, mark=None):
        terms = self.terms(self.k) + ([] if self.total is None else [self.total])
        if mark is not None:
            terms = terms[:-1] + [tie(terms[-1], mark)]
        total = add(*terms)
        self.k -= 1
        if self.k < 0:
            return total
        self.total = ring(total.astype(BF), -1, self.size)
        return [self.total]


def sum_all(vector, marks):
    if marks is None:
        return lax.psum(vector, ("dp", "tensor"))
    size = lax.axis_size("tensor")
    for offset in (CORE, ACROSS, ALONG):
        if offset == ALONG:
            vector = tie(vector, *marks[0])
        vector = vector + swap(vector, offset)
    offset = 1
    while offset < size:
        if 2 * offset == size:
            vector = tie(vector, *marks[1])
        vector = vector + lax.ppermute(vector, "tensor", [(i, i ^ offset) for i in range(size)])
        offset *= 2
    return vector


def on_device(
    tokens, image_flags, cotangent, gain_one, shift_one, w_query, b_query, w_key, w_value, b_value,
    w_out, b_out, gain_two, shift_two, w_up, b_up, w_down, b_down,
):
    dp, size = lax.axis_size("dp"), lax.axis_size("tensor")
    d, z = lax.axis_index("dp"), lax.axis_index("tensor")
    images = image_flags.shape[0]
    all_rows, dim = tokens.shape
    seq = all_rows // images
    assert images == size
    m = up(seq, 256)
    rows = dim // dp
    split = rows % 16 == 0
    span = w_query.shape[1]
    units = w_up.shape[1]
    hidden = up(units, LANES)
    width = 4 * span
    base, wide = span // LANES * LANES, up(span, LANES)
    qw = width - base
    cube = dp == CUBE and split and size == 4
    cfg = dict(m=m, seq=seq, heads=span // HD, base=base, wide=wide, width=width, qw=qw)
    cfg.update(rows=rows, order=ORDER if cube else None)

    own_attn = jnp.concatenate([w_out.T, w_query, w_key, w_value], axis=1).astype(BF)
    own_up = jnp.pad(w_up.astype(BF), ((0, 0), (0, hidden - units)))
    own_down = jnp.pad(w_down.T.astype(BF), ((0, 0), (0, hidden - units)))
    skip = jnp.zeros((span - base,), F32)
    own_bias = jnp.concatenate(
        [skip, b_query, jnp.zeros((span,), F32), b_value, b_up, jnp.zeros((hidden - units,), F32)]
    )[None]
    flag = lax.dynamic_index_in_dim(image_flags, z, 0, keepdims=False)
    place = jnp.stack([d, z, flag]).astype(jnp.int32)

    pad_rows = ((0, m - seq), (0, 0))
    x = jnp.pad(lax.dynamic_slice_in_dim(tokens, z * seq, seq, 0), pad_rows)
    eb = jnp.pad(lax.dynamic_slice_in_dim(cotangent, z * seq, seq, 0) * flag.astype(BF), pad_rows)
    a1, a1t, et, sum_e = norm_one(cfg, place, x, eb, gain_one[None], shift_one[None])

    every = list(range(size))
    pin = {}
    attn_w = gather_all(own_attn, split)
    if cube:
        bits = []
        for _ in range(3):
            top = lax.reduce_precision(own_bias[0], 8, 7)
            bits.append(top.astype(BF))
            own_bias = own_bias - top[None]
        bits = jnp.concatenate(bits)
        count = bits.shape[0]
        extra = up(-(-count // hidden), 16)
        bits = jnp.pad(bits, (0, extra * hidden - count)).reshape(extra, hidden)
        ffn_held = gather_ring(jnp.concatenate([own_up, bits]))
        bias = []
        for v in ffn_held:
            v = v[rows:].reshape(-1)[:count].reshape(3, -1).astype(F32)
            bias.append((v[0] + v[1] + v[2])[None])
        up_held = [v[:rows] for v in ffn_held]
        both_up = [gather_near(up_held, 0), gather_near(ties(up_held, sum_e), 1)]
        far_up = [gather_far(both_up[i], i) for i in range(2)]
        core_up = swap(jnp.stack(both_up), CORE)
        pin["attn0"] = [*far_up]
        own_down = tie(own_down, *far_up)
    else:
        bias = gather_ring(own_bias)
        up_w = gather_all(own_up, split)
    kept = [
        attn_fwd(cfg, place, pin.get(f"attn{k}", []), attn_w[k], a1, bias[k][:, :qw]) for k in every
    ]
    h, a2, a2t = norm_two(
        cfg, place, pin.get("norm_two", []), attn_w, x, b_out[None], gain_two[None], shift_two[None],
        [o for _, o, _ in kept],
    )
    down_w = gather_all(tie(own_down, attn_w[0].arrays[0]), split)
    if cube:
        up_w = gather_groups(both_up, core_up, far_up, swap(jnp.stack(far_up), CORE), rows)
    g, gp, g_down = ffn_one(
        cfg, place, pin.get("ffn_one", []), up_w, a2, jnp.stack(bias)[:, :, qw:], et
    )

    sum_down = scatter_placed(g_down)

    low, high = [1, 0], [3, 2]
    near3, far3, sum_high, dn2 = ffn_two(
        cfg, place, pin.get("two0", []), [up_w[k] for k in high], [down_w[k] for k in high], high, eb,
        a2t, gp, None,
    )
    mixed_links = [ACROSS, ALONG]
    if cube:
        up_high = Scatter([(near3, far3)], mixed_links)
        up_high_core = up_high.step_core()
    near1, far1, sum_low, dh, dhb, dht, vec_two = ffn_two(
        cfg, place, pin.get("two1", []), [up_w[k] for k in low], [down_w[k] for k in low], low, eb,
        a2t, gp, dn2, [h, gain_two[None]],
    )
    sum_dz = [sum_low[1], sum_low[0], sum_high[1], sum_high[0]]
    grads = [None] * size

    def backward(k, after):
        near, far, sums, dqkv = attn_bwd(cfg, place, after, attn_w[k], a1t, dhb, dht, *kept[k])
        grads[k] = (near, far, sums, dqkv)
        return Scatter([(near, far)], [ACROSS if k % 2 else ALONG])

    def finish(after):
        return mix(place, after, down_w, h, g, b_down[None])

    def finish_norm(after):
        return norm_back(
            cfg, place, after, attn_w, x, dh, gain_one[None], [grads[k][3] for k in every]
        )

    if cube:
        up_low = Scatter([(near1, far1)], mixed_links)
        up_z = Around(lambda k: (up_high if k > 1 else up_low).terms(1 - k % 2), size)
        attn_z = Around(lambda k: out[k].terms(0), size)
        out = {}
        pins = {k: [] for k in ("a3", "a2", "a1", "a0", "nb", "mix")}
        pins["a3"] += up_high_core
        pins["a2"] += up_low.step_core() + up_high.step_first(vec_two)
        out[3] = backward(3, pins["a3"])
        mark = grads[3][2]
        pins["a1"] += up_high.step_second(mark) + up_low.step_first(mark) + out[3].step_core()
        out[2] = backward(2, pins["a2"])
        mark = grads[2][2]
        pins["a0"] += up_low.step_second(mark) + out[3].step_first(mark) + out[2].step_core()
        out[1] = backward(1, pins["a1"])
        mark = grads[1][2]
        pins["nb"] += out[3].step_second(mark) + out[2].step_first(mark) + out[1].step_core()
        pins["nb"] += up_z.step(mark)
        out[0] = backward(0, pins["a0"])
        mark = grads[0][2]
        pins["nb"] += out[0].step_core()
        pins["mix"] += out[1].step_first(mark) + out[2].step_second(mark) + attn_z.step(mark)
        zero_first = out[0].step_first()
        pins["mix"] += up_z.step(mark)
        tokens_grad, vec_one = finish_norm(pins["nb"])
        vec_one = tie(vec_one, *zero_first)
        seconds = out[1].step_second(vec_one) + out[0].step_second(vec_one)
        attn_z.step(vec_one)
        up_z.step(vec_one)
        mixed = finish(pins["mix"])
        marks = (seconds + [mixed], attn_z.step())
        grad_up, grad_attn = up_z.step(), attn_z.step()
    else:
        for k in high + low:
            backward(k, [])
        mixed = finish([])
        tokens_grad, vec_one = finish_norm([])
        rejoin = lambda a, b: [a[1], a[0], b[1], b[0]]
        grad_up = scatter_all(rejoin(near1, near3), rejoin(far1, far3))
        grad_attn = scatter_all([g[0][0] for g in grads], [g[1][0] for g in grads])
    sum_qkv = [g[2] for g in grads]
    grad_down = tie(sum_down, vec_one).astype(F32)[:, :units].T
    grad_up, grad_attn = grad_up.astype(F32), grad_attn.astype(F32)
    grad_up = grad_up[:, :units]
    pieces = jnp.concatenate([jnp.concatenate(sum_qkv), jnp.concatenate(sum_dz)], axis=1)
    order = jnp.stack([lax.rem(z - t + size, size) for t in range(size)])
    pieces = jnp.take(pieces, order, axis=0)
    sums = sum_all(
        jnp.concatenate([pieces.reshape(-1), vec_one.reshape(-1), vec_two.reshape(-1), sum_e[0]]),
        marks if cube else None,
    )
    per = qw + hidden
    mine = lax.dynamic_index_in_dim(sums[: size * per].reshape(size, per), z, 0, keepdims=False)
    rest = sums[size * per :].reshape(6, dim)
    at = span - base
    return (
        mixed[:seq],
        tokens_grad[:seq],
        rest[0],
        rest[1],
        grad_attn[:, span : 2 * span],
        mine[at : at + span],
        grad_attn[:, 2 * span : 3 * span],
        grad_attn[:, 3 * span :],
        mine[at + 2 * span : at + 3 * span],
        grad_attn[:, :span].T,
        rest[4],
        rest[2],
        rest[3],
        grad_up,
        mine[qw : qw + units],
        grad_down,
        rest[5],
    )


SPECS_IN = (
    P("dp", None), P("dp"), P("dp", None), P(), P(), P("dp", "tensor"), P("tensor"),
    P("dp", "tensor"), P("dp", "tensor"), P("tensor"), P("tensor", "dp"), P(), P(), P(),
    P("dp", "tensor"), P("tensor"), P("tensor", "dp"), P(),
)
SPECS_OUT = (
    P(("dp", "tensor"), None), P(("dp", "tensor"), None), P(), P(), P("dp", "tensor"), P("tensor"),
    P("dp", "tensor"), P("dp", "tensor"), P("tensor"), P("tensor", "dp"), P(), P(), P(),
    P("dp", "tensor"), P("tensor"), P("tensor", "dp"), P(),
)


def solution(mesh):
    return jax.shard_map(
        on_device, mesh=mesh, in_specs=SPECS_IN, out_specs=SPECS_OUT, check_vma=False
    )
```
